32 devices in a mesh: dp: 8 (over y, x, core), feat: 4 (over z).
Axes of the slice: x: 2, y: 2, z: 4, core: 2. Of those that a mesh axis runs over, the one named last changes fastest.
Arguments:
- hidden_in: bfloat16 [8192, 1024], P(('dp', 'feat')), may hold values from -6 to 6
- query_weight: bfloat16 [1024, 256], P(('dp', 'feat')), may hold values from -0.1875 to 0.1875
- key_weight: bfloat16 [1024, 256], P(('dp', 'feat')), may hold values from -0.1875 to 0.1875
- value_weight: bfloat16 [1024, 1024], P(('dp', 'feat')), may hold values from -0.1875 to 0.1875
- output_weight: bfloat16 [1024, 1024], P(None, ('dp', 'feat')), may hold values from -3 to 3
- gate_weight: bfloat16 [1024, 2752], P('dp', 'feat'), may hold values from -0.1875 to 0.1875
- up_weight: bfloat16 [1024, 2752], P('dp', 'feat'), may hold values from -0.1875 to 0.1875
- down_weight: bfloat16 [2752, 1024], P('feat', 'dp'), may hold values from -0.109375 to 0.109375
- gain_attn: bfloat16 [1024], P(('dp', 'feat')), may hold values from 0.5 to 1.5
- gain_mlp: bfloat16 [1024], P(('dp', 'feat')), may hold values from 0.5 to 1.5
- first_length: int32 [8], P('dp'), may hold values from 128 to 1024, as said below
- cotangent: bfloat16 [8192, 1024], P(('dp', 'feat')), may hold values from -6 to 6
Outputs:
- block_out: bfloat16 [8192, 1024], P(('dp', 'feat'))
- input_grad: float32 [8192, 1024], P(('dp', 'feat'))
- query_grad: float32 [1024, 256], P(('dp', 'feat'))
- key_grad: float32 [1024, 256], P(('dp', 'feat'))
- value_grad: float32 [1024, 1024], P(('dp', 'feat'))
- output_grad: float32 [1024, 1024], P(None, ('dp', 'feat'))
- gate_grad: float32 [1024, 2752], P('dp', 'feat')
- up_grad: float32 [1024, 2752], P('dp', 'feat')
- down_grad: float32 [2752, 1024], P('feat', 'dp')
- gain_attn_grad: float32 [1024], P(('dp', 'feat'))
- gain_mlp_grad: float32 [1024], P(('dp', 'feat'))
The draws below stay inside these ranges and needn't reach their ends.
Inputs may be any that keep to these rules, and one draw needn't show every extreme that they name: Each pack of 1024 tokens holds one sequence of first_length tokens and, after it, one of the rest; the value is 1024, 896 or 128.
All inputs are finite; a program needn't handle non-finite values.
Results may differ from the reference program's by a relative error of at most 0.018.
Values may be sent and summed in bfloat16 or wider, within the bound.
No kernel may reach another device: no remote copies, remote signals or barrier semaphores. Data moves between devices by JAX's collectives and lax.ppermute only.
A program may use at most 192 MiB of HBM per device.

```python
import jax
import jax.numpy as jnp
from jax import lax

D = 1024
H = 16
HF = 16
DV = 64
FF = 2752
SEQ_LEN = 1024
FEAT = 280
PACK_COUNT = 8
TOKENS = 8192
N_FEAT = 4


def draw_first_length(key, part):
    key = jax.random.fold_in(key, 11)
    pattern = jax.random.randint(key, (PACK_COUNT,), 0, 3).astype(jnp.int32)
    pattern = pattern.at[0].set(0)
    pattern = pattern.at[PACK_COUNT - 1].set(2)
    short_part = SEQ_LEN // 8
    return jnp.where(pattern == 0, SEQ_LEN, jnp.where(pattern == 1, SEQ_LEN - short_part, short_part)).astype(jnp.int32)


def spiked(values, rng, source, target, blocks, factor):
    owner, partner = [(jnp.arange(values.shape[dim]) // (values.shape[dim] // blocks)).reshape([-1 if axis == dim else 1 for axis in range(values.ndim)]) for dim in (source, target)]
    chosen = jax.random.permutation(rng, blocks)[partner]
    strong = (owner == chosen) | (owner == (partner + blocks // 2) % blocks)
    return jnp.where(strong, factor * values, values)


def block_levels(stream_key, extent, split, low, high):
    gain = 1.0
    for dim, shards_of in split:
        steps = jax.random.uniform(jax.random.fold_in(jax.random.fold_in(stream_key, 6), dim), (shards_of,), jnp.float32, low / len(split), high / len(split))
        gain = gain * jnp.repeat(jnp.exp(steps), extent[dim] // shards_of).reshape((-1,) + (1,) * (len(extent) - 1 - dim))
    return gain


def bell_draw(stream_key, dims, deviation, reach, shards=(), kind=jnp.bfloat16):
    values = jax.random.normal(stream_key, dims, jnp.float32) * deviation
    if len(shards) > 0:
        values = block_levels(stream_key, dims, shards, -0.22, 0.18) * values
    return jnp.clip(values, min=-reach, max=reach).astype(kind)


def gaussian_with(rng, dims, spread, most, split, heavy, kind=jnp.bfloat16):
    result = spread * jax.random.normal(rng, dims, jnp.float32)
    if split:
        result = result * block_levels(rng, dims, split, -0.22, 0.18)
    return jnp.clip(spiked(result, jax.random.fold_in(rng, 3), *heavy), -most, most).astype(kind)


def setup_inputs(seed: int = 0) -> dict:
    key_of = jax.random.split(jax.random.key(seed), 13)
    hidden_in = bell_draw(key_of[0], (TOKENS, D), 1.0, 6.0, ((0, 32),))
    query_weight = bell_draw(key_of[1], (D, H * HF), D ** -0.5, 0.1875, ((0, 32),))
    key_weight = bell_draw(key_of[2], (D, H * HF), D ** -0.5, 0.1875, ((0, 32),))
    value_weight = bell_draw(key_of[3], (D, H * DV), D ** -0.5, 0.1875, ((0, 32),))
    output_weight = bell_draw(key_of[4], (H * DV, D), (max(1, H * DV // 256)) ** -0.5, 3.0, ((1, 32),))
    gate_weight = bell_draw(key_of[5], (D, FF), D ** -0.5, 0.1875, ((0, 8), (1, 4)))
    up_weight = bell_draw(key_of[6], (D, FF), D ** -0.5, 0.1875, ((0, 8), (1, 4)))
    down_weight = bell_draw(key_of[7], (FF, D), FF ** -0.5, 0.109375, ((0, 4), (1, 8)))
    gain_attn = jnp.clip(1.0 + 0.1 * jax.random.normal(key_of[8], (D,), jnp.float32), 0.5, 1.5).astype(jnp.bfloat16)
    gain_mlp = jnp.clip(1.0 + 0.1 * jax.random.normal(key_of[9], (D,), jnp.float32), 0.5, 1.5).astype(jnp.bfloat16)
    first_length = draw_first_length(jax.random.fold_in(key_of[12], 71), 0)
    cotangent = gaussian_with(key_of[11], (TOKENS, D), 1.0, 6.0, ((0, 32),), (0, 1, 32, 2.75))
    return dict(hidden_in=hidden_in, query_weight=query_weight, key_weight=key_weight, value_weight=value_weight, output_weight=output_weight, gate_weight=gate_weight, up_weight=up_weight, down_weight=down_weight, gain_attn=gain_attn, gain_mlp=gain_mlp, first_length=first_length, cotangent=cotangent)


EPSILON = 1e-05
INV_ROOT2 = 0.7071067811865476
HIGHEST = lax.Precision.HIGHEST

@jax.custom_vjp
def low(v):
    return lax.optimization_barrier(v.astype(jnp.bfloat16)).astype(jnp.float32)

@jax.custom_vjp
def low_back(v):
    return v

def low_keep(v):
    return (low(v), None)

def low_pass(kept, grad):
    return (grad,)

def back_keep(v):
    return (v, None)

def back_low(kept, grad):
    return (low(grad),)
low.defvjp(low_keep, low_pass)
low_back.defvjp(back_keep, back_low)

def taylor(entries):
    halved = entries * 0.5
    quadratic = halved[..., :, None] * halved[..., None, :] * INV_ROOT2
    quadratic = quadratic.reshape(halved.shape[:-1] + (HF * HF,))
    constant = jnp.ones(halved.shape[:-1] + (1,), halved.dtype)
    padding = jnp.zeros(halved.shape[:-1] + (FEAT - 1 - HF - HF * HF,), halved.dtype)
    return jnp.concatenate([constant, halved, quadratic, padding], axis=-1)

def rms_scale(entries, scale_gain):
    return entries * lax.rsqrt(lax.optimization_barrier(jnp.mean(entries * entries, axis=-1, keepdims=True)) + EPSILON) * scale_gain

def product(first_matrix, second_matrix):
    return jnp.dot(first_matrix, second_matrix, precision=HIGHEST, preferred_element_type=jnp.float32)

def pack_allowed(boundary):
    position = jnp.arange(SEQ_LEN, dtype=jnp.int32)
    segment = (position >= boundary).astype(jnp.int32)
    return (position[None, :] <= position[:, None]) & (segment[None, :] == segment[:, None])

def pack_attention(queries, key_rows, value_rows, boundary):
    allowed = pack_allowed(boundary)
    query_feat = low(taylor(queries.reshape(SEQ_LEN, H, HF)))
    key_feat = low(taylor(key_rows.reshape(SEQ_LEN, H, HF)))
    head_values = value_rows.reshape(SEQ_LEN, H, DV)
    group_width = FEAT // N_FEAT
    numerator = jnp.zeros((SEQ_LEN, H, DV), queries.dtype)
    denominator = jnp.zeros((SEQ_LEN, H), queries.dtype)
    for group_index in range(N_FEAT):
        lower_edge = group_index * group_width
        scores = jnp.einsum('thj,shj->hts', query_feat[:, :, lower_edge:lower_edge + group_width], key_feat[:, :, lower_edge:lower_edge + group_width], precision=HIGHEST)
        scores = low(low_back(jnp.where(allowed[None], scores, 0.0)))
        numerator = numerator + jnp.einsum('hts,shv->thv', scores, head_values, precision=HIGHEST)
        denominator = denominator + lax.optimization_barrier(jnp.sum(scores, axis=2)).T
    return (numerator.reshape(SEQ_LEN, H * DV), denominator)

def forward(residual, query_weight, key_weight, value_weight, output_weight, gate_weight, up_weight, down_weight, gain_attn, gain_mlp, first_length):
    attn_in = low(rms_scale(residual, gain_attn))
    queries = low(low_back(product(attn_in, query_weight)))
    key_rows = low(low_back(product(attn_in, key_weight)))
    value_rows = low(low_back(product(attn_in, value_weight)))
    pack_total = first_length.shape[0]
    attend = jax.checkpoint(pack_attention)
    numerator, denominator = lax.map(lambda packed: attend(packed[0], packed[1], packed[2], packed[3]), (queries.reshape(pack_total, SEQ_LEN, H * HF), key_rows.reshape(pack_total, SEQ_LEN, H * HF), value_rows.reshape(pack_total, SEQ_LEN, H * DV), first_length))
    numerator = low_back(numerator.reshape(-1, H, DV))
    denominator = low_back(denominator.reshape(-1, H))
    attended = low((numerator / denominator[:, :, None]).reshape(-1, H * DV))
    middle = residual + low_back(product(attended, output_weight))
    mlp_in = low(rms_scale(middle, gain_mlp))
    gate_value = low_back(product(mlp_in, gate_weight))
    up_proj = low_back(product(mlp_in, up_weight))
    activation = low(jax.nn.silu(gate_value) * up_proj)
    return middle + product(activation, down_weight)

def reference(hidden_in, query_weight, key_weight, value_weight, output_weight, gate_weight, up_weight, down_weight, gain_attn, gain_mlp, first_length, cotangent):
    floats = tuple((source.astype(jnp.float32) for source in (hidden_in, query_weight, key_weight, value_weight, output_weight, gate_weight, up_weight, down_weight, gain_attn, gain_mlp)))

    def closed(*arrays):
        return forward(*arrays, first_length)
    block_out, pull_back = jax.vjp(closed, *floats)
    gradients = pull_back(cotangent.astype(jnp.float32))
    return (block_out.astype(jnp.bfloat16), gradients[0], gradients[1], gradients[2], gradients[3], gradients[4], gradients[5], gradients[6], gradients[7], gradients[8], gradients[9])
```

```python
from functools import partial

import jax
import jax.numpy as jnp
from jax import lax
from jax.experimental import pallas as pl
from jax.experimental.pallas import tpu as pltpu
from jax.sharding import PartitionSpec as P

H = 16
HF = 16
DV = 64
SEQ_LEN = 1024
EPSILON = 1e-05

LANES = 128
TILE = 256
F32 = jnp.float32
BF16 = jnp.bfloat16


def matmul(first_matrix, second_matrix):
    return jnp.dot(first_matrix, second_matrix, preferred_element_type=F32)


def dot_first(first_matrix, second_matrix):
    return lax.dot_general(
        first_matrix, second_matrix, (((0,), (0,)), ((), ())), preferred_element_type=F32
    )


def dot_last(first_matrix, second_matrix):
    return lax.dot_general(
        first_matrix, second_matrix, (((1,), (1,)), ((), ())), preferred_element_type=F32
    )


def hop(block, bit):
    size = lax.axis_size("dp")
    return lax.ppermute(block, "dp", [(i, i ^ (1 << bit)) for i in range(size)])


def turn(block, shift):
    size = lax.axis_size("feat")
    return lax.ppermute(block, "feat", [(i, (i + shift) % size) for i in range(size)])


def spread(block, order):
    pieces = {0: block}
    for bit in order:
        pieces.update({j ^ (1 << bit): hop(piece, bit) for j, piece in pieces.items()})
    return pieces


def collect(terms, order):
    for bit in reversed(order):
        mask = 1 << bit
        kept = {}
        for j in terms:
            if not j & mask:
                other = hop(terms[j ^ mask], bit)
                kept[j] = (terms[j].astype(F32) + other.astype(F32)).astype(BF16)
        terms = kept
    return terms[0]


def pick(blocks, index):
    return lax.dynamic_index_in_dim(blocks, index, 0, keepdims=False)


def place(blocks, sources):
    total = jnp.zeros((len(blocks),) + blocks[0].shape, blocks[0].dtype)
    for block, source in zip(blocks, sources):
        total = lax.dynamic_update_index_in_dim(total, block, source, 0)
    return total


def gather_rows(block, order, me):
    rows = block.shape
    done = []
    for bit in order:
        other = hop(block, bit)
        axis = sum(1 for b in done if b > bit)
        block = jnp.where(
            ((me >> bit) & 1) == 0,
            jnp.stack([block, other], axis),
            jnp.stack([other, block], axis),
        )
        done.append(bit)
    return block.reshape((-1,) + rows[1:])


def scatter_rows(term, order, me, size):
    bits = list(reversed(range(len(order))))
    term = term.reshape((2,) * len(order) + (term.shape[0] // size,) + term.shape[1:])
    for bit in order:
        axis = bits.index(bit)
        mine = (me >> bit) & 1
        kept = lax.dynamic_index_in_dim(term, mine, axis, keepdims=False)
        sent = lax.dynamic_index_in_dim(term, 1 - mine, axis, keepdims=False)
        term = (kept.astype(F32) + hop(sent, bit).astype(F32)).astype(BF16)
        bits.remove(bit)
    return term


def kernel_call(body, out_shapes, operands, scalars=0, scratch=(), flops=0, limit=48):
    smem = pl.BlockSpec(memory_space=pltpu.SMEM)
    vmem = pl.BlockSpec(memory_space=pltpu.VMEM)
    nbytes = sum(o.size * o.dtype.itemsize for o in operands)
    nbytes += sum(o.size * o.dtype.itemsize for o in out_shapes)
    return pl.pallas_call(
        body,
        out_shape=out_shapes,
        in_specs=[smem] * scalars + [vmem] * (len(operands) - scalars),
        out_specs=[vmem] * len(out_shapes),
        scratch_shapes=list(scratch),
        compiler_params=pltpu.CompilerParams(vmem_limit_bytes=limit * 1024 * 1024),
        cost_estimate=pl.CostEstimate(flops=flops, bytes_accessed=nbytes, transcendentals=0),
    )(*operands)


def lane_in(width, low, high):
    lane = lax.broadcasted_iota(jnp.int32, (1, width), 1)
    return (lane >= low) & (lane < high)


def swap_body(width, count, me_ref, in_ref, out_ref):
    me = me_ref[0]
    for j in range(count):
        source = pl.multiple_of((me ^ j) * width, width)
        out_ref[:, j * width : (j + 1) * width] = in_ref[:, pl.ds(source, width)]


def swap_blocks(rows, me):
    count = lax.axis_size("dp")
    width = rows.shape[1] // count
    if width % LANES:
        blocks = rows.reshape(rows.shape[0], count, width)
        return jnp.take(blocks, me ^ jnp.arange(count), axis=1).reshape(rows.shape)
    (out,) = kernel_call(
        partial(swap_body, width, count),
        [jax.ShapeDtypeStruct(rows.shape, rows.dtype)],
        (me.reshape(1), rows),
        scalars=1,
    )
    return out


def attend_body(heads, first_ref, q_ref, k_ref, v_ref, att_ref, attf_ref, rden_ref):
    length = q_ref.shape[0]
    first = first_ref[0]
    qk_width = q_ref.shape[1]
    lower = lane_in(LANES, 0, DV)
    keys = k_ref[...]
    head_keys = [
        jnp.where(lane_in(qk_width, h * HF, (h + 1) * HF), keys, jnp.zeros_like(keys))
        for h in range(heads)
    ]
    head_values = []
    for h in range(heads):
        tile = v_ref[:, (h // 2) * LANES : (h // 2 + 1) * LANES]
        own = lower if h % 2 == 0 else jnp.logical_not(lower)
        head_values.append(jnp.where(own, tile, jnp.ones_like(tile)))
    for i in range(length // TILE):
        extent = (i + 1) * TILE
        rows = slice(i * TILE, extent)
        t_pos = i * TILE + lax.broadcasted_iota(jnp.int32, (TILE, 1), 0)
        s_pos = lax.broadcasted_iota(jnp.int32, (1, extent), 1)
        start = jnp.where(t_pos >= first, first, 0)
        allowed = (s_pos <= t_pos) & (s_pos >= start)
        queries = (q_ref[rows, :].astype(F32) * 0.25).astype(BF16)
        for pair in range(heads // 2):
            outs = []
            for h in (2 * pair, 2 * pair + 1):
                inner = dot_last(queries, head_keys[h][:extent])
                scores = jnp.where(allowed, 1.0 + inner * (1.0 + 0.5 * inner), 0.0)
                outs.append(matmul(scores.astype(BF16), head_values[h][:extent]))
            numer = jnp.where(lower, outs[0], outs[1])
            denom = pltpu.roll(jnp.where(lower, outs[1], outs[0]), DV, 1)
            recip = 1.0 / denom
            attended = numer * recip
            lanes = slice(pair * LANES, (pair + 1) * LANES)
            att_ref[rows, lanes] = attended.astype(BF16)
            attf_ref[rows, lanes] = attended
            rden_ref[rows, lanes] = recip


def attend_back_body(
    heads, first_ref, q_ref, k_ref, v_ref, ag_ref, attf_ref, rden_ref,
    qb_ref, kb_ref, vb_ref, qt_ref, aug_ref, nb_ref,
):
    length = q_ref.shape[0]
    first = first_ref[0]
    qk_width = q_ref.shape[1]
    lower = lane_in(LANES, 0, DV)
    queries = (q_ref[...].astype(F32) * 0.25).astype(BF16)
    keys = (k_ref[...].astype(F32) * 0.25).astype(BF16)
    head_queries, head_keys, head_values = [], [], []
    for h in range(heads):
        own = lane_in(qk_width, h * HF, (h + 1) * HF)
        head_queries.append(jnp.where(own, queries, jnp.zeros_like(queries)))
        head_keys.append(jnp.where(own, keys, jnp.zeros_like(keys)))
    for h in range(heads):
        lanes = slice((h // 2) * LANES, (h // 2 + 1) * LANES)
        own = lower if h % 2 == 0 else jnp.logical_not(lower)
        numer_bar = ag_ref[:, lanes].astype(F32) * rden_ref[:, lanes]
        products = jnp.where(own, numer_bar * attf_ref[:, lanes], 0.0)
        denom_bar = -jnp.sum(products, axis=1, keepdims=True)
        column = DV if h % 2 == 0 else 0
        numer_bar = jnp.where(own, numer_bar, 0.0)
        nb_ref[h] = numer_bar.astype(BF16)
        aug_ref[h] = jnp.where(
            lane_in(LANES, column, column + 1), denom_bar, numer_bar
        ).astype(BF16)
        tile = v_ref[:, lanes]
        head_values.append(jnp.where(own, tile, jnp.ones_like(tile)))
    qt_ref[...] = jnp.zeros_like(qt_ref)
    for i in range(length // TILE):
        low = i * TILE
        extent = length - low
        rows = slice(low, low + TILE)
        s_pos = low + lax.broadcasted_iota(jnp.int32, (TILE, 1), 0)
        t_pos = low + lax.broadcasted_iota(jnp.int32, (1, extent), 1)
        start = jnp.where(t_pos >= first, first, 0)
        allowed = (s_pos <= t_pos) & (s_pos >= start)
        key_total = jnp.zeros((TILE, qk_width), F32)
        query_total = jnp.zeros((qk_width, extent), F32)
        raw_keys = k_ref[rows, :]
        for pair in range(heads // 2):
            value_total = jnp.zeros((TILE, LANES), F32)
            for h in (2 * pair, 2 * pair + 1):
                inner = dot_last(raw_keys, head_queries[h][low:])
                scores = jnp.where(allowed, 1.0 + inner * (1.0 + 0.5 * inner), 0.0)
                value_total += matmul(scores.astype(BF16), nb_ref[h, low:, :])
                bar = dot_last(head_values[h][rows], aug_ref[h, low:, :])
                slope = jnp.where(allowed, bar * (1.0 + inner), 0.0).astype(BF16)
                key_total += matmul(slope, head_queries[h][low:])
                query_total += dot_first(head_keys[h][rows], slope)
            vb_ref[rows, pair * LANES : (pair + 1) * LANES] = value_total.astype(BF16)
        kb_ref[rows, :] = key_total.astype(BF16)
        qt_ref[:, low:] += query_total
    qb_ref[...] = qt_ref[...].T.astype(BF16)


def attend(first, queries, keys, values):
    length, width = values.shape
    heads = width // DV
    return kernel_call(
        partial(attend_body, heads),
        [
            jax.ShapeDtypeStruct((length, width), BF16),
            jax.ShapeDtypeStruct((length, width), F32),
            jax.ShapeDtypeStruct((length, width), F32),
        ],
        (first, queries, keys, values),
        scalars=1,
        flops=2 * heads * length * length * 256,
    )


def attend_back(first, queries, keys, values, att_grad, attf, rden):
    length, width = values.shape
    heads = width // DV
    qk_shape = jax.ShapeDtypeStruct(queries.shape, BF16)
    return kernel_call(
        partial(attend_back_body, heads),
        [qk_shape, qk_shape, jax.ShapeDtypeStruct((length, width), BF16)],
        (first, queries, keys, values, att_grad, attf, rden),
        scalars=1,
        scratch=(
            pltpu.VMEM((queries.shape[1], length), F32),
            pltpu.VMEM((heads, length, LANES), BF16),
            pltpu.VMEM((heads, length, LANES), BF16),
        ),
        flops=5 * heads * length * length * 256,
    )


def norm_scale(rows):
    return lax.rsqrt(jnp.mean(rows * rows, axis=-1, keepdims=True) + EPSILON)


def norm_back(rows, scale, gain, grad):
    inner = jnp.mean(rows * gain * grad, axis=-1, keepdims=True)
    return scale * gain * grad - rows * (scale * scale * scale) * inner


def feed_forward(mlp_rows, cot_rows, gate_mat, up_mat, down_mat):
    gate_value = dot_last(mlp_rows, gate_mat)
    up_proj = dot_last(mlp_rows, up_mat)
    sig = 1.0 / (1.0 + jnp.exp(-gate_value))
    silu = gate_value * sig
    activation = (silu * up_proj).astype(BF16)
    branch = matmul(activation, down_mat)
    activation_grad = dot_last(cot_rows, down_mat)
    gate_bar = (activation_grad * up_proj * sig * (1.0 + gate_value * (1.0 - sig))).astype(BF16)
    up_bar = (activation_grad * silu).astype(BF16)
    down_term = dot_first(activation, cot_rows).astype(BF16)
    gate_term = dot_first(gate_bar, mlp_rows).astype(BF16)
    up_term = dot_first(up_bar, mlp_rows).astype(BF16)
    input_part = matmul(gate_bar, gate_mat) + matmul(up_bar, up_mat)
    return branch, input_part, gate_term, up_term, down_term


def on_device(
    hidden_in,
    query_weight,
    key_weight,
    value_weight,
    output_weight,
    gate_weight,
    up_weight,
    down_weight,
    gain_attn,
    gain_mlp,
    first_length,
    cotangent,
):
    groups = lax.axis_size("feat")
    member = lax.axis_index("feat")
    size = lax.axis_size("dp")
    me = lax.axis_index("dp")
    bits = size.bit_length() - 1
    links = list(range(1, bits))
    orders = (links, links[::-1])
    core = me & 1
    tokens, width = hidden_in.shape
    shifts = range(groups)
    ahead = [(member + s) % groups for s in shifts]
    behind = [(member - s) % groups for s in shifts]

    hidden_rel = [hidden_in] + [turn(hidden_in, s) for s in shifts[1:]]

    rows = query_weight.shape[0]
    qk = H * HF // groups
    vw = H * DV // groups
    gains = jnp.stack([gain_attn, gain_mlp], axis=1)
    gains = jnp.pad(gains, ((0, 0), (0, LANES - 2)))
    attn_pack = jnp.concatenate(
        [
            query_weight.reshape(rows, groups, qk),
            key_weight.reshape(rows, groups, qk),
            value_weight.reshape(rows, groups, vw),
            jnp.broadcast_to(gains[:, None, :], (rows, groups, LANES)),
        ],
        axis=2,
    ).transpose(1, 0, 2)
    attn_rel = [pick(attn_pack, member)]
    attn_rel += [turn(pick(attn_pack, ahead[s]), s) for s in shifts[1:]]
    attn_mat = place(attn_rel, behind).reshape(groups * rows, -1)
    attn_mat = gather_rows(attn_mat, links + [0], me)
    attn_scale = attn_mat[:, 2 * qk + vw].astype(F32)
    mlp_scale = attn_mat[:, 2 * qk + vw + 1].astype(F32)
    attn_mat = attn_mat[:, : 2 * qk + vw]

    output_rel = output_weight.T
    output_mat = place([output_rel] + [turn(output_rel, s) for s in shifts[1:]], behind)
    output_mat = gather_rows(output_mat.reshape(groups * rows, -1), links + [0], me)

    units = down_weight.shape[0]
    half = -(-units // 32) * 16
    stacked = jnp.stack([gate_weight.T, up_weight.T, down_weight])
    stacked = jnp.pad(stacked, ((0, 0), (0, 2 * half - units), (0, 0)))
    block = stacked.shape[2]
    stacked = stacked.reshape(3, 2, half, block).transpose(1, 0, 2, 3).reshape(2, 3 * half, block)
    own = jnp.concatenate([pick(stacked, core), hop(pick(stacked, 1 - core), 0)], axis=1)
    slots = [own] + [turn(own, s) for s in shifts[1:]]
    slots = [spread(slot, orders[s % 2]) for s, slot in enumerate(slots)]
    piece_ids = sorted(slots[0])
    slots = [jnp.concatenate([slot[j] for j in piece_ids], axis=1) for slot in slots]
    gate_mat, up_mat, down_mat = (
        jnp.concatenate([slot[m * half : (m + 1) * half] for slot in slots], axis=0)
        for m in range(3)
    )
    cot_pair = jnp.concatenate([cotangent, hop(cotangent, 0)], axis=0)

    attn_in, projected = [], []
    for rows_in in hidden_rel:
        rows_in = rows_in.astype(F32)
        normed = (rows_in * norm_scale(rows_in) * attn_scale).astype(BF16)
        attn_in.append(normed)
        projected.append(matmul(normed, attn_mat).astype(BF16))
    projected = place(projected, behind).reshape(groups * tokens, -1)
    queries = projected[:, :qk]
    keys = projected[:, qk : 2 * qk]
    values = projected[:, 2 * qk :]
    attended, attf, rden = attend(first_length, queries, keys, values)
    attended = attended.reshape(groups, tokens, vw)
    heads_rel = [pick(attended, member)]
    heads_rel += [turn(pick(attended, ahead[s]), s) for s in shifts[1:]]
    attended = place(heads_rel, behind).transpose(1, 0, 2).reshape(tokens, H * DV)

    residual = hidden_in.astype(F32)
    middle = residual + dot_last(attended, output_mat)
    middle_scale = norm_scale(middle)
    mlp_in = (middle * middle_scale * mlp_scale).astype(BF16)

    mlp_pair = jnp.concatenate([mlp_in, hop(mlp_in, 0)], axis=0)
    mlp_pair = swap_blocks(mlp_pair, me)
    cot_pair = swap_blocks(cot_pair, me)
    branch, input_part, gate_term, up_term, down_term = feed_forward(
        mlp_pair, cot_pair, gate_mat, up_mat, down_mat
    )
    branch = swap_blocks(branch, me)
    input_part = swap_blocks(input_part, me)
    mlp_in_grad = input_part[:tokens] + hop(input_part[tokens:].astype(BF16), 0).astype(F32)
    branch = branch[:tokens] + hop(branch[tokens:].astype(BF16), 0).astype(F32)
    block_out = (middle + branch).astype(BF16)

    middle_grad = cotangent.astype(F32) + norm_back(middle, middle_scale, mlp_scale, mlp_in_grad)
    mlp_gain_term = jnp.sum(mlp_in_grad * middle * middle_scale, axis=0)
    middle_bar = middle_grad.astype(BF16)
    att_grad = matmul(middle_bar, output_mat).astype(BF16)
    att_grad = att_grad.reshape(tokens, groups, vw).transpose(1, 0, 2)
    grad_rel = [pick(att_grad, member)]
    grad_rel += [turn(pick(att_grad, ahead[s]), s) for s in shifts[1:]]
    att_grad = place(grad_rel, behind).reshape(groups * tokens, vw)

    query_bar, key_bar, value_bar = attend_back(
        first_length, queries, keys, values, att_grad, attf, rden
    )
    bars = jnp.concatenate([query_bar, key_bar, value_bar], axis=1)
    bars = bars.reshape(groups, tokens, -1)
    bars_rel = [pick(bars, behind[s]) for s in shifts]
    attn_in_grad = dot_last(bars_rel[0], attn_mat)
    for s in shifts[1:]:
        part = dot_last(pick(bars, ahead[s]), attn_mat).astype(BF16)
        attn_in_grad = attn_in_grad + turn(part, s).astype(F32)
    attn_term = sum(dot_first(attn_in[s], bars_rel[s]) for s in shifts).astype(BF16)
    attn_term = scatter_rows(attn_term, [0] + links[::-1], me, size)
    attn_term = attn_term.reshape(groups, rows, -1)
    term_rel = [pick(attn_term, member)]
    term_rel += [turn(pick(attn_term, ahead[s]), s) for s in shifts[1:]]
    attn_grad = place(term_rel, behind).astype(F32).transpose(1, 0, 2)
    query_grad = attn_grad[:, :, :qk].reshape(rows, H * HF)
    key_grad = attn_grad[:, :, qk : 2 * qk].reshape(rows, H * HF)
    value_grad = attn_grad[:, :, 2 * qk :].reshape(rows, H * DV)

    attn_gain_grad = (
        jnp.sum(query_grad * query_weight.astype(F32), axis=1)
        + jnp.sum(key_grad * key_weight.astype(F32), axis=1)
        + jnp.sum(value_grad * value_weight.astype(F32), axis=1)
    ) / gain_attn.astype(F32)
    input_grad = middle_grad + norm_back(residual, norm_scale(residual), attn_scale, attn_in_grad)

    output_term = jnp.concatenate(
        [
            dot_first(middle_bar, attended),
            jnp.pad(mlp_gain_term[:, None], ((0, 0), (0, LANES - 1))),
        ],
        axis=1,
    ).astype(BF16)
    output_term = scatter_rows(output_term, [0] + links, me, size).reshape(groups, rows, -1)
    output_sum = pick(output_term, member).astype(F32)
    for s in shifts[1:]:
        output_sum = output_sum + turn(pick(output_term, ahead[s]), s).astype(F32)
    output_grad = output_sum[:, : H * DV].T
    mlp_gain_grad = output_sum[:, H * DV]

    unit_width = 2 * block
    totals = []
    for s in shifts:
        terms = {}
        for place_of, j in enumerate(piece_ids):
            lanes = slice(place_of * unit_width, (place_of + 1) * unit_width)
            terms[j] = jnp.concatenate(
                [term[s * half : (s + 1) * half, lanes] for term in (gate_term, up_term, down_term)],
                axis=0,
            )
        totals.append(collect(terms, orders[s % 2]))
    total = totals[0].astype(F32)
    for s in shifts[1:]:
        total = total + turn(totals[s], -s).astype(F32)
    mine, other = total[:, :block], hop(total[:, block:], 0)
    total = jnp.where(core == 0, jnp.stack([mine, other]), jnp.stack([other, mine]))
    total = total.reshape(2, 3, half, block).transpose(1, 0, 2, 3)
    total = total.reshape(3, 2 * half, block)[:, :units]
    return (
        block_out,
        input_grad,
        query_grad,
        key_grad,
        value_grad,
        output_grad,
        total[0].T,
        total[1].T,
        total[2],
        attn_gain_grad,
        mlp_gain_grad,
    )


def solution(mesh):
    both = ("dp", "feat")
    in_specs = (
        P(both, None),
        P(both, None),
        P(both, None),
        P(both, None),
        P(None, both),
        P("dp", "feat"),
        P("dp", "feat"),
        P("feat", "dp"),
        P(both),
        P(both),
        P("dp"),
        P(both, None),
    )
    out_specs = (
        P(both, None),
        P(both, None),
        P(both, None),
        P(both, None),
        P(both, None),
        P(None, both),
        P("dp", "feat"),
        P("dp", "feat"),
        P("feat", "dp"),
        P(both),
        P(both),
    )
    return jax.shard_map(
        on_device, mesh=mesh, in_specs=in_specs, out_specs=out_specs, check_vma=False
    )
```

```python
from functools import partial

import jax
import jax.numpy as jnp
from jax import lax
from jax.experimental import pallas as pl
from jax.experimental.pallas import tpu as pltpu
from jax.sharding import PartitionSpec as P

H = 16
HF = 16
DV = 64
SEQ_LEN = 1024
EPSILON = 1e-05

LANES = 128
TILE = 256
GROUPS = 4
F32 = jnp.float32
BF16 = jnp.bfloat16

SLOT_MASKS = (0, 2, 1, 3)
SPLIT_BITS = 2
SPLIT = 1 << SPLIT_BITS


def matmul(first_matrix, second_matrix):
    return jnp.dot(first_matrix, second_matrix, preferred_element_type=F32)


def dot_first(first_matrix, second_matrix):
    return lax.dot_general(
        first_matrix, second_matrix, (((0,), (0,)), ((), ())), preferred_element_type=F32
    )


def dot_last(first_matrix, second_matrix):
    return lax.dot_general(
        first_matrix, second_matrix, (((1,), (1,)), ((), ())), preferred_element_type=F32
    )


def hop(block, bit):
    return lax.ppermute(block, f"bit{bit}", [(0, 1), (1, 0)])


def cross(block, mask):
    return lax.ppermute(block, "feat", [(i, i ^ mask) for i in range(GROUPS)])


def home_pairs(mask):
    pairs = []
    for core in range(2):
        for z in range(GROUPS):
            group = 2 * (z & 1) + core
            pairs.append((core * GROUPS + z, (z >> 1) * GROUPS + (group ^ mask)))
    return pairs


def home(block, mask):
    return lax.ppermute(block, ("bit0", "feat"), home_pairs(mask))


def away(block, mask):
    return lax.ppermute(block, ("bit0", "feat"), [(b, a) for a, b in home_pairs(mask)])


def after(block, *earlier):
    return lax.optimization_barrier((block,) + earlier)[0]


def add_rounded(first, second):
    return (first.astype(F32) + second.astype(F32)).astype(BF16)


def pick(blocks, index, axis=0):
    return lax.dynamic_index_in_dim(blocks, index, axis, keepdims=False)


def place(blocks, sources):
    total = jnp.zeros((len(blocks),) + blocks[0].shape, blocks[0].dtype)
    for block, source in zip(blocks, sources):
        total = lax.dynamic_update_index_in_dim(total, block, source, 0)
    return total


def pair_up(bit, own, other, axis):
    return jnp.where(bit == 0, jnp.stack([own, other], axis), jnp.stack([other, own], axis))


def kernel_call(body, outs, operands, scalars=0, remote=0, scratch=(), flops=0, limit=56):
    smem = pl.BlockSpec(memory_space=pltpu.SMEM)
    vmem = pl.BlockSpec(memory_space=pltpu.VMEM)
    hbm = pl.BlockSpec(memory_space=pl.ANY)
    outs = [jax.ShapeDtypeStruct(shape, dtype) for shape, dtype in outs]
    nbytes = sum(o.size * o.dtype.itemsize for o in list(operands) + outs)
    plain = len(operands) - scalars - remote
    return pl.pallas_call(
        body,
        out_shape=outs,
        in_specs=[smem] * scalars + [vmem] * plain + [hbm] * remote,
        out_specs=[vmem] * len(outs),
        scratch_shapes=list(scratch),
        compiler_params=pltpu.CompilerParams(vmem_limit_bytes=limit * 1024 * 1024),
        cost_estimate=pl.CostEstimate(flops=flops, bytes_accessed=nbytes, transcendentals=0),
    )(*operands)


def lane_in(width, low, high):
    lane = lax.broadcasted_iota(jnp.int32, (1, width), 1)
    return (lane >= low) & (lane < high)


def block_at(index, size):
    return pl.ds(pl.multiple_of(index * size, size), size)


def masked(own, values):
    return jnp.where(own, values, jnp.zeros_like(values))


def front_body(
    first_ref, group_ref, h0_ref, h1_ref, pair_ref, w_ref,
    hr_ref, qkv_ref, kept_ref, sent_ref, attf_ref, rden_ref, att_ref,
):
    first, group = first_ref[0], group_ref[0]
    tokens = h0_ref.shape[0]
    length, width = att_ref.shape
    heads = width // DV
    qk = heads * HF
    for k, (h_ref, at) in enumerate(((h0_ref, 0), (h1_ref, 0), (pair_ref, 0), (pair_ref, tokens))):
        rows = h_ref[at : at + tokens, :].astype(F32)
        scale = lax.rsqrt(jnp.mean(rows * rows, axis=1, keepdims=True) + EPSILON)
        normed = (rows * scale).astype(BF16)
        hr_ref[k] = normed
        qkv_ref[block_at(group ^ SLOT_MASKS[k], tokens), :] = matmul(normed, w_ref[...]).astype(BF16)
    lower = lane_in(LANES, 0, DV)
    keys = qkv_ref[:, qk : 2 * qk]
    head_keys = [masked(lane_in(qk, h * HF, (h + 1) * HF), keys) for h in range(heads)]
    head_values = []
    for h in range(heads):
        low = 2 * qk + (h // 2) * LANES
        tile = qkv_ref[:, low : low + LANES]
        own = lower if h % 2 == 0 else jnp.logical_not(lower)
        head_values.append(jnp.where(own, tile, jnp.ones_like(tile)))
    for i in range(length // TILE):
        extent = (i + 1) * TILE
        rows = slice(i * TILE, extent)
        t_pos = i * TILE + lax.broadcasted_iota(jnp.int32, (TILE, 1), 0)
        s_pos = lax.broadcasted_iota(jnp.int32, (1, extent), 1)
        start = jnp.where(t_pos >= first, first, 0)
        allowed = (s_pos <= t_pos) & (s_pos >= start)
        queries = (qkv_ref[rows, :qk].astype(F32) * 0.25).astype(BF16)
        for pair in range(heads // 2):
            outs = []
            for h in (2 * pair, 2 * pair + 1):
                inner = dot_last(queries, head_keys[h][:extent])
                scores = jnp.where(allowed, 1.0 + inner * (1.0 + 0.5 * inner), 0.0)
                outs.append(matmul(scores.astype(BF16), head_values[h][:extent]))
            numer = jnp.where(lower, outs[0], outs[1])
            denom = pltpu.roll(jnp.where(lower, outs[1], outs[0]), DV, 1)
            recip = 1.0 / denom
            attended = numer * recip
            lanes = slice(pair * LANES, (pair + 1) * LANES)
            att_ref[rows, lanes] = attended.astype(BF16)
            attf_ref[rows, lanes] = attended
            rden_ref[rows, lanes] = recip
    for k, mask in enumerate(SLOT_MASKS):
        out_ref = (kept_ref, sent_ref)[k // 2]
        at = (k % 2) * width
        out_ref[:, at : at + width] = att_ref[block_at(group ^ mask, tokens), :]


def back_body(
    first_ref, group_ref, g0_ref, g1_ref, near_ref, qkv_ref, attf_ref, rden_ref, hr_ref, w_ref,
    kept_ref, sent_ref, term_ref, qt_ref, aug_ref, nb_ref, ag_ref, bars_ref,
):
    first, group = first_ref[0], group_ref[0]
    tokens = g0_ref.shape[0]
    length, width = ag_ref.shape
    heads = width // DV
    qk = heads * HF
    for k, (g_ref, at) in enumerate(((g0_ref, 0), (g1_ref, 0), (near_ref, 0), (near_ref, width))):
        ag_ref[block_at(group ^ SLOT_MASKS[k], tokens), :] = g_ref[:, at : at + width]
    lower = lane_in(LANES, 0, DV)
    queries = (qkv_ref[:, :qk].astype(F32) * 0.25).astype(BF16)
    raw_keys = qkv_ref[:, qk : 2 * qk]
    keys = (raw_keys.astype(F32) * 0.25).astype(BF16)
    head_queries, head_keys, head_values = [], [], []
    for h in range(heads):
        own = lane_in(qk, h * HF, (h + 1) * HF)
        head_queries.append(masked(own, queries))
        head_keys.append(masked(own, keys))
    for h in range(heads):
        lanes = slice((h // 2) * LANES, (h // 2 + 1) * LANES)
        own = lower if h % 2 == 0 else jnp.logical_not(lower)
        numer_bar = ag_ref[:, lanes].astype(F32) * rden_ref[:, lanes]
        products = jnp.where(own, numer_bar * attf_ref[:, lanes], 0.0)
        denom_bar = -jnp.sum(products, axis=1, keepdims=True)
        column = DV if h % 2 == 0 else 0
        numer_bar = jnp.where(own, numer_bar, 0.0)
        nb_ref[h] = numer_bar.astype(BF16)
        aug_ref[h] = jnp.where(
            lane_in(LANES, column, column + 1), denom_bar, numer_bar
        ).astype(BF16)
        low = 2 * qk + (h // 2) * LANES
        tile = qkv_ref[:, low : low + LANES]
        head_values.append(jnp.where(own, tile, jnp.ones_like(tile)))
    qt_ref[...] = jnp.zeros_like(qt_ref)
    for i in range(length // TILE):
        low = i * TILE
        extent = length - low
        rows = slice(low, low + TILE)
        s_pos = low + lax.broadcasted_iota(jnp.int32, (TILE, 1), 0)
        t_pos = low + lax.broadcasted_iota(jnp.int32, (1, extent), 1)
        start = jnp.where(t_pos >= first, first, 0)
        allowed = (s_pos <= t_pos) & (s_pos >= start)
        key_total = jnp.zeros((TILE, qk), F32)
        query_total = jnp.zeros((qk, extent), F32)
        for pair in range(heads // 2):
            value_total = jnp.zeros((TILE, LANES), F32)
            for h in (2 * pair, 2 * pair + 1):
                inner = dot_last(raw_keys[rows], head_queries[h][low:])
                scores = jnp.where(allowed, 1.0 + inner * (1.0 + 0.5 * inner), 0.0)
                value_total += matmul(scores.astype(BF16), nb_ref[h, low:, :])
                bar = dot_last(head_values[h][rows], aug_ref[h, low:, :])
                slope = jnp.where(allowed, bar * (1.0 + inner), 0.0).astype(BF16)
                key_total += matmul(slope, head_queries[h][low:])
                query_total += dot_first(head_keys[h][rows], slope)
            lanes = slice(2 * qk + pair * LANES, 2 * qk + (pair + 1) * LANES)
            bars_ref[rows, lanes] = value_total.astype(BF16)
        bars_ref[rows, qk : 2 * qk] = key_total.astype(BF16)
        qt_ref[:, low:] += query_total
    bars_ref[:, :qk] = qt_ref[...].T.astype(BF16)
    term = jnp.zeros((bars_ref.shape[1], hr_ref.shape[2]), F32)
    for k, mask in enumerate(SLOT_MASKS):
        bars = bars_ref[block_at(group ^ mask, tokens), :]
        (kept_ref, sent_ref)[k // 2][k % 2] = dot_last(bars, w_ref[...]).astype(BF16)
        term += dot_first(bars, hr_ref[k])
    term_ref[...] = term.T.astype(BF16)


def middle_body(
    member_ref, a0_ref, a1_ref, hidden_ref, w_ref,
    middle_ref, mlp_ref, att_ref, gain_ref,
):
    member = member_ref[0]
    part = a0_ref.shape[1] // 2
    for m, mask in enumerate((0, 1, 2, 3)):
        at = (m % 2) * part
        att_ref[:, block_at(member ^ mask, part)] = (a0_ref, a1_ref)[m // 2][:, at : at + part]
    width = att_ref.shape[1]
    pick_gain = jnp.where(lane_in(LANES, 0, 1), jnp.ones((8, LANES), BF16), 0)
    gain = dot_last(pick_gain, w_ref[:, width:])
    gain_ref[...] = gain
    middle = hidden_ref[...].astype(F32) + dot_last(att_ref[...], w_ref[:, :width])
    middle_ref[...] = middle
    scale = lax.rsqrt(jnp.mean(middle * middle, axis=1, keepdims=True) + EPSILON)
    mlp_ref[...] = (middle * scale * gain[:1]).astype(BF16)


def middle_back_body(
    member_ref, own_ref, near_ref, far_ref, middle_ref, gain_ref, cot_ref, attended_ref, w_ref,
    grad_ref, g0_ref, g1_ref, out_ref, att_ref,
):
    member = member_ref[0]
    width = att_ref.shape[1]
    part = g0_ref.shape[1] // 2
    gain = gain_ref[:1]
    mlp_grad = own_ref[...].astype(F32) + near_ref[...].astype(F32) + far_ref[...].astype(F32)
    middle = middle_ref[...]
    scale = lax.rsqrt(jnp.mean(middle * middle, axis=1, keepdims=True) + EPSILON)
    normed = middle * scale
    scaled = mlp_grad * gain
    inner = jnp.mean(normed * scaled, axis=1, keepdims=True)
    grad = cot_ref[...].astype(F32) + scale * (scaled - normed * inner)
    grad_ref[...] = grad
    bar = grad.astype(BF16)
    att_ref[...] = matmul(bar, w_ref[:, :width]).astype(BF16)
    for m, mask in enumerate((0, 1, 2, 3)):
        at = (m % 2) * part
        (g0_ref, g1_ref)[m // 2][:, at : at + part] = att_ref[:, block_at(member ^ mask, part)]
    out_ref[:, :width] = dot_first(bar, attended_ref[...]).astype(BF16)
    term = jnp.sum(mlp_grad * normed, axis=0, keepdims=True)
    out_ref[:, width:] = jnp.broadcast_to(term, (LANES, term.shape[1])).T.astype(BF16)


def load_units(units, piece_ref, weight_refs, sems):
    parts, slots, _, part = piece_ref.shape
    copies = []
    for m, w_ref in enumerate(weight_refs):
        for y in range(parts):
            for s in range(slots):
                copies.append(
                    pltpu.make_async_copy(
                        piece_ref.at[y, s, pl.ds(m * units, units), :],
                        w_ref.at[pl.ds(s * units, units), pl.ds(y * part, part)],
                        sems.at[(m * parts + y) * slots + s],
                    )
                )
    for copy in copies:
        copy.start()
    return copies


def forward_units(total, x_ref, c_ref, weight_refs, hidden_refs, put):
    wg_ref, wu_ref, wd_ref = weight_refs
    tokens = TILE
    edges = list(range(0, total, TILE)) + [total]
    spans = list(zip(edges[:-1], edges[1:]))

    for b in range(x_ref.shape[0] // tokens):
        rows = slice(b * tokens, (b + 1) * tokens)
        x_rows = x_ref[rows, :]
        c_rows = c_ref[rows, :]
        kept = []
        for low, high in spans:
            gate = dot_last(x_rows, wg_ref[low:high, :])
            up = dot_last(x_rows, wu_ref[low:high, :])
            back = dot_last(c_rows, wd_ref[low:high, :])
            sig = 1.0 / (1.0 + jnp.exp(-gate))
            silu = gate * sig
            act = (silu * up).astype(BF16)
            gate_bar = (back * up * (sig + silu * (1.0 - sig))).astype(BF16)
            up_bar = (back * silu).astype(BF16)
            for value, ref in zip((act, gate_bar, up_bar), hidden_refs):
                ref[low:high, rows] = value.T
            kept.append((act, gate_bar, up_bar))
        branch = sum(matmul(kept[n][0], wd_ref[low:high, :]) for n, (low, high) in enumerate(spans))
        grad = sum(matmul(kept[n][1], wg_ref[low:high, :]) for n, (low, high) in enumerate(spans))
        grad += sum(matmul(kept[n][2], wu_ref[low:high, :]) for n, (low, high) in enumerate(spans))
        put(b, branch, grad)


def forward_body(units, count, moved, *refs):
    me_ref, x_refs, c_refs, piece_ref, refs = refs[0], refs[1:4], refs[4:7], refs[7], refs[8:]
    grad_refs, branch_refs, refs = refs[:SPLIT], refs[SPLIT : SPLIT + 2], refs[SPLIT + 2 :]
    x_ref, c_ref, hidden_refs, weight_refs, sems = *refs[:2], refs[2:5], refs[5:8], refs[8]
    copies = load_units(units, piece_ref, weight_refs, sems)
    tokens = x_refs[0].shape[0]
    me = me_ref[0]
    block = x_ref.shape[1] // count
    for (own, far, pair), ref_out in ((x_refs, x_ref), (c_refs, c_ref)):
        for low, ref in ((0, own), (tokens, far), (2 * tokens, pair)):
            rows = slice(low, low + ref.shape[0])
            if moved:
                for j in range(count):
                    lanes = slice(j * block, (j + 1) * block)
                    ref_out[rows, lanes] = ref[:, block_at(me ^ j, block)]
            else:
                ref_out[rows, :] = ref[...]
    for copy in copies:
        copy.wait()

    def put(b, branch, grad):
        def store(ref, value):
            value = value.astype(BF16)
            if moved:
                for j in range(count):
                    ref[:, block_at(me ^ j, block)] = value[:, j * block : (j + 1) * block]
            else:
                ref[...] = value

        store(grad_refs[b], grad)
        store(branch_refs[b // 2].at[b % 2], branch)

    forward_units(weight_refs[0].shape[0], x_ref, c_ref, weight_refs, hidden_refs, put)


def weights_body(units, part_ref, x_ref, c_ref, act_ref, gate_ref, up_ref, term_ref):
    slots, _, part = term_ref.shape
    step = min(part, 256)
    for m, (left, right) in enumerate(((gate_ref, x_ref), (up_ref, x_ref), (act_ref, c_ref))):
        for at in range(0, part, step):
            lanes = pl.ds(pl.multiple_of(part_ref[0] * part + at, step), step)
            out = matmul(left[...], right[:, lanes]).astype(BF16)
            rows = slice(m * units, (m + 1) * units)
            for s in range(slots):
                term_ref[s, rows, at : at + step] = out[s * units : (s + 1) * units]


def on_device(
    dp,
    hidden_in,
    query_weight,
    key_weight,
    value_weight,
    output_weight,
    gate_weight,
    up_weight,
    down_weight,
    gain_attn,
    gain_mlp,
    first_length,
    cotangent,
):
    member = lax.axis_index("feat")
    me = lax.axis_index(dp)
    bits = len(dp)
    size = 1 << bits
    links = list(range(1, bits))
    core = me & 1
    group = 2 * (member & 1) + core
    tokens, width = hidden_in.shape
    length = GROUPS * tokens
    place_arr, member_arr, group_arr = (me % SPLIT).reshape(1), member.reshape(1), group.reshape(1)

    latest = {}

    def send(link, how, *blocks):
        blocks = [after(block, *latest.get(link, ())) for block in blocks]
        latest[link] = tuple(how(block) for block in blocks)
        return latest[link] if len(blocks) > 1 else latest[link][0]

    def link_of(bit):
        return ("core", "x", "y")[min(bit, 2)]

    def swap_bit(block, bit):
        return send(link_of(bit), partial(hop, bit=bit), block)

    def reduce_bits(term, order, left):
        left = sorted(left, reverse=True)
        for bit in order:
            axis = left.index(bit)
            mine = (me >> bit) & 1
            other = swap_bit(pick(term, 1 - mine, axis), bit)
            term = add_rounded(pick(term, mine, axis), other)
            left.remove(bit)
        return term

    rows = query_weight.shape[0]
    qk = H * HF // GROUPS
    vw = H * DV // GROUPS
    attn_pack = jnp.concatenate(
        [
            query_weight.reshape(rows, GROUPS, qk),
            key_weight.reshape(rows, GROUPS, qk),
            value_weight.reshape(rows, GROUPS, vw),
        ],
        axis=2,
    )
    attn_pack = (attn_pack.astype(F32) * gain_attn.astype(F32)[:, None, None]).astype(BF16)
    cols = attn_pack.shape[2]
    attn_pack = attn_pack.transpose(1, 0, 2).reshape(2, 2, rows, cols)
    sent = pick(attn_pack, 1 - core, 1).reshape(2 * rows, cols)
    lengths = jnp.broadcast_to(first_length.astype(BF16)[:, None], (16, cols))
    sent = swap_bit(jnp.concatenate([lengths, sent], axis=0), 0)
    first = jnp.where((member >> 1) == core, first_length, sent[0, :1].astype(jnp.int32))
    sent = sent[16:].reshape(2, rows, cols)
    attn_pack = pair_up(core, pick(attn_pack, core, 1), sent, 2)

    output_pack = jnp.concatenate(
        [output_weight.T, jnp.pad(gain_mlp[:, None], ((0, 0), (0, LANES - 1)))], axis=1
    )
    same = pick(attn_pack, member & 1).reshape(rows, 2 * cols)
    flip = pick(attn_pack, 1 - (member & 1)).reshape(rows, 2 * cols)
    far = cross(jnp.concatenate([same, flip, output_pack], axis=1), 2)
    flips = [
        jnp.concatenate([flip, output_pack], axis=1),
        far[:, 2 * cols :],
    ]
    near = cross(jnp.concatenate(flips, axis=0), 1)
    both = [
        jnp.concatenate([same, output_pack], axis=1),
        near[:rows],
        jnp.concatenate([far[:, : 2 * cols], far[:, 4 * cols :]], axis=1),
        near[rows:],
    ]
    hidden = [away(hidden_in, mask) for mask in (0, 2)]
    both = after(place(both, [member ^ m for m in range(GROUPS)]), *hidden)
    hidden_units = down_weight.shape[0]
    units = -(-hidden_units // (16 * SPLIT)) * 16
    stacked = jnp.stack([gate_weight.T, up_weight.T, down_weight])
    stacked = jnp.pad(stacked, ((0, 0), (0, SPLIT * units - hidden_units), (0, 0)))
    block = stacked.shape[2]
    aligned = block % LANES == 0
    stacked = stacked.reshape(3, 2, 2, units, block)
    side = (me >> 1) & 1
    kept = [pick(stacked, side, 1), swap_bit(pick(stacked, 1 - side, 1), 1)]
    sent = swap_bit(jnp.concatenate([pick(part, 1 - core, 1) for part in kept], axis=2), 0)
    kept = [pick(part, core, 1) for part in kept]
    own = jnp.concatenate([kept[0], sent[:, :, :block], kept[1], sent[:, :, block:]], axis=2)
    own = own.reshape(3 * units, SPLIT * block)
    cot_far = swap_bit(cotangent, 1)

    output_mat = both[:, :, 2 * cols :].reshape(GROUPS * rows, -1)
    output_mat = pair_up((me >> links[-1]) & 1, output_mat, swap_bit(output_mat, links[-1]), 0)
    attn_mat = both[:, :, : 2 * cols].reshape(GROUPS, rows, 2, cols).transpose(2, 0, 1, 3)
    for bit in links:
        attn_mat = pair_up((me >> bit) & 1, attn_mat, swap_bit(attn_mat, bit), 0)
        attn_mat = attn_mat.reshape((-1,) + attn_mat.shape[2:])
    attn_mat = attn_mat.reshape(width, cols)
    hidden_pair = swap_bit(jnp.concatenate(hidden, axis=0), 0)

    far_axes = dp[: bits - SPLIT_BITS] + ("feat",)
    pieces = lax.all_gather(after(own, *hidden), far_axes)
    pieces = pieces.reshape(-1, GROUPS, 3 * units, SPLIT * block)
    if not aligned:
        pieces = pieces.transpose(1, 2, 0, 3).reshape(1, GROUPS, 3 * units, width)

    def pair_with(own, far):
        return [own, far, swap_bit(jnp.concatenate([own, far], axis=0), 0)]


    hr, qkv, out, sent, attf, rden = kernel_call(
        front_body,
        [((GROUPS, tokens, width), BF16), ((length, cols), BF16)]
        + [((tokens, 2 * vw), BF16)] * 2
        + [((length, vw), F32)] * 2,
        (first, group_arr, *hidden, hidden_pair, attn_mat),
        scalars=2,
        scratch=(pltpu.VMEM((length, vw), BF16),),
        flops=8 * 2**30,
    )
    sent = swap_bit(sent, 0)
    for axis, bit in enumerate(links[-2::-1] + [0], 1):
        output_mat = pair_up((me >> bit) & 1, output_mat, swap_bit(output_mat, bit), axis)
    output_mat = output_mat.reshape(width, -1)
    cots = pair_with(cotangent, cot_far)
    out = [jnp.concatenate([part[:, at : at + vw] for part in (out, sent)], axis=1) for at in (0, vw)]
    out = [home(out[0], 0), home(out[1], 2)]
    middle, mlp_in, attended, gain8 = kernel_call(
        middle_body,
        [
            ((tokens, width), F32),
            ((tokens, width), BF16),
            ((tokens, H * DV), BF16),
            ((8, width), F32),
        ],
        (member_arr, *out, hidden_in, output_mat),
        scalars=1,
        flops=2**30,
    )

    mlps = pair_with(mlp_in, swap_bit(mlp_in, 1))
    swap = lambda v: v
    if not aligned:
        order = jnp.arange(size) ^ (me % SPLIT)
        swap = lambda v: jnp.take(
            v.reshape(v.shape[:-1] + (size, block)), order, axis=v.ndim - 1
        ).reshape(v.shape)
    rows_shape = ((SPLIT * tokens, width), BF16)

    hidden_shape = (GROUPS * units, SPLIT * tokens)
    *grads, branch, branch_sent, x_all, c_all, act_t, gate_t, up_t = kernel_call(
        partial(forward_body, units, size, aligned),
        [((tokens, width), BF16)] * SPLIT
        + [((2, tokens, width), BF16)] * 2
        + [rows_shape] * 2
        + [(hidden_shape, BF16)] * 3,
        (place_arr, *[swap(v) for v in mlps], *[swap(v) for v in cots], pieces),
        scalars=1,
        remote=1,
        scratch=(
            *[pltpu.VMEM((GROUPS * units, width), BF16)] * 3,
            pltpu.SemaphoreType.DMA((3 * GROUPS * pieces.shape[0],)),
        ),
        flops=12 * 2**30,
    )
    branch, branch_sent, grads = swap(branch), swap(branch_sent), [swap(v) for v in grads]
    grad_far = add_rounded(grads[1], swap_bit(grads[3], 0))
    grad_near = swap_bit(grads[2], 0)
    x_all = after(x_all, grad_far)
    grad_far = swap_bit(grad_far, 1)
    branch_sent = swap_bit(branch_sent, 0)
    branch_sum = add_rounded(branch[1], branch_sent[1])
    branch_far = swap_bit(branch_sum, 1)
    parts = pieces.shape[0]

    def weight_terms(part):
        (term,) = kernel_call(
            partial(weights_body, units),
            [((GROUPS, 3 * units, width // parts), BF16)],
            (part.reshape(1), x_all, c_all, act_t, gate_t, up_t),
            scalars=1,
            flops=6 * 2**30 // parts,
        )
        return term

    if parts == 2:
        part = me >> SPLIT_BITS
        term_sent, term = weight_terms(1 - part), weight_terms(part)
        term_sum = add_rounded(term, swap_bit(term_sent, SPLIT_BITS))
    else:
        far_bits = list(range(SPLIT_BITS, bits))[::-1]
        term = weight_terms(jnp.zeros((), jnp.int32))
        term_sum = term.reshape(GROUPS, 3 * units, -1, SPLIT * block).transpose(2, 0, 1, 3)
        term_sum = term_sum.reshape((2,) * len(far_bits) + term_sum.shape[1:])
        term_sum = reduce_bits(term_sum, far_bits, far_bits)
    total = lax.psum_scatter(term_sum, "feat")

    middle_grad, *att_grad, output_term = kernel_call(
        middle_back_body,
        [((tokens, width), F32)]
        + [((tokens, 2 * vw), BF16)] * 2
        + [((width, H * DV + LANES), BF16)],
        (member_arr, grads[0], grad_near, after(grad_far, term, branch_sum), middle, gain8, cotangent, attended, output_mat),
        scalars=1,
        scratch=(pltpu.VMEM((tokens, H * DV), BF16),),
        flops=2**30,
    )
    att_grad = [away(part, mask) for part, mask in zip(att_grad, (0, 2))]
    output_term = output_term.reshape((2,) * bits + (GROUPS, rows, H * DV + LANES))
    output_term = reduce_bits(output_term, [0], range(bits))
    att_sent = jnp.concatenate([part[:, vw:] for part in att_grad], axis=1)
    att_grad.append(swap_bit(att_sent, 0))
    output_term = reduce_bits(output_term, links[:1], links)
    att_grad = [after(part, term_sum) for part in att_grad]
    input_parts, input_sent, attn_term = kernel_call(
        back_body,
        [((2, tokens, width), BF16)] * 2 + [((width, cols), BF16)],
        (first, group_arr, *att_grad, qkv, attf, rden, hr, attn_mat),
        scalars=2,
        scratch=(
            pltpu.VMEM((qk, length), F32),
            pltpu.VMEM((vw // DV, length, LANES), BF16),
            pltpu.VMEM((vw // DV, length, LANES), BF16),
            pltpu.VMEM((length, vw), BF16),
            pltpu.VMEM((length, cols), BF16),
        ),
        flops=12 * 2**30,
    )
    input_sent = swap_bit(input_sent, 0)
    input_parts = [add_rounded(input_parts[k], input_sent[k]) for k in range(2)]
    input_parts = [home(input_parts[0], 0), home(input_parts[1], 2)]
    scaled_grad = input_parts[0].astype(F32) + input_parts[1].astype(F32)
    residual = hidden_in.astype(F32)
    scale = lax.rsqrt(jnp.mean(residual * residual, axis=1, keepdims=True) + EPSILON)
    normed = residual * scale
    inner = jnp.mean(normed * scaled_grad, axis=1, keepdims=True)
    input_grad = middle_grad + scale * (scaled_grad - normed * inner)

    attn_term = after(attn_term, input_sent).reshape((2,) * len(links) + (2, GROUPS, rows, cols))
    attn_term = reduce_bits(attn_term, links[:0:-1], links)
    output_term = reduce_bits(output_term, links[1:], links[1:])
    attn_term = reduce_bits(attn_term, links[:1], links[:1])
    attn_term = attn_term.transpose(1, 2, 0, 3).reshape(GROUPS, rows, 2 * cols)
    both = jnp.concatenate([attn_term, output_term], axis=2)
    both = [pick(both, member ^ m) for m in range(GROUPS)]
    both = [both[0]] + [cross(after(both[m], total), m) for m in range(1, GROUPS)]
    output_sum = sum(part[:, 2 * cols :].astype(F32) for part in both)
    output_grad = output_sum[:, : H * DV].T
    mlp_gain_grad = output_sum[:, H * DV]
    same = both[0][:, : 2 * cols].astype(F32) + both[2][:, : 2 * cols].astype(F32)
    flip = both[1][:, : 2 * cols].astype(F32) + both[3][:, : 2 * cols].astype(F32)
    halves = pair_up(member & 1, same, flip, 0).reshape(2, rows, 2, cols)
    halves = pair_up(core, pick(halves, core, 2), swap_bit(pick(halves, 1 - core, 2), 0), 1)
    attn_grad = halves.reshape(GROUPS, rows, cols).transpose(1, 0, 2)
    scale_rows = gain_attn.astype(F32)[:, None]
    query_raw = attn_grad[:, :, :qk].reshape(rows, H * HF)
    key_raw = attn_grad[:, :, qk : 2 * qk].reshape(rows, H * HF)
    value_raw = attn_grad[:, :, 2 * qk :].reshape(rows, H * DV)
    attn_gain_grad = (
        jnp.sum(query_raw * query_weight.astype(F32), axis=1)
        + jnp.sum(key_raw * key_weight.astype(F32), axis=1)
        + jnp.sum(value_raw * value_weight.astype(F32), axis=1)
    )

    block_out = (
        middle
        + branch[0].astype(F32)
        + branch_sent[0].astype(F32)
        + branch_far.astype(F32)
    ).astype(BF16)

    total = total.astype(F32)
    lanes = [slice(j * block, (j + 1) * block) for j in range(SPLIT)]
    near = swap_bit(jnp.concatenate([total[:, lanes[1]], total[:, lanes[3]]], axis=1), 0)
    far = jnp.concatenate([total[:, lanes[2]], near[:, block:]], axis=0).astype(BF16)
    far = swap_bit(far, 1).astype(F32)
    shares = [total[:, lanes[0]], near[:, :block], far[: 3 * units], far[3 * units :]]
    shares = [jnp.where(core == 0, shares[k], shares[k ^ 1]) for k in range(SPLIT)]
    shares = [jnp.where(side == 0, shares[k], shares[k ^ 2]) for k in range(SPLIT)]
    total = jnp.stack([share.reshape(3, units, block) for share in shares], axis=1)
    total = total.reshape(3, SPLIT * units, block)[:, :hidden_units]
    return (
        block_out,
        input_grad,
        query_raw * scale_rows,
        key_raw * scale_rows,
        value_raw * scale_rows,
        output_grad,
        total[0].T,
        total[1].T,
        total[2],
        attn_gain_grad,
        mlp_gain_grad,
    )


def solution(mesh):
    bits = mesh.shape["dp"].bit_length() - 1
    dp = tuple(f"bit{bit}" for bit in reversed(range(bits)))
    fine = jax.sharding.Mesh(mesh.devices.reshape((2,) * bits + (GROUPS,)), dp + ("feat",))
    both = dp + ("feat",)
    in_specs = (
        P(both, None),
        P(both, None),
        P(both, None),
        P(both, None),
        P(None, both),
        P(dp, "feat"),
        P(dp, "feat"),
        P("feat", dp),
        P(both),
        P(both),
        P(dp),
        P(both, None),
    )
    out_specs = (
        P(both, None),
        P(both, None),
        P(both, None),
        P(both, None),
        P(both, None),
        P(None, both),
        P(dp, "feat"),
        P(dp, "feat"),
        P("feat", dp),
        P(both),
        P(both),
    )
    return jax.shard_map(
        partial(on_device, dp), mesh=fine, in_specs=in_specs, out_specs=out_specs, check_vma=False
    )
```

```python
from functools import partial

import jax
import jax.numpy as jnp
from jax import lax
from jax.experimental import pallas as pl
from jax.experimental.pallas import tpu as pltpu
from jax.sharding import PartitionSpec as P

H = 16
HF = 16
DV = 64
SEQ_LEN = 1024
EPSILON = 1e-05

LANES = 128
TILE = 256
GROUPS = 4
F32 = jnp.float32
BF16 = jnp.bfloat16

SLOT_MASKS = (0, 2, 1, 3)
SPLIT_BITS = 2
SPLIT = 1 << SPLIT_BITS
TERM_ROWS = ((0, 256), (256, 528))


def matmul(first_matrix, second_matrix):
    return jnp.dot(first_matrix, second_matrix, preferred_element_type=F32)


def dot_first(first_matrix, second_matrix):
    return lax.dot_general(
        first_matrix, second_matrix, (((0,), (0,)), ((), ())), preferred_element_type=F32
    )


def dot_last(first_matrix, second_matrix):
    return lax.dot_general(
        first_matrix, second_matrix, (((1,), (1,)), ((), ())), preferred_element_type=F32
    )


def hop(block, bit):
    return lax.ppermute(block, f"bit{bit}", [(0, 1), (1, 0)])


def cross(block, mask):
    return lax.ppermute(block, "feat", [(i, i ^ mask) for i in range(GROUPS)])


def home_pairs(mask):
    pairs = []
    for core in range(2):
        for z in range(GROUPS):
            group = 2 * (z & 1) + core
            pairs.append((core * GROUPS + z, (z >> 1) * GROUPS + (group ^ mask)))
    return pairs


def home(block, mask):
    return lax.ppermute(block, ("bit0", "feat"), home_pairs(mask))


def away(block, mask):
    return lax.ppermute(block, ("bit0", "feat"), [(b, a) for a, b in home_pairs(mask)])


def after(block, *earlier):
    return lax.optimization_barrier((block,) + earlier)[0]


def add_rounded(first, second):
    return (first.astype(F32) + second.astype(F32)).astype(BF16)


def pick(blocks, index, axis=0):
    return lax.dynamic_index_in_dim(blocks, index, axis, keepdims=False)


def place(blocks, sources):
    total = jnp.zeros((len(blocks),) + blocks[0].shape, blocks[0].dtype)
    for block, source in zip(blocks, sources):
        total = lax.dynamic_update_index_in_dim(total, block, source, 0)
    return total


def pair_up(bit, own, other, axis):
    return jnp.where(bit == 0, jnp.stack([own, other], axis), jnp.stack([other, own], axis))


def kernel_call(body, outs, operands, scalars=0, remote=0, scratch=(), flops=0, limit=56):
    smem = pl.BlockSpec(memory_space=pltpu.SMEM)
    vmem = pl.BlockSpec(memory_space=pltpu.VMEM)
    hbm = pl.BlockSpec(memory_space=pl.ANY)
    out_specs = [hbm if len(out) > 2 else vmem for out in outs]
    outs = [jax.ShapeDtypeStruct(out[0], out[1]) for out in outs]
    nbytes = sum(o.size * o.dtype.itemsize for o in list(operands) + outs)
    plain = len(operands) - scalars - remote
    return pl.pallas_call(
        body,
        out_shape=outs,
        in_specs=[smem] * scalars + [vmem] * plain + [hbm] * remote,
        out_specs=out_specs,
        scratch_shapes=list(scratch),
        compiler_params=pltpu.CompilerParams(vmem_limit_bytes=limit * 1024 * 1024),
        cost_estimate=pl.CostEstimate(flops=flops, bytes_accessed=nbytes, transcendentals=0),
    )(*operands)


def lane_in(width, low, high):
    lane = lax.broadcasted_iota(jnp.int32, (1, width), 1)
    return (lane >= low) & (lane < high)


def block_at(index, size):
    return pl.ds(pl.multiple_of(index * size, size), size)


def masked(own, values):
    return jnp.where(own, values, jnp.zeros_like(values))


def front_body(
    first_ref, group_ref, h0_ref, h1_ref, pair_ref, w_ref,
    hr_ref, qkv_ref, kept_ref, sent_ref, attf_ref, rden_ref, att_ref,
):
    first, group = first_ref[0], group_ref[0]
    tokens = h0_ref.shape[0]
    length, width = att_ref.shape
    heads = width // DV
    qk = heads * HF
    for k, (h_ref, at) in enumerate(((h0_ref, 0), (h1_ref, 0), (pair_ref, 0), (pair_ref, tokens))):
        rows = h_ref[at : at + tokens, :].astype(F32)
        scale = lax.rsqrt(jnp.mean(rows * rows, axis=1, keepdims=True) + EPSILON)
        normed = (rows * scale).astype(BF16)
        hr_ref[k] = normed
        qkv_ref[block_at(group ^ SLOT_MASKS[k], tokens), :] = matmul(normed, w_ref[...]).astype(BF16)
    lower = lane_in(LANES, 0, DV)
    keys = qkv_ref[:, qk : 2 * qk]
    head_keys = [masked(lane_in(qk, h * HF, (h + 1) * HF), keys) for h in range(heads)]
    head_values = []
    for h in range(heads):
        low = 2 * qk + (h // 2) * LANES
        tile = qkv_ref[:, low : low + LANES]
        own = lower if h % 2 == 0 else jnp.logical_not(lower)
        head_values.append(jnp.where(own, tile, jnp.ones_like(tile)))
    for i in range(length // TILE):
        extent = (i + 1) * TILE
        rows = slice(i * TILE, extent)
        t_pos = i * TILE + lax.broadcasted_iota(jnp.int32, (TILE, 1), 0)
        s_pos = lax.broadcasted_iota(jnp.int32, (1, extent), 1)
        start = jnp.where(t_pos >= first, first, 0)
        allowed = (s_pos <= t_pos) & (s_pos >= start)
        queries = (qkv_ref[rows, :qk].astype(F32) * 0.25).astype(BF16)
        for pair in range(heads // 2):
            outs = []
            for h in (2 * pair, 2 * pair + 1):
                inner = dot_last(queries, head_keys[h][:extent])
                scores = jnp.where(allowed, 1.0 + inner * (1.0 + 0.5 * inner), 0.0)
                outs.append(matmul(scores.astype(BF16), head_values[h][:extent]))
            numer = jnp.where(lower, outs[0], outs[1])
            denom = pltpu.roll(jnp.where(lower, outs[1], outs[0]), DV, 1)
            recip = 1.0 / denom
            attended = numer * recip
            lanes = slice(pair * LANES, (pair + 1) * LANES)
            att_ref[rows, lanes] = attended.astype(BF16)
            attf_ref[rows, lanes] = attended
            rden_ref[rows, lanes] = recip
    for k, mask in enumerate(SLOT_MASKS):
        out_ref = (kept_ref, sent_ref)[k // 2]
        at = (k % 2) * width
        out_ref[:, at : at + width] = att_ref[block_at(group ^ mask, tokens), :]


def back_body(
    first_ref, group_ref, g0_ref, g1_ref, near_ref, qkv_ref, attf_ref, rden_ref, hr_ref, w_ref,
    kept_ref, sent_ref, term_ref, qt_ref, aug_ref, nb_ref, ag_ref, bars_ref,
):
    first, group = first_ref[0], group_ref[0]
    tokens = g0_ref.shape[0]
    length, width = ag_ref.shape
    heads = width // DV
    qk = heads * HF
    for k, (g_ref, at) in enumerate(((g0_ref, 0), (g1_ref, 0), (near_ref, 0), (near_ref, width))):
        ag_ref[block_at(group ^ SLOT_MASKS[k], tokens), :] = g_ref[:, at : at + width]
    lower = lane_in(LANES, 0, DV)
    queries = (qkv_ref[:, :qk].astype(F32) * 0.25).astype(BF16)
    raw_keys = qkv_ref[:, qk : 2 * qk]
    keys = (raw_keys.astype(F32) * 0.25).astype(BF16)
    head_queries, head_keys, head_values = [], [], []
    for h in range(heads):
        own = lane_in(qk, h * HF, (h + 1) * HF)
        head_queries.append(masked(own, queries))
        head_keys.append(masked(own, keys))
    for h in range(heads):
        lanes = slice((h // 2) * LANES, (h // 2 + 1) * LANES)
        own = lower if h % 2 == 0 else jnp.logical_not(lower)
        numer_bar = ag_ref[:, lanes].astype(F32) * rden_ref[:, lanes]
        products = jnp.where(own, numer_bar * attf_ref[:, lanes], 0.0)
        denom_bar = -jnp.sum(products, axis=1, keepdims=True)
        column = DV if h % 2 == 0 else 0
        numer_bar = jnp.where(own, numer_bar, 0.0)
        nb_ref[h] = numer_bar.astype(BF16)
        aug_ref[h] = jnp.where(
            lane_in(LANES, column, column + 1), denom_bar, numer_bar
        ).astype(BF16)
        low = 2 * qk + (h // 2) * LANES
        tile = qkv_ref[:, low : low + LANES]
        head_values.append(jnp.where(own, tile, jnp.ones_like(tile)))
    qt_ref[...] = jnp.zeros_like(qt_ref)
    for i in range(length // TILE):
        low = i * TILE
        extent = length - low
        rows = slice(low, low + TILE)
        s_pos = low + lax.broadcasted_iota(jnp.int32, (TILE, 1), 0)
        t_pos = low + lax.broadcasted_iota(jnp.int32, (1, extent), 1)
        start = jnp.where(t_pos >= first, first, 0)
        allowed = (s_pos <= t_pos) & (s_pos >= start)
        key_total = jnp.zeros((TILE, qk), F32)
        query_total = jnp.zeros((qk, extent), F32)
        for pair in range(heads // 2):
            value_total = jnp.zeros((TILE, LANES), F32)
            for h in (2 * pair, 2 * pair + 1):
                inner = dot_last(raw_keys[rows], head_queries[h][low:])
                scores = jnp.where(allowed, 1.0 + inner * (1.0 + 0.5 * inner), 0.0)
                value_total += matmul(scores.astype(BF16), nb_ref[h, low:, :])
                bar = dot_last(head_values[h][rows], aug_ref[h, low:, :])
                slope = jnp.where(allowed, bar * (1.0 + inner), 0.0).astype(BF16)
                key_total += matmul(slope, head_queries[h][low:])
                query_total += dot_first(head_keys[h][rows], slope)
            lanes = slice(2 * qk + pair * LANES, 2 * qk + (pair + 1) * LANES)
            bars_ref[rows, lanes] = value_total.astype(BF16)
        bars_ref[rows, qk : 2 * qk] = key_total.astype(BF16)
        qt_ref[:, low:] += query_total
    bars_ref[:, :qk] = qt_ref[...].T.astype(BF16)
    term = jnp.zeros((bars_ref.shape[1], hr_ref.shape[2]), F32)
    for k, mask in enumerate(SLOT_MASKS):
        bars = bars_ref[block_at(group ^ mask, tokens), :]
        (kept_ref, sent_ref)[k // 2][k % 2] = dot_last(bars, w_ref[...]).astype(BF16)
        term += dot_first(bars, hr_ref[k])
    term_ref[...] = term.T.astype(BF16)


def middle_body(
    member_ref, a0_ref, a1_ref, hidden_ref, w_ref,
    middle_ref, mlp_ref, att_ref, gain_ref,
):
    member = member_ref[0]
    part = a0_ref.shape[1] // 2
    for m, mask in enumerate((0, 1, 2, 3)):
        at = (m % 2) * part
        att_ref[:, block_at(member ^ mask, part)] = (a0_ref, a1_ref)[m // 2][:, at : at + part]
    width = att_ref.shape[1]
    pick_gain = jnp.where(lane_in(LANES, 0, 1), jnp.ones((8, LANES), BF16), 0)
    gain = dot_last(pick_gain, w_ref[:, width:])
    gain_ref[...] = gain
    middle = hidden_ref[...].astype(F32) + dot_last(att_ref[...], w_ref[:, :width])
    middle_ref[...] = middle
    scale = lax.rsqrt(jnp.mean(middle * middle, axis=1, keepdims=True) + EPSILON)
    mlp_ref[...] = (middle * scale * gain[:1]).astype(BF16)


def middle_back_body(
    member_ref, own_ref, near_ref, far_ref, middle_ref, gain_ref, cot_ref, attended_ref, w_ref,
    grad_ref, g0_ref, g1_ref, out_ref, att_ref,
):
    member = member_ref[0]
    width = att_ref.shape[1]
    part = g0_ref.shape[1] // 2
    gain = gain_ref[:1]
    mlp_grad = own_ref[0].astype(F32) + near_ref[0].astype(F32) + far_ref[...].astype(F32)
    middle = middle_ref[...]
    scale = lax.rsqrt(jnp.mean(middle * middle, axis=1, keepdims=True) + EPSILON)
    normed = middle * scale
    scaled = mlp_grad * gain
    inner = jnp.mean(normed * scaled, axis=1, keepdims=True)
    grad = cot_ref[...].astype(F32) + scale * (scaled - normed * inner)
    grad_ref[...] = grad
    bar = grad.astype(BF16)
    att_ref[...] = matmul(bar, w_ref[:, :width]).astype(BF16)
    for m, mask in enumerate((0, 1, 2, 3)):
        at = (m % 2) * part
        (g0_ref, g1_ref)[m // 2][:, at : at + part] = att_ref[:, block_at(member ^ mask, part)]
    out_ref[:, :width] = dot_first(bar, attended_ref[...]).astype(BF16)
    term = jnp.sum(mlp_grad * normed, axis=0, keepdims=True)
    out_ref[:, width:] = jnp.broadcast_to(term, (LANES, term.shape[1])).T.astype(BF16)


def start_copies(pairs, sems, first):
    copies = [
        pltpu.make_async_copy(source, target, sems.at[first + n])
        for n, (source, target) in enumerate(pairs)
    ]
    for copy in copies:
        copy.start()
    return copies


def wait_copies(copies):
    for copy in copies:
        copy.wait()


def feature_pairs(place, count, moved, own_order, device_order):
    if not moved:
        return [(own_order, device_order)]
    block = own_order.shape[1] // count
    return [
        (own_order.at[:, block_at(place ^ j, block)], device_order.at[:, pl.ds(j * block, block)])
        for j in range(count)
    ]


def row_pairs(place, count, moved, refs, out_ref):
    pairs, low = [], 0
    for ref in refs:
        rows = ref.shape[0]
        pairs += feature_pairs(place, count, moved, ref, out_ref.at[pl.ds(low, rows), :])
        low += rows
    return pairs


def unit_pairs(units, piece_ref, weight_refs):
    parts, slots, _, part = piece_ref.shape
    return [
        (
            piece_ref.at[y, s, pl.ds(m * units, units), :],
            w_ref.at[pl.ds(s * units, units), pl.ds(y * part, part)],
        )
        for m, w_ref in enumerate(weight_refs)
        for y in range(parts)
        for s in range(slots)
    ]


def forward_units(total, x_ref, c_ref, weight_refs, hidden_refs, put):
    wg_ref, wu_ref, wd_ref = weight_refs
    tokens = TILE
    edges = list(range(0, total, TILE)) + [total]
    spans = list(zip(edges[:-1], edges[1:]))

    for b in range(x_ref.shape[0] // tokens):
        rows = slice(b * tokens, (b + 1) * tokens)
        x_rows = x_ref[rows, :]
        c_rows = c_ref[rows, :]
        kept = []
        for low, high in spans:
            gate = dot_last(x_rows, wg_ref[low:high, :])
            up = dot_last(x_rows, wu_ref[low:high, :])
            back = dot_last(c_rows, wd_ref[low:high, :])
            sig = 1.0 / (1.0 + jnp.exp(-gate))
            silu = gate * sig
            act = (silu * up).astype(BF16)
            gate_bar = (back * up * (sig + silu * (1.0 - sig))).astype(BF16)
            up_bar = (back * silu).astype(BF16)
            for value, ref in zip((act, gate_bar, up_bar), hidden_refs):
                ref[low:high, rows] = value.T
            kept.append((act, gate_bar, up_bar))
        branch = sum(matmul(kept[n][0], wd_ref[low:high, :]) for n, (low, high) in enumerate(spans))
        grad = sum(matmul(kept[n][1], wg_ref[low:high, :]) for n, (low, high) in enumerate(spans))
        grad += sum(matmul(kept[n][2], wu_ref[low:high, :]) for n, (low, high) in enumerate(spans))
        put(b, branch, grad)


def weight_units(units, index, x_ref, c_ref, hidden_refs, term_ref):
    slots, _, part = term_ref.shape
    step = min(part, 256)
    act_ref, gate_ref, up_ref = hidden_refs
    for m, (left, right) in enumerate(((gate_ref, x_ref), (up_ref, x_ref), (act_ref, c_ref))):
        for at in range(0, part, step):
            lanes = pl.ds(pl.multiple_of(index * part + at, step), step)
            out = matmul(left[...], right[:, lanes]).astype(BF16)
            rows = slice(m * units, (m + 1) * units)
            for s in range(slots):
                term_ref[s, rows, at : at + step] = out[s * units : (s + 1) * units]


def feed_forward_body(units, count, moved, parts, *refs):
    spot_ref, x_refs, c_refs, piece_ref, refs = refs[0], refs[1:4], refs[4:7], refs[7], refs[8:]
    grad_refs, branch_refs, term_refs, refs = refs[:2], refs[2:4], refs[4 : 4 + 2 * parts], refs[4 + 2 * parts :]
    x_ref, c_ref, weight_refs, hidden_refs = refs[0], refs[1], refs[2:5], refs[5:8]
    branch_buf, grad_buf, term_buf, sems = refs[8:]
    place, index = spot_ref[0], spot_ref[1]
    pairs = row_pairs(place, count, moved, x_refs, x_ref)
    pairs += row_pairs(place, count, moved, c_refs, c_ref)
    pairs += unit_pairs(units, piece_ref, weight_refs)
    wait_copies(start_copies(pairs, sems, 0))
    stores = []

    def put(b, branch, grad):
        branch_buf[b] = branch.astype(BF16)
        grad_buf[b] = grad.astype(BF16)
        done = feature_pairs(place, count, moved, grad_refs[b // 2].at[b % 2], grad_buf.at[b])
        done += feature_pairs(place, count, moved, branch_refs[b // 2].at[b % 2], branch_buf.at[b])
        done = [(source, target) for target, source in done]
        stores.extend(start_copies(done, sems, len(pairs) + len(stores)))

    forward_units(weight_refs[0].shape[0], x_ref, c_ref, weight_refs, hidden_refs, put)
    for n in range(parts):
        which = index if n == parts - 1 else 1 - index
        weight_units(units, which, x_ref, c_ref, hidden_refs, term_buf.at[n])
        for h, rows in enumerate(TERM_ROWS):
            done = [(term_buf.at[n, :, pl.ds(rows[0], rows[1] - rows[0]), :], term_refs[2 * n + h])]
            stores.extend(start_copies(done, sems, len(pairs) + len(stores)))
    wait_copies(stores)


def on_device(
    dp,
    hidden_in,
    query_weight,
    key_weight,
    value_weight,
    output_weight,
    gate_weight,
    up_weight,
    down_weight,
    gain_attn,
    gain_mlp,
    first_length,
    cotangent,
):
    member = lax.axis_index("feat")
    me = lax.axis_index(dp)
    bits = len(dp)
    size = 1 << bits
    links = list(range(1, bits))
    core = me & 1
    group = 2 * (member & 1) + core
    tokens, width = hidden_in.shape
    length = GROUPS * tokens
    member_arr, group_arr = member.reshape(1), group.reshape(1)

    latest = {}

    def send(link, how, *blocks):
        blocks = [after(block, *latest.get(link, ())) for block in blocks]
        latest[link] = tuple(how(block) for block in blocks)
        return latest[link] if len(blocks) > 1 else latest[link][0]

    def link_of(bit):
        return ("core", "x", "y")[min(bit, 2)]

    def swap_bit(block, bit):
        return send(link_of(bit), partial(hop, bit=bit), block)

    def reduce_bits(term, order, left):
        left = sorted(left, reverse=True)
        for bit in order:
            axis = left.index(bit)
            mine = (me >> bit) & 1
            other = swap_bit(pick(term, 1 - mine, axis), bit)
            term = add_rounded(pick(term, mine, axis), other)
            left.remove(bit)
        return term

    rows = query_weight.shape[0]
    qk = H * HF // GROUPS
    vw = H * DV // GROUPS
    attn_pack = jnp.concatenate(
        [
            query_weight.reshape(rows, GROUPS, qk),
            key_weight.reshape(rows, GROUPS, qk),
            value_weight.reshape(rows, GROUPS, vw),
        ],
        axis=2,
    )
    attn_pack = (attn_pack.astype(F32) * gain_attn.astype(F32)[:, None, None]).astype(BF16)
    cols = attn_pack.shape[2]
    attn_pack = attn_pack.transpose(1, 0, 2).reshape(2, 2, rows, cols)
    sent = pick(attn_pack, 1 - core, 1).reshape(2 * rows, cols)
    lengths = jnp.broadcast_to(first_length.astype(BF16)[:, None], (16, cols))
    sent = swap_bit(jnp.concatenate([lengths, sent], axis=0), 0)
    first = jnp.where((member >> 1) == core, first_length, sent[0, :1].astype(jnp.int32))
    sent = sent[16:].reshape(2, rows, cols)
    attn_pack = pair_up(core, pick(attn_pack, core, 1), sent, 2)

    output_pack = jnp.concatenate(
        [output_weight.T, jnp.pad(gain_mlp[:, None], ((0, 0), (0, LANES - 1)))], axis=1
    )
    same = pick(attn_pack, member & 1).reshape(rows, 2 * cols)
    flip = pick(attn_pack, 1 - (member & 1)).reshape(rows, 2 * cols)
    far = cross(jnp.concatenate([same, flip, output_pack], axis=1), 2)
    flips = [
        jnp.concatenate([flip, output_pack], axis=1),
        far[:, 2 * cols :],
    ]
    hidden = [away(hidden_in, mask) for mask in (0, 2)]
    near = cross(after(jnp.concatenate(flips, axis=0), *hidden), 1)
    both = [
        jnp.concatenate([same, output_pack], axis=1),
        near[:rows],
        jnp.concatenate([far[:, : 2 * cols], far[:, 4 * cols :]], axis=1),
        near[rows:],
    ]
    both = after(place(both, [member ^ m for m in range(GROUPS)]), *hidden)
    hidden_units = down_weight.shape[0]
    units = -(-hidden_units // (16 * SPLIT)) * 16
    stacked = jnp.stack([gate_weight.T, up_weight.T, down_weight])
    stacked = jnp.pad(stacked, ((0, 0), (0, SPLIT * units - hidden_units), (0, 0)))
    block = stacked.shape[2]
    aligned = block % LANES == 0
    stacked = stacked.reshape(3, 2, 2, units, block)
    side = (me >> 1) & 1
    kept = [pick(stacked, side, 1), swap_bit(pick(stacked, 1 - side, 1), 1)]
    sent = swap_bit(jnp.concatenate([pick(part, 1 - core, 1) for part in kept], axis=2), 0)
    kept = [pick(part, core, 1) for part in kept]
    own = jnp.concatenate([kept[0], sent[:, :, :block], kept[1], sent[:, :, block:]], axis=2)
    output_mat = both[:, :, 2 * cols :].reshape(GROUPS * rows, -1)
    output_mat = pair_up((me >> links[-1]) & 1, output_mat, swap_bit(output_mat, links[-1]), 0)
    attn_mat = both[:, :, : 2 * cols].reshape(GROUPS, rows, 2, cols).transpose(2, 0, 1, 3)
    for bit in links:
        attn_mat = pair_up((me >> bit) & 1, attn_mat, swap_bit(attn_mat, bit), 0)
        attn_mat = attn_mat.reshape((-1,) + attn_mat.shape[2:])
    attn_mat = attn_mat.reshape(width, cols)
    hidden_pair = swap_bit(jnp.concatenate(hidden, axis=0), 0)

    far_axes = dp[: bits - SPLIT_BITS] + ("feat",)

    pieces = lax.all_gather(after(own.reshape(3 * units, SPLIT * block), *hidden), far_axes)
    pieces = pieces.reshape(-1, GROUPS, 3 * units, SPLIT * block)
    if not aligned:
        pieces = pieces.transpose(1, 2, 0, 3).reshape(1, GROUPS, 3 * units, width)

    def pair_with(own, far):
        return [own, far, swap_bit(jnp.concatenate([own, far], axis=0), 0)]

    hr, qkv, out, sent, attf, rden = kernel_call(
        front_body,
        [((GROUPS, tokens, width), BF16), ((length, cols), BF16)]
        + [((tokens, 2 * vw), BF16)] * 2
        + [((length, vw), F32)] * 2,
        (first, group_arr, *hidden, hidden_pair, attn_mat),
        scalars=2,
        scratch=(pltpu.VMEM((length, vw), BF16),),
        flops=8 * 2**30,
    )
    sent = swap_bit(sent, 0)
    for axis, bit in enumerate(links[-2::-1], 1):
        output_mat = pair_up((me >> bit) & 1, output_mat, swap_bit(output_mat, bit), axis)
    cot_far = swap_bit(cotangent, 1)
    for axis, bit in ((len(links), 0),):
        output_mat = pair_up((me >> bit) & 1, output_mat, swap_bit(output_mat, bit), axis)
    output_mat = output_mat.reshape(width, -1)
    cots = pair_with(cotangent, cot_far)
    out = [jnp.concatenate([part[:, at : at + vw] for part in (out, sent)], axis=1) for at in (0, vw)]
    out = [home(out[0], 0), home(out[1], 2)]
    middle, mlp_in, attended, gain8 = kernel_call(
        middle_body,
        [
            ((tokens, width), F32),
            ((tokens, width), BF16),
            ((tokens, H * DV), BF16),
            ((8, width), F32),
        ],
        (member_arr, *out, hidden_in, output_mat),
        scalars=1,
        flops=2**30,
    )

    mlps = pair_with(mlp_in, swap_bit(mlp_in, 1))
    swap = lambda v: v
    if not aligned:
        order = jnp.arange(size) ^ (me % SPLIT)
        swap = lambda v: jnp.take(
            v.reshape(v.shape[:-1] + (size, block)), order, axis=v.ndim - 1
        ).reshape(v.shape)
    rows_scratch = pltpu.VMEM((SPLIT * tokens, width), BF16)
    blocks = (SPLIT, tokens, width)
    blocks_scratch = pltpu.VMEM(blocks, BF16)
    parts = pieces.shape[0]
    part = me >> SPLIT_BITS if parts == 2 else jnp.zeros((), jnp.int32)
    spot = jnp.stack([me % SPLIT, part])
    sems = pltpu.SemaphoreType.DMA((160,))
    sources = [swap(v) for v in mlps + cots]

    term_shape = (GROUPS, 3 * units, width // parts)
    outs = kernel_call(
        partial(feed_forward_body, units, size, aligned, parts),
        [((2, tokens, width), BF16, True)] * 4
        + [((GROUPS, high - low, width // parts), BF16, True) for low, high in TERM_ROWS] * parts,
        (spot, *sources, pieces),
        scalars=1,
        remote=7,
        scratch=(
            rows_scratch,
            rows_scratch,
            *[pltpu.VMEM((GROUPS * units, width), BF16)] * 3,
            *[pltpu.VMEM((GROUPS * units, SPLIT * tokens), BF16)] * 3,
            blocks_scratch,
            blocks_scratch,
            pltpu.VMEM((parts,) + term_shape, BF16),
            sems,
        ),
        flops=20 * 2**30,
    )
    grads, grads_sent, branch, branch_sent = [swap(v) for v in outs[:4]]
    terms = outs[4:]
    grads_sent = swap_bit(grads_sent, 0)
    grad_far = swap_bit(add_rounded(grads[1], grads_sent[1]), 1)
    branch_sent = swap_bit(branch_sent, 0)
    branch_sum = add_rounded(branch[1], branch_sent[1])
    branch_far = swap_bit(branch_sum, 1)
    def reduce_terms(terms):
        if parts == 2:
            return add_rounded(terms[1], swap_bit(terms[0], SPLIT_BITS))
        far_bits = list(range(SPLIT_BITS, bits))[::-1]
        term = terms[0].reshape(GROUPS, terms[0].shape[1], -1, SPLIT * block).transpose(2, 0, 1, 3)
        return reduce_bits(term.reshape((2,) * len(far_bits) + term.shape[1:]), far_bits, far_bits)

    terms = [after(term, grad_far) if n >= 2 * (parts - 1) else term for n, term in enumerate(terms)]
    sums = [reduce_terms(terms[h::2]) for h in range(2)]
    totals = [lax.psum_scatter(term, "feat") for term in sums]

    middle_grad, *att_grad, output_term = kernel_call(
        middle_back_body,
        [((tokens, width), F32)]
        + [((tokens, 2 * vw), BF16)] * 2
        + [((width, H * DV + LANES), BF16)],
        (member_arr, grads, grads_sent, after(grad_far, branch_sum), middle, gain8, cotangent, attended, output_mat),
        scalars=1,
        scratch=(pltpu.VMEM((tokens, H * DV), BF16),),
        flops=2**30,
    )
    att_grad = [away(part, mask) for part, mask in zip(att_grad, (0, 2))]
    output_term = output_term.reshape((2,) * bits + (GROUPS, rows, H * DV + LANES))
    output_term = reduce_bits(output_term, [0], range(bits))
    att_sent = jnp.concatenate([part[:, vw:] for part in att_grad], axis=1)
    att_grad.append(swap_bit(after(att_sent, sums[0]), 0))
    output_term = reduce_bits(output_term, links[:1], links)
    att_grad = [after(part, *sums) for part in att_grad]
    input_parts, input_sent, attn_term = kernel_call(
        back_body,
        [((2, tokens, width), BF16)] * 2 + [((width, cols), BF16)],
        (first, group_arr, *att_grad, qkv, attf, rden, hr, attn_mat),
        scalars=2,
        scratch=(
            pltpu.VMEM((qk, length), F32),
            pltpu.VMEM((vw // DV, length, LANES), BF16),
            pltpu.VMEM((vw // DV, length, LANES), BF16),
            pltpu.VMEM((length, vw), BF16),
            pltpu.VMEM((length, cols), BF16),
        ),
        flops=12 * 2**30,
    )
    input_sent = swap_bit(input_sent, 0)
    input_parts = [after(add_rounded(input_parts[k], input_sent[k]), *totals) for k in range(2)]
    input_parts = [home(input_parts[0], 0), home(input_parts[1], 2)]
    scaled_grad = input_parts[0].astype(F32) + input_parts[1].astype(F32)
    residual = hidden_in.astype(F32)
    scale = lax.rsqrt(jnp.mean(residual * residual, axis=1, keepdims=True) + EPSILON)
    normed = residual * scale
    inner = jnp.mean(normed * scaled_grad, axis=1, keepdims=True)
    input_grad = middle_grad + scale * (scaled_grad - normed * inner)

    total = jnp.concatenate(totals, axis=0).astype(F32)
    lanes = [slice(j * block, (j + 1) * block) for j in range(SPLIT)]

    def share_total():
        near = swap_bit(jnp.concatenate([total[:, lanes[1]], total[:, lanes[3]]], axis=1), 0)
        far = jnp.concatenate([total[:, lanes[2]], near[:, block:]], axis=0).astype(BF16)
        return near, swap_bit(far, 1).astype(F32)

    attn_term = after(attn_term, input_sent).reshape((2,) * len(links) + (2, GROUPS, rows, cols))
    attn_term = reduce_bits(attn_term, links[:0:-1], links)
    output_term = reduce_bits(output_term, links[1:], links[1:])
    attn_term = reduce_bits(attn_term, links[:1], links[:1])
    attn_term = attn_term.transpose(1, 2, 0, 3).reshape(GROUPS, rows, 2 * cols)
    both = jnp.concatenate([attn_term, output_term], axis=2)
    both = [pick(both, member ^ m) for m in range(GROUPS)]
    both = [both[0]] + [cross(after(both[m], *totals), m) for m in range(1, GROUPS)]
    output_sum = sum(part[:, 2 * cols :].astype(F32) for part in both)
    output_grad = output_sum[:, : H * DV].T
    mlp_gain_grad = output_sum[:, H * DV]
    same = both[0][:, : 2 * cols].astype(F32) + both[2][:, : 2 * cols].astype(F32)
    flip = both[1][:, : 2 * cols].astype(F32) + both[3][:, : 2 * cols].astype(F32)
    halves = pair_up(member & 1, same, flip, 0).reshape(2, rows, 2, cols)
    near, far = share_total()
    halves = after(halves, far)
    halves = pair_up(core, pick(halves, core, 2), swap_bit(pick(halves, 1 - core, 2), 0), 1)
    attn_grad = halves.reshape(GROUPS, rows, cols).transpose(1, 0, 2)
    scale_rows = gain_attn.astype(F32)[:, None]
    query_raw = attn_grad[:, :, :qk].reshape(rows, H * HF)
    key_raw = attn_grad[:, :, qk : 2 * qk].reshape(rows, H * HF)
    value_raw = attn_grad[:, :, 2 * qk :].reshape(rows, H * DV)
    attn_gain_grad = (
        jnp.sum(query_raw * query_weight.astype(F32), axis=1)
        + jnp.sum(key_raw * key_weight.astype(F32), axis=1)
        + jnp.sum(value_raw * value_weight.astype(F32), axis=1)
    )

    block_out = (
        middle
        + branch[0].astype(F32)
        + branch_sent[0].astype(F32)
        + branch_far.astype(F32)
    ).astype(BF16)

    shares = [total[:, lanes[0]], near[:, :block], far[: 3 * units], far[3 * units :]]
    shares = [jnp.where(core == 0, shares[k], shares[k ^ 1]) for k in range(SPLIT)]
    shares = [jnp.where(side == 0, shares[k], shares[k ^ 2]) for k in range(SPLIT)]
    total = jnp.stack([share.reshape(3, units, block) for share in shares], axis=1)
    total = total.reshape(3, SPLIT * units, block)[:, :hidden_units]
    return (
        block_out,
        input_grad,
        query_raw * scale_rows,
        key_raw * scale_rows,
        value_raw * scale_rows,
        output_grad,
        total[0].T,
        total[1].T,
        total[2],
        attn_gain_grad,
        mlp_gain_grad,
    )


def solution(mesh):
    bits = mesh.shape["dp"].bit_length() - 1
    dp = tuple(f"bit{bit}" for bit in reversed(range(bits)))
    fine = jax.sharding.Mesh(mesh.devices.reshape((2,) * bits + (GROUPS,)), dp + ("feat",))
    both = dp + ("feat",)
    in_specs = (
        P(both, None),
        P(both, None),
        P(both, None),
        P(both, None),
        P(None, both),
        P(dp, "feat"),
        P(dp, "feat"),
        P("feat", dp),
        P(both),
        P(both),
        P(dp),
        P(both, None),
    )
    out_specs = (
        P(both, None),
        P(both, None),
        P(both, None),
        P(both, None),
        P(both, None),
        P(None, both),
        P(dp, "feat"),
        P(dp, "feat"),
        P("feat", dp),
        P(both),
        P(both),
    )
    return jax.shard_map(
        partial(on_device, dp), mesh=fine, in_specs=in_specs, out_specs=out_specs, check_vma=False
    )
```

```python
from functools import partial

import jax
import jax.numpy as jnp
from jax import lax
from jax.experimental import pallas as pl
from jax.experimental.pallas import tpu as pltpu
from jax.sharding import PartitionSpec as P

H = 16
HF = 16
DV = 64
SEQ_LEN = 1024
EPSILON = 1e-05

LANES = 128
TILE = 256
GROUPS = 4
F32 = jnp.float32
BF16 = jnp.bfloat16

SLOT_MASKS = (0, 2, 1, 3)
SPLIT_BITS = 2
SPLIT = 1 << SPLIT_BITS
TERM_ROWS = ((0, 176), (176, 528))


def matmul(first_matrix, second_matrix):
    return jnp.dot(first_matrix, second_matrix, preferred_element_type=F32)


def dot_first(first_matrix, second_matrix):
    return lax.dot_general(
        first_matrix, second_matrix, (((0,), (0,)), ((), ())), preferred_element_type=F32
    )


def dot_last(first_matrix, second_matrix):
    return lax.dot_general(
        first_matrix, second_matrix, (((1,), (1,)), ((), ())), preferred_element_type=F32
    )


def hop(block, bit):
    return lax.ppermute(block, f"bit{bit}", [(0, 1), (1, 0)])


def cross(block, mask):
    return lax.ppermute(block, "feat", [(i, i ^ mask) for i in range(GROUPS)])


def home_pairs(mask):
    pairs = []
    for core in range(2):
        for z in range(GROUPS):
            group = 2 * (z & 1) + core
            pairs.append((core * GROUPS + z, (z >> 1) * GROUPS + (group ^ mask)))
    return pairs


def home(block, mask):
    return lax.ppermute(block, ("bit0", "feat"), home_pairs(mask))


def away(block, mask):
    return lax.ppermute(block, ("bit0", "feat"), [(b, a) for a, b in home_pairs(mask)])


def after(block, *earlier):
    return lax.optimization_barrier((block,) + earlier)[0]


def add_rounded(first, second):
    return (first.astype(F32) + second.astype(F32)).astype(BF16)


def pick(blocks, index, axis=0):
    return lax.dynamic_index_in_dim(blocks, index, axis, keepdims=False)


def place(blocks, sources):
    total = jnp.zeros((len(blocks),) + blocks[0].shape, blocks[0].dtype)
    for block, source in zip(blocks, sources):
        total = lax.dynamic_update_index_in_dim(total, block, source, 0)
    return total


def pair_up(bit, own, other, axis):
    return jnp.where(bit == 0, jnp.stack([own, other], axis), jnp.stack([other, own], axis))


def kernel_call(body, outs, operands, scalars=0, remote=0, scratch=(), flops=0, limit=56):
    smem = pl.BlockSpec(memory_space=pltpu.SMEM)
    vmem = pl.BlockSpec(memory_space=pltpu.VMEM)
    hbm = pl.BlockSpec(memory_space=pl.ANY)
    out_specs = [hbm if len(out) > 2 else vmem for out in outs]
    outs = [jax.ShapeDtypeStruct(out[0], out[1]) for out in outs]
    nbytes = sum(o.size * o.dtype.itemsize for o in list(operands) + outs)
    return pl.pallas_call(
        body,
        out_shape=outs,
        in_specs=[smem] * scalars + [vmem] * (len(operands) - scalars - remote) + [hbm] * remote,
        out_specs=out_specs,
        scratch_shapes=list(scratch),
        compiler_params=pltpu.CompilerParams(vmem_limit_bytes=limit * 1024 * 1024),
        cost_estimate=pl.CostEstimate(flops=flops, bytes_accessed=nbytes, transcendentals=0),
    )(*operands)


def lane_in(width, low, high):
    lane = lax.broadcasted_iota(jnp.int32, (1, width), 1)
    return (lane >= low) & (lane < high)


def block_at(index, size):
    return pl.ds(pl.multiple_of(index * size, size), size)


def masked(own, values):
    return jnp.where(own, values, jnp.zeros_like(values))


def front_body(
    first_ref, group_ref, h0_ref, h1_ref, pair_ref, w_ref,
    hr_ref, qkv_ref, kept_ref, sent_ref, attf_ref, rden_ref, att_ref,
):
    first, group = first_ref[0], group_ref[0]
    tokens = h0_ref.shape[0]
    length, width = att_ref.shape
    heads = width // DV
    qk = heads * HF
    for k, (h_ref, at) in enumerate(((h0_ref, 0), (h1_ref, 0), (pair_ref, 0), (pair_ref, tokens))):
        rows = h_ref[at : at + tokens, :].astype(F32)
        scale = lax.rsqrt(jnp.mean(rows * rows, axis=1, keepdims=True) + EPSILON)
        normed = (rows * scale).astype(BF16)
        hr_ref[k] = normed
        qkv_ref[block_at(group ^ SLOT_MASKS[k], tokens), :] = matmul(normed, w_ref[...]).astype(BF16)
    lower = lane_in(LANES, 0, DV)
    keys = qkv_ref[:, qk : 2 * qk]
    head_keys = [masked(lane_in(qk, h * HF, (h + 1) * HF), keys) for h in range(heads)]
    head_values = []
    for h in range(heads):
        low = 2 * qk + (h // 2) * LANES
        tile = qkv_ref[:, low : low + LANES]
        own = lower if h % 2 == 0 else jnp.logical_not(lower)
        head_values.append(jnp.where(own, tile, jnp.ones_like(tile)))
    for i in range(length // TILE):
        extent = (i + 1) * TILE
        rows = slice(i * TILE, extent)
        t_pos = i * TILE + lax.broadcasted_iota(jnp.int32, (TILE, 1), 0)
        s_pos = lax.broadcasted_iota(jnp.int32, (1, extent), 1)
        start = jnp.where(t_pos >= first, first, 0)
        allowed = (s_pos <= t_pos) & (s_pos >= start)
        queries = (qkv_ref[rows, :qk].astype(F32) * 0.25).astype(BF16)
        for pair in range(heads // 2):
            outs = []
            for h in (2 * pair, 2 * pair + 1):
                inner = dot_last(queries, head_keys[h][:extent])
                scores = jnp.where(allowed, 1.0 + inner * (1.0 + 0.5 * inner), 0.0)
                outs.append(matmul(scores.astype(BF16), head_values[h][:extent]))
            numer = jnp.where(lower, outs[0], outs[1])
            denom = pltpu.roll(jnp.where(lower, outs[1], outs[0]), DV, 1)
            recip = 1.0 / denom
            attended = numer * recip
            lanes = slice(pair * LANES, (pair + 1) * LANES)
            att_ref[rows, lanes] = attended.astype(BF16)
            attf_ref[rows, lanes] = attended
            rden_ref[rows, lanes] = recip
    for k, mask in enumerate(SLOT_MASKS):
        out_ref = (kept_ref, sent_ref)[k // 2]
        at = (k % 2) * width
        out_ref[:, at : at + width] = att_ref[block_at(group ^ mask, tokens), :]


def back_body(
    first_ref, group_ref, g0_ref, g1_ref, near_ref, qkv_ref, attf_ref, rden_ref, hr_in, w_in,
    kept_ref, sent_ref, term_ref, qt_ref, aug_ref, nb_ref, ag_ref, bars_ref, hr_ref, w_ref, sems,
):
    loads = start_copies([(hr_in, hr_ref), (w_in, w_ref)], sems, 0)
    first, group = first_ref[0], group_ref[0]
    tokens = g0_ref.shape[0]
    length, width = ag_ref.shape
    heads = width // DV
    qk = heads * HF
    for k, (g_ref, at) in enumerate(((g0_ref, 0), (g1_ref, 0), (near_ref, 0), (near_ref, width))):
        ag_ref[block_at(group ^ SLOT_MASKS[k], tokens), :] = g_ref[:, at : at + width]
    lower = lane_in(LANES, 0, DV)
    queries = (qkv_ref[:, :qk].astype(F32) * 0.25).astype(BF16)
    raw_keys = qkv_ref[:, qk : 2 * qk]
    keys = (raw_keys.astype(F32) * 0.25).astype(BF16)
    head_queries, head_keys, head_values = [], [], []
    for h in range(heads):
        own = lane_in(qk, h * HF, (h + 1) * HF)
        head_queries.append(masked(own, queries))
        head_keys.append(masked(own, keys))
    for h in range(heads):
        lanes = slice((h // 2) * LANES, (h // 2 + 1) * LANES)
        own = lower if h % 2 == 0 else jnp.logical_not(lower)
        numer_bar = ag_ref[:, lanes].astype(F32) * rden_ref[:, lanes]
        products = jnp.where(own, numer_bar * attf_ref[:, lanes], 0.0)
        denom_bar = -jnp.sum(products, axis=1, keepdims=True)
        column = DV if h % 2 == 0 else 0
        numer_bar = jnp.where(own, numer_bar, 0.0)
        nb_ref[h] = numer_bar.astype(BF16)
        aug_ref[h] = jnp.where(
            lane_in(LANES, column, column + 1), denom_bar, numer_bar
        ).astype(BF16)
        low = 2 * qk + (h // 2) * LANES
        tile = qkv_ref[:, low : low + LANES]
        head_values.append(jnp.where(own, tile, jnp.ones_like(tile)))
    qt_ref[...] = jnp.zeros_like(qt_ref)
    for i in range(length // TILE):
        low = i * TILE
        extent = length - low
        rows = slice(low, low + TILE)
        s_pos = low + lax.broadcasted_iota(jnp.int32, (TILE, 1), 0)
        t_pos = low + lax.broadcasted_iota(jnp.int32, (1, extent), 1)
        start = jnp.where(t_pos >= first, first, 0)
        allowed = (s_pos <= t_pos) & (s_pos >= start)
        key_total = jnp.zeros((TILE, qk), F32)
        query_total = jnp.zeros((qk, extent), F32)
        for pair in range(heads // 2):
            value_total = jnp.zeros((TILE, LANES), F32)
            for h in (2 * pair, 2 * pair + 1):
                inner = dot_last(raw_keys[rows], head_queries[h][low:])
                scores = jnp.where(allowed, 1.0 + inner * (1.0 + 0.5 * inner), 0.0)
                value_total += matmul(scores.astype(BF16), nb_ref[h, low:, :])
                bar = dot_last(head_values[h][rows], aug_ref[h, low:, :])
                slope = jnp.where(allowed, bar * (1.0 + inner), 0.0).astype(BF16)
                key_total += matmul(slope, head_queries[h][low:])
                query_total += dot_first(head_keys[h][rows], slope)
            lanes = slice(2 * qk + pair * LANES, 2 * qk + (pair + 1) * LANES)
            bars_ref[rows, lanes] = value_total.astype(BF16)
        bars_ref[rows, qk : 2 * qk] = key_total.astype(BF16)
        qt_ref[:, low:] += query_total
    bars_ref[:, :qk] = qt_ref[...].T.astype(BF16)
    for copy in loads:
        copy.wait()
    term = jnp.zeros((bars_ref.shape[1], hr_ref.shape[2]), F32)
    for k, mask in enumerate(SLOT_MASKS):
        bars = bars_ref[block_at(group ^ mask, tokens), :]
        (kept_ref, sent_ref)[k // 2][k % 2] = dot_last(bars, w_ref[...]).astype(BF16)
        term += dot_first(bars, hr_ref[k])
    term_ref[...] = term.T.astype(BF16)


def middle_body(
    member_ref, a0_ref, a1_ref, hidden_ref, w_ref,
    middle_ref, mlp_ref, att_ref, gain_ref,
):
    member = member_ref[0]
    part = a0_ref.shape[1] // 2
    for m, mask in enumerate((0, 1, 2, 3)):
        at = (m % 2) * part
        att_ref[:, block_at(member ^ mask, part)] = (a0_ref, a1_ref)[m // 2][:, at : at + part]
    width = att_ref.shape[1]
    pick_gain = jnp.where(lane_in(LANES, 0, 1), jnp.ones((8, LANES), BF16), 0)
    gain = dot_last(pick_gain, w_ref[:, width:])
    gain_ref[...] = gain
    middle = hidden_ref[...].astype(F32) + dot_last(att_ref[...], w_ref[:, :width])
    middle_ref[...] = middle
    scale = lax.rsqrt(jnp.mean(middle * middle, axis=1, keepdims=True) + EPSILON)
    mlp_ref[...] = (middle * scale * gain[:1]).astype(BF16)


def middle_back_body(
    member_ref, own_ref, near_ref, far_ref, middle_ref, gain_ref, cot_ref, attended_ref, w_ref,
    grad_ref, g0_ref, g1_ref, out_ref, att_ref,
):
    member = member_ref[0]
    width = att_ref.shape[1]
    part = g0_ref.shape[1] // 2
    gain = gain_ref[:1]
    mlp_grad = own_ref[0].astype(F32) + near_ref[0].astype(F32) + far_ref[...].astype(F32)
    middle = middle_ref[...]
    scale = lax.rsqrt(jnp.mean(middle * middle, axis=1, keepdims=True) + EPSILON)
    normed = middle * scale
    scaled = mlp_grad * gain
    inner = jnp.mean(normed * scaled, axis=1, keepdims=True)
    grad = cot_ref[...].astype(F32) + scale * (scaled - normed * inner)
    grad_ref[...] = grad
    bar = grad.astype(BF16)
    att_ref[...] = matmul(bar, w_ref[:, :width]).astype(BF16)
    for m, mask in enumerate((0, 1, 2, 3)):
        at = (m % 2) * part
        (g0_ref, g1_ref)[m // 2][:, at : at + part] = att_ref[:, block_at(member ^ mask, part)]
    out_ref[:, :width] = dot_first(bar, attended_ref[...]).astype(BF16)
    term = jnp.sum(mlp_grad * normed, axis=0, keepdims=True)
    out_ref[:, width:] = jnp.broadcast_to(term, (LANES, term.shape[1])).T.astype(BF16)


def start_copies(pairs, sems, first):
    copies = [
        pltpu.make_async_copy(source, target, sems.at[first + n])
        for n, (source, target) in enumerate(pairs)
    ]
    for copy in copies:
        copy.start()
    return copies


def forward_units(x_blocks, c_blocks, weights_ref, hidden_refs, put):
    wg_ref, wu_ref, wd_ref = (weights_ref.at[m] for m in range(3))
    total = weights_ref.shape[1]
    edges = list(range(0, total, TILE)) + [total]
    spans = list(zip(edges[:-1], edges[1:]))
    tokens = TILE

    for b, (x_ref, c_ref) in enumerate(zip(x_blocks, c_blocks)):
        rows = slice(b * tokens, (b + 1) * tokens)
        x_rows = x_ref[...]
        c_rows = c_ref[...]
        kept = []
        for low, high in spans:
            gate = dot_last(x_rows, wg_ref[low:high, :])
            up = dot_last(x_rows, wu_ref[low:high, :])
            back = dot_last(c_rows, wd_ref[low:high, :])
            sig = 1.0 / (1.0 + jnp.exp(-gate))
            silu = gate * sig
            act = (silu * up).astype(BF16)
            gate_bar = (back * up * (sig + silu * (1.0 - sig))).astype(BF16)
            up_bar = (back * silu).astype(BF16)
            for value, ref in zip((act, gate_bar, up_bar), hidden_refs):
                ref[low:high, rows] = value.T
            kept.append((act, gate_bar, up_bar))
        branch = sum(matmul(kept[n][0], wd_ref[low:high, :]) for n, (low, high) in enumerate(spans))
        grad = sum(matmul(kept[n][1], wg_ref[low:high, :]) for n, (low, high) in enumerate(spans))
        grad += sum(matmul(kept[n][2], wu_ref[low:high, :]) for n, (low, high) in enumerate(spans))
        put(b, branch, grad)


def weight_units(units, index, x_blocks, c_blocks, hidden_refs, term_ref):
    slots, _, part = term_ref.shape
    step = min(part, 256)
    act_ref, gate_ref, up_ref = hidden_refs
    for m, (left, right) in enumerate(
        ((gate_ref, x_blocks), (up_ref, x_blocks), (act_ref, c_blocks))
    ):
        for at in range(0, part, step):
            lanes = pl.ds(pl.multiple_of(index * part + at, step), step)
            rows = jnp.concatenate([ref[:, lanes] for ref in right], axis=0)
            out = matmul(left[...], rows).astype(BF16)
            for s in range(slots):
                term_ref[s, m * units : (m + 1) * units, at : at + step] = out[
                    s * units : (s + 1) * units
                ]


def feed_forward_body(units, parts, *refs):
    index_ref, sources, piece_ref, refs = refs[0], refs[1:7], refs[7], refs[8:]
    grad_refs, branch_refs, term_refs, refs = refs[:2], refs[2:4], refs[4 : 4 + 2 * parts], refs[4 + 2 * parts :]
    rows_ref, weights_ref, hidden_refs, branch_buf, grad_buf, term_buf, sems = *refs[:2], refs[2:5], *refs[5:]
    tokens = sources[0].shape[0]
    pairs = [
        (source, rows_ref.at[n // 3, pl.ds(tokens * (n % 3), source.shape[0]), :])
        for n, source in enumerate(sources)
    ]
    count, slots, _, part = piece_ref.shape
    pairs += [
        (
            piece_ref.at[y, s, pl.ds(m * units, units), :],
            weights_ref.at[m, pl.ds(s * units, units), pl.ds(y * part, part)],
        )
        for m in range(3)
        for y in range(count)
        for s in range(slots)
    ]
    for copy in start_copies(pairs, sems, 0):
        copy.wait()
    x_blocks, c_blocks = (
        [rows_ref.at[n, pl.ds(tokens * b, tokens), :] for b in range(SPLIT)] for n in range(2)
    )
    stores = []

    def put(b, branch, grad):
        branch_buf[b] = branch.astype(BF16)
        grad_buf[b] = grad.astype(BF16)
        done = [
            (grad_buf.at[b], grad_refs[b // 2].at[b % 2]),
            (branch_buf.at[b], branch_refs[b // 2].at[b % 2]),
        ]
        stores.extend(start_copies(done, sems, len(pairs) + len(stores)))

    forward_units(x_blocks, c_blocks, weights_ref, hidden_refs, put)
    for n in range(parts):
        which = index_ref[0] if n == parts - 1 else 1 - index_ref[0]
        weight_units(units, which, x_blocks, c_blocks, hidden_refs, term_buf.at[n])
        for h, rows in enumerate(TERM_ROWS):
            done = [(term_buf.at[n, :, pl.ds(rows[0], rows[1] - rows[0]), :], term_refs[2 * n + h])]
            stores.extend(start_copies(done, sems, len(pairs) + len(stores)))
    for copy in stores:
        copy.wait()


def on_device(
    dp,
    hidden_in,
    query_weight,
    key_weight,
    value_weight,
    output_weight,
    gate_weight,
    up_weight,
    down_weight,
    gain_attn,
    gain_mlp,
    first_length,
    cotangent,
):
    member = lax.axis_index("feat")
    me = lax.axis_index(dp)
    bits = len(dp)
    size = 1 << bits
    links = list(range(1, bits))
    core = me & 1
    group = 2 * (member & 1) + core
    tokens, width = hidden_in.shape
    length = GROUPS * tokens
    member_arr, group_arr = member.reshape(1), group.reshape(1)

    latest = {}

    def send(link, how, *blocks):
        blocks = [after(block, *latest.get(link, ())) for block in blocks]
        latest[link] = tuple(how(block) for block in blocks)
        return latest[link] if len(blocks) > 1 else latest[link][0]

    def link_of(bit):
        return ("core", "x", "y")[min(bit, 2)]

    def swap_bit(block, bit):
        return send(link_of(bit), partial(hop, bit=bit), block)

    def reduce_bits(term, order, left):
        left = sorted(left, reverse=True)
        for bit in order:
            axis = left.index(bit)
            mine = (me >> bit) & 1
            other = swap_bit(pick(term, 1 - mine, axis), bit)
            term = add_rounded(pick(term, mine, axis), other)
            left.remove(bit)
        return term

    side = (me >> 1) & 1

    def in_place(shares):
        shares = [jnp.where(core == 0, shares[k], shares[k ^ 1]) for k in range(SPLIT)]
        return [jnp.where(side == 0, shares[k], shares[k ^ 2]) for k in range(SPLIT)]

    rows = query_weight.shape[0]
    qk = H * HF // GROUPS
    vw = H * DV // GROUPS
    attn_pack = jnp.concatenate(
        [
            query_weight.reshape(rows, GROUPS, qk),
            key_weight.reshape(rows, GROUPS, qk),
            value_weight.reshape(rows, GROUPS, vw),
        ],
        axis=2,
    )
    attn_pack = (attn_pack.astype(F32) * gain_attn.astype(F32)[:, None, None]).astype(BF16)
    cols = attn_pack.shape[2]
    attn_pack = attn_pack.transpose(1, 0, 2).reshape(2, 2, rows, cols)
    sent = pick(attn_pack, 1 - core, 1).reshape(2 * rows, cols)
    lengths = jnp.broadcast_to(first_length.astype(BF16)[:, None], (16, cols))
    sent = swap_bit(jnp.concatenate([lengths, sent], axis=0), 0)
    first = jnp.where((member >> 1) == core, first_length, sent[0, :1].astype(jnp.int32))
    sent = sent[16:].reshape(2, rows, cols)
    attn_pack = pair_up(core, pick(attn_pack, core, 1), sent, 2)

    output_pack = jnp.concatenate(
        [output_weight.T, jnp.pad(gain_mlp[:, None], ((0, 0), (0, LANES - 1)))], axis=1
    )
    same = pick(attn_pack, member & 1).reshape(rows, 2 * cols)
    flip = pick(attn_pack, 1 - (member & 1)).reshape(rows, 2 * cols)
    far = cross(jnp.concatenate([same, flip, output_pack], axis=1), 2)
    flips = [
        jnp.concatenate([flip, output_pack], axis=1),
        far[:, 2 * cols :],
    ]
    hidden = [away(hidden_in, mask) for mask in (0, 2)]
    near = cross(after(jnp.concatenate(flips, axis=0), *hidden), 1)
    both = [
        jnp.concatenate([same, output_pack], axis=1),
        near[:rows],
        jnp.concatenate([far[:, : 2 * cols], far[:, 4 * cols :]], axis=1),
        near[rows:],
    ]
    both = after(place(both, [member ^ m for m in range(GROUPS)]), *hidden)
    hidden_units = down_weight.shape[0]
    units = -(-hidden_units // (16 * SPLIT)) * 16
    stacked = jnp.stack([gate_weight.T, up_weight.T, down_weight])
    stacked = jnp.pad(stacked, ((0, 0), (0, SPLIT * units - hidden_units), (0, 0)))
    block = stacked.shape[2]
    aligned = block % LANES == 0
    stacked = stacked.reshape(3, 2, 2, units, block)
    kept = [pick(stacked, side, 1), swap_bit(pick(stacked, 1 - side, 1), 1)]
    sent = swap_bit(jnp.concatenate([pick(part, 1 - core, 1) for part in kept], axis=2), 0)
    kept = [pick(part, core, 1) for part in kept]
    own = in_place([kept[0], sent[:, :, :block], kept[1], sent[:, :, block:]])
    own = jnp.concatenate(own, axis=2)
    output_mat = both[:, :, 2 * cols :].reshape(GROUPS * rows, -1)
    output_mat = pair_up((me >> links[-1]) & 1, output_mat, swap_bit(output_mat, links[-1]), 0)
    attn_mat = both[:, :, : 2 * cols].reshape(GROUPS, rows, 2, cols).transpose(2, 0, 1, 3)
    for bit in links:
        attn_mat = pair_up((me >> bit) & 1, attn_mat, swap_bit(attn_mat, bit), 0)
        attn_mat = attn_mat.reshape((-1,) + attn_mat.shape[2:])
    attn_mat = attn_mat.reshape(width, cols)
    hidden_pair = swap_bit(jnp.concatenate(hidden, axis=0), 0)

    far_axes = dp[: bits - SPLIT_BITS] + ("feat",)

    weights = lax.all_gather(after(own.reshape(3 * units, SPLIT * block), *hidden), far_axes)
    weights = weights.reshape(-1, GROUPS, 3 * units, SPLIT * block)
    if not aligned:
        weights = weights.transpose(1, 2, 0, 3).reshape(1, GROUPS, 3 * units, width)

    def pair_with(own, far):
        return [own, far, swap_bit(jnp.concatenate([own, far], axis=0), 0)]

    hr, qkv, out, sent, attf, rden = kernel_call(
        front_body,
        [((GROUPS, tokens, width), BF16), ((length, cols), BF16)]
        + [((tokens, 2 * vw), BF16)] * 2
        + [((length, vw), F32)] * 2,
        (first, group_arr, *hidden, hidden_pair, attn_mat),
        scalars=2,
        scratch=(pltpu.VMEM((length, vw), BF16),),
        flops=8 * 2**30,
        limit=24,
    )
    sent = swap_bit(sent, 0)
    for axis, bit in enumerate(links[-2::-1], 1):
        output_mat = pair_up((me >> bit) & 1, output_mat, swap_bit(output_mat, bit), axis)
    cot_far = swap_bit(cotangent, 1)
    for axis, bit in ((len(links), 0),):
        output_mat = pair_up((me >> bit) & 1, output_mat, swap_bit(output_mat, bit), axis)
    output_mat = output_mat.reshape(width, -1)
    cots = pair_with(cotangent, cot_far)
    out = [jnp.concatenate([part[:, at : at + vw] for part in (out, sent)], axis=1) for at in (0, vw)]
    out = [home(out[0], 0), home(out[1], 2)]
    middle, mlp_in, attended, gain8 = kernel_call(
        middle_body,
        [
            ((tokens, width), F32),
            ((tokens, width), BF16),
            ((tokens, H * DV), BF16),
            ((8, width), F32),
        ],
        (member_arr, *out, hidden_in, output_mat),
        scalars=1,
        flops=2**30,
        limit=12,
    )

    mlps = pair_with(mlp_in, swap_bit(mlp_in, 1))
    blocks = (SPLIT, tokens, width)
    parts = 2 if aligned and bits == SPLIT_BITS + 1 else 1
    part = me >> SPLIT_BITS if parts == 2 else jnp.zeros((), jnp.int32)
    term_shape = (GROUPS, 3 * units, width // parts)
    outs = kernel_call(
        partial(feed_forward_body, units, parts),
        [((2, tokens, width), BF16, True)] * 4
        + [((GROUPS, high - low, width // parts), BF16, True) for low, high in TERM_ROWS] * parts,
        (part.reshape(1), *mlps, *cots, weights),
        scalars=1,
        remote=7,
        scratch=(
            pltpu.VMEM((2, SPLIT * tokens, width), BF16),
            pltpu.VMEM((3, GROUPS * units, width), BF16),
            *[pltpu.VMEM((GROUPS * units, SPLIT * tokens), BF16)] * 3,
            pltpu.VMEM(blocks, BF16),
            pltpu.VMEM(blocks, BF16),
            pltpu.VMEM((parts,) + term_shape, BF16),
            pltpu.SemaphoreType.DMA((6 + 3 * weights.shape[0] * GROUPS + 2 * SPLIT + 2 * parts,)),
        ),
        flops=20 * 2**30,
        limit=56,
    )
    grads, grads_sent, branch, branch_sent = outs[:4]
    terms = outs[4:]
    grads_sent = swap_bit(grads_sent, 0)
    grad_far = swap_bit(add_rounded(grads[1], grads_sent[1]), 1)
    branch_sent = swap_bit(branch_sent, 0)
    def reduce_terms(terms):
        if parts == 2:
            return add_rounded(terms[1], swap_bit(terms[0], SPLIT_BITS))
        far_bits = list(range(SPLIT_BITS, bits))[::-1]
        term = terms[0].reshape(GROUPS, terms[0].shape[1], -1, SPLIT * block).transpose(2, 0, 1, 3)
        return reduce_bits(term.reshape((2,) * len(far_bits) + term.shape[1:]), far_bits, far_bits)

    terms = [after(term, grad_far) if n >= 2 * (parts - 1) else term for n, term in enumerate(terms)]
    sums = [reduce_terms(terms[h::2]) for h in range(2)]
    totals = [lax.psum_scatter(term, "feat") for term in sums]

    middle_grad, *att_grad, output_term = kernel_call(
        middle_back_body,
        [((tokens, width), F32)]
        + [((tokens, 2 * vw), BF16)] * 2
        + [((width, H * DV + LANES), BF16)],
        (member_arr, grads, grads_sent, after(grad_far, sums[0]), middle, gain8, cotangent, attended, output_mat),
        scalars=1,
        scratch=(pltpu.VMEM((tokens, H * DV), BF16),),
        flops=2**30,
        limit=56,
    )
    att_grad = [away(part, mask) for part, mask in zip(att_grad, (0, 2))]
    output_term = after(output_term, *att_grad).reshape((2,) * bits + (GROUPS, rows, H * DV + LANES))
    output_term = reduce_bits(output_term, [0], range(bits))
    att_sent = jnp.concatenate([part[:, vw:] for part in att_grad], axis=1)
    att_grad.append(swap_bit(after(att_sent, sums[0]), 0))
    output_term = reduce_bits(output_term, links[:1], links)
    branch_far = swap_bit(add_rounded(branch[1], branch_sent[1]), 1)
    att_grad = [after(part, sums[0]) for part in att_grad]
    input_parts, input_sent, attn_term = kernel_call(
        back_body,
        [((2, tokens, width), BF16)] * 2 + [((width, cols), BF16)],
        (first, group_arr, *att_grad, qkv, attf, rden, hr, attn_mat),
        scalars=2,
        scratch=(
            pltpu.VMEM((qk, length), F32),
            pltpu.VMEM((vw // DV, length, LANES), BF16),
            pltpu.VMEM((vw // DV, length, LANES), BF16),
            pltpu.VMEM((length, vw), BF16),
            pltpu.VMEM((length, cols), BF16),
            pltpu.VMEM(hr.shape, BF16),
            pltpu.VMEM(attn_mat.shape, BF16),
            pltpu.SemaphoreType.DMA((2,)),
        ),
        flops=12 * 2**30,
        remote=2,
        limit=56,
    )
    input_sent = swap_bit(input_sent, 0)
    input_parts = [after(add_rounded(input_parts[k], input_sent[k]), sums[1]) for k in range(2)]
    input_parts = [home(input_parts[0], 0), home(input_parts[1], 2)]
    total = jnp.concatenate(totals, axis=0).astype(F32)
    lanes = [total[:, j * block : (j + 1) * block] for j in range(SPLIT)]

    def share_total():
        own = [jnp.where(core == 0, lanes[x], lanes[x + 1]) for x in (0, 2)]
        sent = [jnp.where(core == 0, lanes[x + 1], lanes[x]) for x in (0, 2)]
        near = swap_bit(jnp.concatenate(sent, axis=1), 0)
        near = [near[:, :block], near[:, block:]]
        mine = [jnp.where(side == 0, both[0], both[1]) for both in (own, near)]
        sent = [jnp.where(side == 0, both[1], both[0]) for both in (own, near)]
        far = swap_bit(jnp.concatenate(sent, axis=0).astype(BF16), 1).astype(F32)
        return in_place([*mine, far[: 3 * units], far[3 * units :]]), far

    attn_term = after(attn_term, input_sent).reshape((2,) * len(links) + (2, GROUPS, rows, cols))
    attn_term = reduce_bits(attn_term, links[:0:-1], links)
    output_term = reduce_bits(output_term, links[1:], links[1:])
    attn_term = reduce_bits(attn_term, links[:1], links[:1])
    shares, shares_last = share_total()
    other = swap_bit(pick(attn_term, 1 - core), 0)
    attn_term = pair_up(core, pick(attn_term, core), other, 2).reshape(GROUPS, rows, 2 * cols)
    both = jnp.concatenate([attn_term, output_term], axis=2)
    kept, sent = ([pick(both, member ^ m) for m in pair] for pair in ((0, 2), (1, 3)))
    sent = after(jnp.stack(sent), *totals)
    input_parts = [after(part, sent) for part in input_parts]
    scaled_grad = input_parts[0].astype(F32) + input_parts[1].astype(F32)
    residual = hidden_in.astype(F32)
    scale = lax.rsqrt(jnp.mean(residual * residual, axis=1, keepdims=True) + EPSILON)
    normed = residual * scale
    inner = jnp.mean(normed * scaled_grad, axis=1, keepdims=True)
    input_grad = middle_grad + scale * (scaled_grad - normed * inner)

    sent = cross(sent, 1)
    out = [add_rounded(kept[k][:, 2 * cols :], sent[k][:, 2 * cols :]) for k in range(2)]
    same, flip = ([part[k][:, : 2 * cols] for k in range(2)] for part in (kept, sent))
    last = after(jnp.concatenate([same[1], flip[1], out[1]], axis=1), shares_last)
    last = cross(last, 2).astype(F32)
    output_sum = out[0].astype(F32) + last[:, 4 * cols :]
    output_grad = output_sum[:, : H * DV].T
    mlp_gain_grad = output_sum[:, H * DV]
    same = same[0].astype(F32) + last[:, : 2 * cols]
    flip = flip[0].astype(F32) + last[:, 2 * cols : 4 * cols]
    attn_grad = pair_up(member & 1, same, flip, 0).reshape(2, rows, 2, cols)
    attn_grad = attn_grad.transpose(1, 0, 2, 3).reshape(rows, GROUPS, cols)
    scale_rows = gain_attn.astype(F32)[:, None]
    query_raw = attn_grad[:, :, :qk].reshape(rows, H * HF)
    key_raw = attn_grad[:, :, qk : 2 * qk].reshape(rows, H * HF)
    value_raw = attn_grad[:, :, 2 * qk :].reshape(rows, H * DV)
    attn_gain_grad = (
        jnp.sum(query_raw * query_weight.astype(F32), axis=1)
        + jnp.sum(key_raw * key_weight.astype(F32), axis=1)
        + jnp.sum(value_raw * value_weight.astype(F32), axis=1)
    )

    block_out = (
        middle
        + branch[0].astype(F32)
        + branch_sent[0].astype(F32)
        + branch_far.astype(F32)
    ).astype(BF16)

    total = jnp.stack([share.reshape(3, units, block) for share in shares], axis=1)
    total = total.reshape(3, SPLIT * units, block)[:, :hidden_units]
    return (
        block_out,
        input_grad,
        query_raw * scale_rows,
        key_raw * scale_rows,
        value_raw * scale_rows,
        output_grad,
        total[0].T,
        total[1].T,
        total[2],
        attn_gain_grad,
        mlp_gain_grad,
    )


def solution(mesh):
    bits = mesh.shape["dp"].bit_length() - 1
    dp = tuple(f"bit{bit}" for bit in reversed(range(bits)))
    fine = jax.sharding.Mesh(mesh.devices.reshape((2,) * bits + (GROUPS,)), dp + ("feat",))
    both = dp + ("feat",)
    in_specs = (
        P(both, None),
        P(both, None),
        P(both, None),
        P(both, None),
        P(None, both),
        P(dp, "feat"),
        P(dp, "feat"),
        P("feat", dp),
        P(both),
        P(both),
        P(dp),
        P(both, None),
    )
    out_specs = (
        P(both, None),
        P(both, None),
        P(both, None),
        P(both, None),
        P(both, None),
        P(None, both),
        P(dp, "feat"),
        P(dp, "feat"),
        P("feat", dp),
        P(both),
        P(both),
    )
    return jax.shard_map(
        partial(on_device, dp), mesh=fine, in_specs=in_specs, out_specs=out_specs, check_vma=False
    )
```

```python
from functools import partial

import jax
import jax.numpy as jnp
from jax import lax
from jax.experimental import pallas as pl
from jax.experimental.pallas import tpu as pltpu
from jax.sharding import PartitionSpec as P

H = 16
HF = 16
DV = 64
SEQ_LEN = 1024
EPSILON = 1e-05

LANES = 128
TILE = 256
GROUPS = 4
F32 = jnp.float32
BF16 = jnp.bfloat16

SLOT_MASKS = (0, 2, 1, 3)
SPLIT_BITS = 2
SPLIT = 1 << SPLIT_BITS


def matmul(first_matrix, second_matrix):
    return jnp.dot(first_matrix, second_matrix, preferred_element_type=F32)


def dot_first(first_matrix, second_matrix):
    return lax.dot_general(
        first_matrix, second_matrix, (((0,), (0,)), ((), ())), preferred_element_type=F32
    )


def dot_last(first_matrix, second_matrix):
    return lax.dot_general(
        first_matrix, second_matrix, (((1,), (1,)), ((), ())), preferred_element_type=F32
    )


def hop(block, bit):
    return lax.ppermute(block, f"bit{bit}", [(0, 1), (1, 0)])


def cross(block, mask):
    return lax.ppermute(block, "feat", [(i, i ^ mask) for i in range(GROUPS)])


def home_pairs(mask):
    pairs = []
    for core in range(2):
        for z in range(GROUPS):
            group = 2 * (z & 1) + core
            pairs.append((core * GROUPS + z, (z >> 1) * GROUPS + (group ^ mask)))
    return pairs


def home(block, mask):
    return lax.ppermute(block, ("bit0", "feat"), home_pairs(mask))


def away(block, mask):
    return lax.ppermute(block, ("bit0", "feat"), [(b, a) for a, b in home_pairs(mask)])


def after(block, *earlier):
    return lax.optimization_barrier((block,) + earlier)[0]


def add_rounded(first, second):
    return (first.astype(F32) + second.astype(F32)).astype(BF16)


def pick(blocks, index, axis=0):
    return lax.dynamic_index_in_dim(blocks, index, axis, keepdims=False)


def place(blocks, sources):
    total = jnp.zeros((len(blocks),) + blocks[0].shape, blocks[0].dtype)
    for block, source in zip(blocks, sources):
        total = lax.dynamic_update_index_in_dim(total, block, source, 0)
    return total


def pair_up(bit, own, other, axis):
    return jnp.where(bit == 0, jnp.stack([own, other], axis), jnp.stack([other, own], axis))


def kernel_call(body, outs, operands, scalars=0, remote=0, scratch=(), flops=0, limit=56):
    smem = pl.BlockSpec(memory_space=pltpu.SMEM)
    vmem = pl.BlockSpec(memory_space=pltpu.VMEM)
    hbm = pl.BlockSpec(memory_space=pl.ANY)
    out_specs = [hbm if len(out) > 2 else vmem for out in outs]
    outs = [jax.ShapeDtypeStruct(out[0], out[1]) for out in outs]
    nbytes = sum(o.size * o.dtype.itemsize for o in list(operands) + outs)
    return pl.pallas_call(
        body,
        out_shape=outs,
        in_specs=[smem] * scalars + [vmem] * (len(operands) - scalars - remote) + [hbm] * remote,
        out_specs=out_specs,
        scratch_shapes=list(scratch),
        compiler_params=pltpu.CompilerParams(vmem_limit_bytes=limit * 1024 * 1024),
        cost_estimate=pl.CostEstimate(flops=flops, bytes_accessed=nbytes, transcendentals=0),
    )(*operands)


def lane_in(width, low, high):
    lane = lax.broadcasted_iota(jnp.int32, (1, width), 1)
    return (lane >= low) & (lane < high)


def block_at(index, size):
    return pl.ds(pl.multiple_of(index * size, size), size)


def masked(own, values):
    return jnp.where(own, values, jnp.zeros_like(values))


def front_body(
    first_ref, group_ref, h0_ref, h1_ref, pair_ref, w_ref,
    hr_ref, qkv_ref, kept_ref, sent_ref, attf_ref, rden_ref, att_ref,
):
    first, group = first_ref[0], group_ref[0]
    tokens = h0_ref.shape[0]
    length, width = att_ref.shape
    heads = width // DV
    qk = heads * HF
    for k, (h_ref, at) in enumerate(((h0_ref, 0), (h1_ref, 0), (pair_ref, 0), (pair_ref, tokens))):
        rows = h_ref[at : at + tokens, :].astype(F32)
        scale = lax.rsqrt(jnp.mean(rows * rows, axis=1, keepdims=True) + EPSILON)
        normed = (rows * scale).astype(BF16)
        hr_ref[k] = normed
        qkv_ref[block_at(group ^ SLOT_MASKS[k], tokens), :] = matmul(normed, w_ref[...]).astype(BF16)
    lower = lane_in(LANES, 0, DV)
    keys = qkv_ref[:, qk : 2 * qk]
    head_keys = [masked(lane_in(qk, h * HF, (h + 1) * HF), keys) for h in range(heads)]
    head_values = []
    for h in range(heads):
        low = 2 * qk + (h // 2) * LANES
        tile = qkv_ref[:, low : low + LANES]
        own = lower if h % 2 == 0 else jnp.logical_not(lower)
        head_values.append(jnp.where(own, tile, jnp.ones_like(tile)))
    for i in range(length // TILE):
        extent = (i + 1) * TILE
        rows = slice(i * TILE, extent)
        t_pos = i * TILE + lax.broadcasted_iota(jnp.int32, (TILE, 1), 0)
        s_pos = lax.broadcasted_iota(jnp.int32, (1, extent), 1)
        start = jnp.where(t_pos >= first, first, 0)
        allowed = (s_pos <= t_pos) & (s_pos >= start)
        queries = (qkv_ref[rows, :qk].astype(F32) * 0.25).astype(BF16)
        for pair in range(heads // 2):
            outs = []
            for h in (2 * pair, 2 * pair + 1):
                inner = dot_last(queries, head_keys[h][:extent])
                scores = jnp.where(allowed, 1.0 + inner * (1.0 + 0.5 * inner), 0.0)
                outs.append(matmul(scores.astype(BF16), head_values[h][:extent]))
            numer = jnp.where(lower, outs[0], outs[1])
            denom = pltpu.roll(jnp.where(lower, outs[1], outs[0]), DV, 1)
            recip = 1.0 / denom
            attended = numer * recip
            lanes = slice(pair * LANES, (pair + 1) * LANES)
            att_ref[rows, lanes] = attended.astype(BF16)
            attf_ref[rows, lanes] = attended
            rden_ref[rows, lanes] = recip
    for k, mask in enumerate(SLOT_MASKS):
        out_ref = (kept_ref, sent_ref)[k // 2]
        at = (k % 2) * width
        out_ref[:, at : at + width] = att_ref[block_at(group ^ mask, tokens), :]


def back_body(
    first_ref, group_ref, g0_ref, g1_ref, near_ref, qkv_ref, attf_ref, rden_ref, hr_in, w_in,
    kept_ref, sent_ref, term_ref, qt_ref, aug_ref, nb_ref, ag_ref, bars_ref, hr_ref, w_ref, sems,
):
    loads = start_copies([(hr_in, hr_ref), (w_in, w_ref)], sems, 0)
    first, group = first_ref[0], group_ref[0]
    tokens = g0_ref.shape[0]
    length, width = ag_ref.shape
    heads = width // DV
    qk = heads * HF
    for k, (g_ref, at) in enumerate(((g0_ref, 0), (g1_ref, 0), (near_ref, 0), (near_ref, width))):
        ag_ref[block_at(group ^ SLOT_MASKS[k], tokens), :] = g_ref[:, at : at + width]
    lower = lane_in(LANES, 0, DV)
    queries = (qkv_ref[:, :qk].astype(F32) * 0.25).astype(BF16)
    raw_keys = qkv_ref[:, qk : 2 * qk]
    keys = (raw_keys.astype(F32) * 0.25).astype(BF16)
    head_queries, head_keys, head_values = [], [], []
    for h in range(heads):
        own = lane_in(qk, h * HF, (h + 1) * HF)
        head_queries.append(masked(own, queries))
        head_keys.append(masked(own, keys))
    for h in range(heads):
        lanes = slice((h // 2) * LANES, (h // 2 + 1) * LANES)
        own = lower if h % 2 == 0 else jnp.logical_not(lower)
        numer_bar = ag_ref[:, lanes].astype(F32) * rden_ref[:, lanes]
        products = jnp.where(own, numer_bar * attf_ref[:, lanes], 0.0)
        denom_bar = -jnp.sum(products, axis=1, keepdims=True)
        column = DV if h % 2 == 0 else 0
        numer_bar = jnp.where(own, numer_bar, 0.0)
        nb_ref[h] = numer_bar.astype(BF16)
        aug_ref[h] = jnp.where(
            lane_in(LANES, column, column + 1), denom_bar, numer_bar
        ).astype(BF16)
        low = 2 * qk + (h // 2) * LANES
        tile = qkv_ref[:, low : low + LANES]
        head_values.append(jnp.where(own, tile, jnp.ones_like(tile)))
    qt_ref[...] = jnp.zeros_like(qt_ref)
    for i in range(length // TILE):
        low = i * TILE
        extent = length - low
        rows = slice(low, low + TILE)
        s_pos = low + lax.broadcasted_iota(jnp.int32, (TILE, 1), 0)
        t_pos = low + lax.broadcasted_iota(jnp.int32, (1, extent), 1)
        start = jnp.where(t_pos >= first, first, 0)
        allowed = (s_pos <= t_pos) & (s_pos >= start)
        key_total = jnp.zeros((TILE, qk), F32)
        query_total = jnp.zeros((qk, extent), F32)
        for pair in range(heads // 2):
            value_total = jnp.zeros((TILE, LANES), F32)
            for h in (2 * pair, 2 * pair + 1):
                inner = dot_last(raw_keys[rows], head_queries[h][low:])
                scores = jnp.where(allowed, 1.0 + inner * (1.0 + 0.5 * inner), 0.0)
                value_total += matmul(scores.astype(BF16), nb_ref[h, low:, :])
                bar = dot_last(head_values[h][rows], aug_ref[h, low:, :])
                slope = jnp.where(allowed, bar * (1.0 + inner), 0.0).astype(BF16)
                key_total += matmul(slope, head_queries[h][low:])
                query_total += dot_first(head_keys[h][rows], slope)
            lanes = slice(2 * qk + pair * LANES, 2 * qk + (pair + 1) * LANES)
            bars_ref[rows, lanes] = value_total.astype(BF16)
        bars_ref[rows, qk : 2 * qk] = key_total.astype(BF16)
        qt_ref[:, low:] += query_total
    bars_ref[:, :qk] = qt_ref[...].T.astype(BF16)
    for copy in loads:
        copy.wait()
    term = jnp.zeros((bars_ref.shape[1], hr_ref.shape[2]), F32)
    for k, mask in enumerate(SLOT_MASKS):
        bars = bars_ref[block_at(group ^ mask, tokens), :]
        (kept_ref, sent_ref)[k // 2][k % 2] = dot_last(bars, w_ref[...]).astype(BF16)
        term += dot_first(bars, hr_ref[k])
    term_ref[...] = term.T.astype(BF16)


def middle_body(
    member_ref, a0_ref, a1_ref, hidden_ref, w_ref,
    middle_ref, mlp_ref, att_ref, gain_ref,
):
    member = member_ref[0]
    part = a0_ref.shape[1] // 2
    for m, mask in enumerate((0, 1, 2, 3)):
        at = (m % 2) * part
        att_ref[:, block_at(member ^ mask, part)] = (a0_ref, a1_ref)[m // 2][:, at : at + part]
    width = att_ref.shape[1]
    pick_gain = jnp.where(lane_in(LANES, 0, 1), jnp.ones((8, LANES), BF16), 0)
    gain = dot_last(pick_gain, w_ref[:, width:])
    gain_ref[...] = gain
    middle = hidden_ref[...].astype(F32) + dot_last(att_ref[...], w_ref[:, :width])
    middle_ref[...] = middle
    scale = lax.rsqrt(jnp.mean(middle * middle, axis=1, keepdims=True) + EPSILON)
    mlp_ref[...] = (middle * scale * gain[:1]).astype(BF16)


def middle_back_body(
    member_ref, own_ref, near_ref, far_ref, middle_ref, gain_ref, cot_ref, attended_ref, w_ref,
    grad_ref, g0_ref, g1_ref, out_ref, att_ref,
):
    member = member_ref[0]
    width = att_ref.shape[1]
    part = g0_ref.shape[1] // 2
    gain = gain_ref[:1]
    mlp_grad = own_ref[0].astype(F32) + near_ref[0].astype(F32) + far_ref[...].astype(F32)
    middle = middle_ref[...]
    scale = lax.rsqrt(jnp.mean(middle * middle, axis=1, keepdims=True) + EPSILON)
    normed = middle * scale
    scaled = mlp_grad * gain
    inner = jnp.mean(normed * scaled, axis=1, keepdims=True)
    grad = cot_ref[...].astype(F32) + scale * (scaled - normed * inner)
    grad_ref[...] = grad
    bar = grad.astype(BF16)
    att_ref[...] = matmul(bar, w_ref[:, :width]).astype(BF16)
    for m, mask in enumerate((0, 1, 2, 3)):
        at = (m % 2) * part
        (g0_ref, g1_ref)[m // 2][:, at : at + part] = att_ref[:, block_at(member ^ mask, part)]
    out_ref[:, :width] = dot_first(bar, attended_ref[...]).astype(BF16)
    term = jnp.sum(mlp_grad * normed, axis=0, keepdims=True)
    out_ref[:, width:] = jnp.broadcast_to(term, (LANES, term.shape[1])).T.astype(BF16)


def start_copies(pairs, sems, first):
    copies = [
        pltpu.make_async_copy(source, target, sems.at[first + n])
        for n, (source, target) in enumerate(pairs)
    ]
    for copy in copies:
        copy.start()
    return copies


def forward_units(x_blocks, c_blocks, weights_ref, hidden_refs, put):
    wg_ref, wu_ref, wd_ref = (weights_ref.at[m] for m in range(3))
    total = weights_ref.shape[1]
    edges = list(range(0, total, TILE)) + [total]
    spans = list(zip(edges[:-1], edges[1:]))
    tokens = TILE

    for b, (x_ref, c_ref) in enumerate(zip(x_blocks, c_blocks)):
        rows = slice(b * tokens, (b + 1) * tokens)
        x_rows = x_ref[...]
        c_rows = c_ref[...]
        kept = []
        for low, high in spans:
            gate = dot_last(x_rows, wg_ref[low:high, :])
            up = dot_last(x_rows, wu_ref[low:high, :])
            back = dot_last(c_rows, wd_ref[low:high, :])
            sig = 1.0 / (1.0 + jnp.exp(-gate))
            silu = gate * sig
            act = (silu * up).astype(BF16)
            gate_bar = (back * up * (sig + silu * (1.0 - sig))).astype(BF16)
            up_bar = (back * silu).astype(BF16)
            for value, ref in zip((act, gate_bar, up_bar), hidden_refs):
                ref[low:high, rows] = value.T
            kept.append((act, gate_bar, up_bar))
        branch = sum(matmul(kept[n][0], wd_ref[low:high, :]) for n, (low, high) in enumerate(spans))
        grad = sum(matmul(kept[n][1], wg_ref[low:high, :]) for n, (low, high) in enumerate(spans))
        grad += sum(matmul(kept[n][2], wu_ref[low:high, :]) for n, (low, high) in enumerate(spans))
        put(b, branch, grad)


def weight_terms(units, index, m, left_ref, rows_ref, term_ref):
    slots, _, part = term_ref.shape
    step = min(part, 256)
    for at in range(0, part, step):
        lanes = pl.ds(pl.multiple_of(index * part + at, step), step)
        out = matmul(left_ref[...], rows_ref[:, lanes]).astype(BF16)
        for s in range(slots):
            term_ref[s, m * units : (m + 1) * units, at : at + step] = out[s * units : (s + 1) * units]


def weight_body(units, parts, sides, *refs):
    index_ref, lefts, refs = refs[0], refs[1 : 1 + len(sides)], refs[1 + len(sides) :]
    count = 3 * len(set(sides))
    sources, term_refs, refs = refs[:count], refs[count : count + parts], refs[count + parts :]
    rows_ref, left_refs, sems = refs[0], refs[1 : 1 + len(sides)], refs[1 + len(sides)]
    tokens = sources[0].shape[0]
    pairs = [
        (source, rows_ref.at[n // 3, pl.ds(tokens * (n % 3), source.shape[0]), :])
        for n, source in enumerate(sources)
    ]
    for copy in start_copies(pairs + list(zip(lefts, left_refs)), sems, 0):
        copy.wait()
    for n, term_ref in enumerate(term_refs):
        index = index_ref[0] if n == parts - 1 else 1 - index_ref[0]
        for m, side in enumerate(sides):
            weight_terms(units, index, m, left_refs[m], rows_ref.at[side], term_ref)


def feed_forward_body(units, parts, *refs):
    index_ref, sources, piece_ref, refs = refs[0], refs[1:7], refs[7], refs[8:]
    grad_refs, branch_refs, hidden_outs, refs = refs[:2], refs[2:4], refs[4:6], refs[6:]
    term_refs, refs = refs[:parts], refs[parts:]
    rows_ref, weights_ref, hidden_refs, branch_buf, grad_buf, term_buf, sems = *refs[:2], refs[2:5], *refs[5:]
    tokens = sources[0].shape[0]
    pairs = [
        (source, rows_ref.at[n // 3, pl.ds(tokens * (n % 3), source.shape[0]), :])
        for n, source in enumerate(sources)
    ]
    count, slots, _, part = piece_ref.shape
    pairs += [
        (
            piece_ref.at[y, s, pl.ds(m * units, units), :],
            weights_ref.at[m, pl.ds(s * units, units), pl.ds(y * part, part)],
        )
        for m in range(3)
        for y in range(count)
        for s in range(slots)
    ]
    for copy in start_copies(pairs, sems, 0):
        copy.wait()
    x_blocks, c_blocks = (
        [rows_ref.at[n, pl.ds(tokens * b, tokens), :] for b in range(SPLIT)] for n in range(2)
    )
    stores = []

    def put(b, branch, grad):
        branch_buf[b] = branch.astype(BF16)
        grad_buf[b] = grad.astype(BF16)
        done = [
            (grad_buf.at[b], grad_refs[b // 2].at[b % 2]),
            (branch_buf.at[b], branch_refs[b // 2].at[b % 2]),
        ]
        lanes = pl.ds(b * tokens, tokens)
        outs = zip((hidden_refs[0], hidden_refs[2]), hidden_outs)
        done += [(ref.at[:, lanes], out.at[:, lanes]) for ref, out in outs]
        stores.extend(start_copies(done, sems, len(pairs) + len(stores)))

    forward_units(x_blocks, c_blocks, weights_ref, hidden_refs, put)
    for n, term_ref in enumerate(term_refs):
        index = index_ref[0] if n == parts - 1 else 1 - index_ref[0]
        weight_terms(units, index, 0, hidden_refs[1], rows_ref.at[0], term_buf.at[n])
        stores.extend(start_copies([(term_buf.at[n], term_ref)], sems, len(pairs) + len(stores)))
    for copy in stores:
        copy.wait()


def on_device(
    dp,
    hidden_in,
    query_weight,
    key_weight,
    value_weight,
    output_weight,
    gate_weight,
    up_weight,
    down_weight,
    gain_attn,
    gain_mlp,
    first_length,
    cotangent,
):
    member = lax.axis_index("feat")
    me = lax.axis_index(dp)
    bits = len(dp)
    size = 1 << bits
    links = list(range(1, bits))
    core = me & 1
    group = 2 * (member & 1) + core
    tokens, width = hidden_in.shape
    length = GROUPS * tokens
    member_arr, group_arr = member.reshape(1), group.reshape(1)

    latest = {}

    def send(link, how, *blocks):
        blocks = [after(block, *latest.get(link, ())) for block in blocks]
        latest[link] = tuple(how(block) for block in blocks)
        return latest[link] if len(blocks) > 1 else latest[link][0]

    def link_of(bit):
        return ("core", "x", "y")[min(bit, 2)]

    def swap_bit(block, bit):
        return send(link_of(bit), partial(hop, bit=bit), block)

    def reduce_bits(term, order, left):
        left = sorted(left, reverse=True)
        for bit in order:
            axis = left.index(bit)
            mine = (me >> bit) & 1
            other = swap_bit(pick(term, 1 - mine, axis), bit)
            term = add_rounded(pick(term, mine, axis), other)
            left.remove(bit)
        return term

    side = (me >> 1) & 1

    def in_place(shares):
        shares = [jnp.where(core == 0, shares[k], shares[k ^ 1]) for k in range(SPLIT)]
        return [jnp.where(side == 0, shares[k], shares[k ^ 2]) for k in range(SPLIT)]

    rows = query_weight.shape[0]
    qk = H * HF // GROUPS
    vw = H * DV // GROUPS
    attn_pack = jnp.concatenate(
        [
            query_weight.reshape(rows, GROUPS, qk),
            key_weight.reshape(rows, GROUPS, qk),
            value_weight.reshape(rows, GROUPS, vw),
        ],
        axis=2,
    )
    attn_pack = (attn_pack.astype(F32) * gain_attn.astype(F32)[:, None, None]).astype(BF16)
    cols = attn_pack.shape[2]
    attn_pack = attn_pack.transpose(1, 0, 2).reshape(2, 2, rows, cols)
    sent = pick(attn_pack, 1 - core, 1).reshape(2 * rows, cols)
    lengths = jnp.broadcast_to(first_length.astype(BF16)[:, None], (16, cols))
    sent = swap_bit(jnp.concatenate([lengths, sent], axis=0), 0)
    first = jnp.where((member >> 1) == core, first_length, sent[0, :1].astype(jnp.int32))
    sent = sent[16:].reshape(2, rows, cols)
    attn_pack = pair_up(core, pick(attn_pack, core, 1), sent, 2)

    output_pack = jnp.concatenate(
        [output_weight.T, jnp.pad(gain_mlp[:, None], ((0, 0), (0, LANES - 1)))], axis=1
    )
    same = pick(attn_pack, member & 1).reshape(rows, 2 * cols)
    flip = pick(attn_pack, 1 - (member & 1)).reshape(rows, 2 * cols)
    far = cross(jnp.concatenate([same, flip, output_pack], axis=1), 2)
    flips = [
        jnp.concatenate([flip, output_pack], axis=1),
        far[:, 2 * cols :],
    ]
    hidden = [away(hidden_in, mask) for mask in (0, 2)]
    near = cross(after(jnp.concatenate(flips, axis=0), *hidden), 1)
    both = [
        jnp.concatenate([same, output_pack], axis=1),
        near[:rows],
        jnp.concatenate([far[:, : 2 * cols], far[:, 4 * cols :]], axis=1),
        near[rows:],
    ]
    both = after(place(both, [member ^ m for m in range(GROUPS)]), *hidden)
    hidden_units = down_weight.shape[0]
    units = -(-hidden_units // (16 * SPLIT)) * 16
    stacked = jnp.stack([gate_weight.T, up_weight.T, down_weight])
    stacked = jnp.pad(stacked, ((0, 0), (0, SPLIT * units - hidden_units), (0, 0)))
    block = stacked.shape[2]
    aligned = block % LANES == 0
    stacked = stacked.reshape(3, 2, 2, units, block)
    kept = [pick(stacked, side, 1), swap_bit(pick(stacked, 1 - side, 1), 1)]
    sent = swap_bit(jnp.concatenate([pick(part, 1 - core, 1) for part in kept], axis=2), 0)
    kept = [pick(part, core, 1) for part in kept]
    own = in_place([kept[0], sent[:, :, :block], kept[1], sent[:, :, block:]])
    own = jnp.concatenate(own, axis=2)
    output_mat = both[:, :, 2 * cols :].reshape(GROUPS * rows, -1)
    output_mat = pair_up((me >> links[-1]) & 1, output_mat, swap_bit(output_mat, links[-1]), 0)
    attn_mat = both[:, :, : 2 * cols].reshape(GROUPS, rows, 2, cols).transpose(2, 0, 1, 3)
    for bit in links:
        attn_mat = pair_up((me >> bit) & 1, attn_mat, swap_bit(attn_mat, bit), 0)
        attn_mat = attn_mat.reshape((-1,) + attn_mat.shape[2:])
    attn_mat = attn_mat.reshape(width, cols)
    hidden_pair = swap_bit(jnp.concatenate(hidden, axis=0), 0)

    far_axes = dp[: bits - SPLIT_BITS] + ("feat",)

    weights = lax.all_gather(after(own.reshape(3 * units, SPLIT * block), *hidden), far_axes)
    weights = weights.reshape(-1, GROUPS, 3 * units, SPLIT * block)
    if not aligned:
        weights = weights.transpose(1, 2, 0, 3).reshape(1, GROUPS, 3 * units, width)

    def pair_with(own, far):
        return [own, far, swap_bit(jnp.concatenate([own, far], axis=0), 0)]

    hr, qkv, out, sent, attf, rden = kernel_call(
        front_body,
        [((GROUPS, tokens, width), BF16), ((length, cols), BF16)]
        + [((tokens, 2 * vw), BF16)] * 2
        + [((length, vw), F32)] * 2,
        (first, group_arr, *hidden, hidden_pair, attn_mat),
        scalars=2,
        scratch=(pltpu.VMEM((length, vw), BF16),),
        flops=8 * 2**30,
        limit=24,
    )
    sent = swap_bit(sent, 0)
    for axis, bit in enumerate(links[-2::-1], 1):
        output_mat = pair_up((me >> bit) & 1, output_mat, swap_bit(output_mat, bit), axis)
    cot_far = swap_bit(cotangent, 1)
    for axis, bit in ((len(links), 0),):
        output_mat = pair_up((me >> bit) & 1, output_mat, swap_bit(output_mat, bit), axis)
    output_mat = output_mat.reshape(width, -1)
    cots = pair_with(cotangent, cot_far)
    out = [jnp.concatenate([part[:, at : at + vw] for part in (out, sent)], axis=1) for at in (0, vw)]
    out = [home(out[0], 0), home(out[1], 2)]
    middle, mlp_in, attended, gain8 = kernel_call(
        middle_body,
        [
            ((tokens, width), F32),
            ((tokens, width), BF16),
            ((tokens, H * DV), BF16),
            ((8, width), F32),
        ],
        (member_arr, *out, hidden_in, output_mat),
        scalars=1,
        flops=2**30,
        limit=12,
    )

    mlps = pair_with(mlp_in, swap_bit(mlp_in, 1))
    blocks = (SPLIT, tokens, width)
    parts = 2 if aligned and bits == SPLIT_BITS + 1 else 1
    part = me >> SPLIT_BITS if parts == 2 else jnp.zeros((), jnp.int32)
    hidden_shape = (GROUPS * units, SPLIT * tokens)
    outs = kernel_call(
        partial(feed_forward_body, units, parts),
        [((2, tokens, width), BF16, True)] * 4
        + [(hidden_shape, BF16, True)] * 2
        + [((GROUPS, units, width // parts), BF16, True)] * parts,
        (part.reshape(1), *mlps, *cots, weights),
        scalars=1,
        remote=7,
        scratch=(
            pltpu.VMEM((2, SPLIT * tokens, width), BF16),
            pltpu.VMEM((3, GROUPS * units, width), BF16),
            *[pltpu.VMEM(hidden_shape, BF16)] * 3,
            pltpu.VMEM(blocks, BF16),
            pltpu.VMEM(blocks, BF16),
            pltpu.VMEM((parts, GROUPS, units, width // parts), BF16),
            pltpu.SemaphoreType.DMA((6 + 3 * weights.shape[0] * GROUPS + 4 * SPLIT + parts,)),
        ),
        flops=14 * 2**30,
        limit=56,
    )
    grads, grads_sent, branch, branch_sent, act_t, up_t = outs[:6]

    late = kernel_call(
        partial(weight_body, units, parts, (0, 1)),
        [((GROUPS, 2 * units, width // parts), BF16)] * parts,
        (part.reshape(1), up_t, act_t, *mlps, *cots),
        scalars=1,
        remote=8,
        scratch=(
            pltpu.VMEM((2, SPLIT * tokens, width), BF16),
            *[pltpu.VMEM(hidden_shape, BF16)] * 2,
            pltpu.SemaphoreType.DMA((8,)),
        ),
        flops=4 * 2**30,
        limit=56,
    )
    terms = [pair[n] for n in range(parts) for pair in (outs[6:], late)]
    grads_sent = swap_bit(grads_sent, 0)
    grad_far = swap_bit(add_rounded(grads[1], grads_sent[1]), 1)
    branch_sent = swap_bit(branch_sent, 0)
    def reduce_terms(terms):
        if parts == 2:
            return add_rounded(terms[1], swap_bit(terms[0], SPLIT_BITS))
        far_bits = list(range(SPLIT_BITS, bits))[::-1]
        term = terms[0].reshape(GROUPS, terms[0].shape[1], -1, SPLIT * block).transpose(2, 0, 1, 3)
        return reduce_bits(term.reshape((2,) * len(far_bits) + term.shape[1:]), far_bits, far_bits)

    terms = [after(term, grad_far) if n >= 2 * (parts - 1) else term for n, term in enumerate(terms)]
    sums = [reduce_terms(terms[h::2]) for h in range(2)]
    totals = [lax.psum_scatter(term, "feat") for term in sums]

    middle_grad, *att_grad, output_term = kernel_call(
        middle_back_body,
        [((tokens, width), F32)]
        + [((tokens, 2 * vw), BF16)] * 2
        + [((width, H * DV + LANES), BF16)],
        (member_arr, grads, grads_sent, after(grad_far, sums[0]), middle, gain8, cotangent, attended, output_mat),
        scalars=1,
        scratch=(pltpu.VMEM((tokens, H * DV), BF16),),
        flops=2**30,
        limit=56,
    )
    att_grad = [away(part, mask) for part, mask in zip(att_grad, (0, 2))]
    output_term = after(output_term, *att_grad).reshape((2,) * bits + (GROUPS, rows, H * DV + LANES))
    output_term = reduce_bits(output_term, [0], range(bits))
    att_sent = jnp.concatenate([part[:, vw:] for part in att_grad], axis=1)
    att_grad.append(swap_bit(after(att_sent, sums[0]), 0))
    output_term = reduce_bits(output_term, links[:1], links)
    branch_far = swap_bit(add_rounded(branch[1], branch_sent[1]), 1)
    att_grad = [after(part, sums[0]) for part in att_grad]
    input_parts, input_sent, attn_term = kernel_call(
        back_body,
        [((2, tokens, width), BF16)] * 2 + [((width, cols), BF16)],
        (first, group_arr, *att_grad, qkv, attf, rden, hr, attn_mat),
        scalars=2,
        scratch=(
            pltpu.VMEM((qk, length), F32),
            pltpu.VMEM((vw // DV, length, LANES), BF16),
            pltpu.VMEM((vw // DV, length, LANES), BF16),
            pltpu.VMEM((length, vw), BF16),
            pltpu.VMEM((length, cols), BF16),
            pltpu.VMEM(hr.shape, BF16),
            pltpu.VMEM(attn_mat.shape, BF16),
            pltpu.SemaphoreType.DMA((2,)),
        ),
        flops=12 * 2**30,
        remote=2,
        limit=56,
    )
    input_sent = swap_bit(input_sent, 0)
    input_parts = [after(add_rounded(input_parts[k], input_sent[k]), sums[1]) for k in range(2)]
    input_parts = [home(input_parts[0], 0), home(input_parts[1], 2)]
    total = jnp.concatenate(totals, axis=0).astype(F32)
    lanes = [total[:, j * block : (j + 1) * block] for j in range(SPLIT)]

    def share_total():
        own = [jnp.where(core == 0, lanes[x], lanes[x + 1]) for x in (0, 2)]
        sent = [jnp.where(core == 0, lanes[x + 1], lanes[x]) for x in (0, 2)]
        near = swap_bit(jnp.concatenate(sent, axis=1), 0)
        near = [near[:, :block], near[:, block:]]
        mine = [jnp.where(side == 0, both[0], both[1]) for both in (own, near)]
        sent = [jnp.where(side == 0, both[1], both[0]) for both in (own, near)]
        far = swap_bit(jnp.concatenate(sent, axis=0).astype(BF16), 1).astype(F32)
        return in_place([*mine, far[: 3 * units], far[3 * units :]]), far

    attn_term = after(attn_term, input_sent).reshape((2,) * len(links) + (2, GROUPS, rows, cols))
    attn_term = reduce_bits(attn_term, links[:0:-1], links)
    output_term = reduce_bits(output_term, links[1:], links[1:])
    attn_term = reduce_bits(attn_term, links[:1], links[:1])
    shares, shares_last = share_total()
    other = swap_bit(pick(attn_term, 1 - core), 0)
    attn_term = pair_up(core, pick(attn_term, core), other, 2).reshape(GROUPS, rows, 2 * cols)
    both = jnp.concatenate([attn_term, output_term], axis=2)
    kept, sent = ([pick(both, member ^ m) for m in pair] for pair in ((0, 2), (1, 3)))
    sent = after(jnp.stack(sent), *totals)
    input_parts = [after(part, sent) for part in input_parts]
    scaled_grad = input_parts[0].astype(F32) + input_parts[1].astype(F32)
    residual = hidden_in.astype(F32)
    scale = lax.rsqrt(jnp.mean(residual * residual, axis=1, keepdims=True) + EPSILON)
    normed = residual * scale
    inner = jnp.mean(normed * scaled_grad, axis=1, keepdims=True)
    input_grad = middle_grad + scale * (scaled_grad - normed * inner)

    sent = cross(sent, 1)
    out = [add_rounded(kept[k][:, 2 * cols :], sent[k][:, 2 * cols :]) for k in range(2)]
    same, flip = ([part[k][:, : 2 * cols] for k in range(2)] for part in (kept, sent))
    last = after(jnp.concatenate([same[1], flip[1], out[1]], axis=1), shares_last)
    last = cross(last, 2).astype(F32)
    output_sum = out[0].astype(F32) + last[:, 4 * cols :]
    output_grad = output_sum[:, : H * DV].T
    mlp_gain_grad = output_sum[:, H * DV]
    same = same[0].astype(F32) + last[:, : 2 * cols]
    flip = flip[0].astype(F32) + last[:, 2 * cols : 4 * cols]
    attn_grad = pair_up(member & 1, same, flip, 0).reshape(2, rows, 2, cols)
    attn_grad = attn_grad.transpose(1, 0, 2, 3).reshape(rows, GROUPS, cols)
    scale_rows = gain_attn.astype(F32)[:, None]
    query_raw = attn_grad[:, :, :qk].reshape(rows, H * HF)
    key_raw = attn_grad[:, :, qk : 2 * qk].reshape(rows, H * HF)
    value_raw = attn_grad[:, :, 2 * qk :].reshape(rows, H * DV)
    attn_gain_grad = (
        jnp.sum(query_raw * query_weight.astype(F32), axis=1)
        + jnp.sum(key_raw * key_weight.astype(F32), axis=1)
        + jnp.sum(value_raw * value_weight.astype(F32), axis=1)
    )

    block_out = (
        middle
        + branch[0].astype(F32)
        + branch_sent[0].astype(F32)
        + branch_far.astype(F32)
    ).astype(BF16)

    total = jnp.stack([share.reshape(3, units, block) for share in shares], axis=1)
    total = total.reshape(3, SPLIT * units, block)[:, :hidden_units]
    return (
        block_out,
        input_grad,
        query_raw * scale_rows,
        key_raw * scale_rows,
        value_raw * scale_rows,
        output_grad,
        total[0].T,
        total[1].T,
        total[2],
        attn_gain_grad,
        mlp_gain_grad,
    )


def solution(mesh):
    bits = mesh.shape["dp"].bit_length() - 1
    dp = tuple(f"bit{bit}" for bit in reversed(range(bits)))
    fine = jax.sharding.Mesh(mesh.devices.reshape((2,) * bits + (GROUPS,)), dp + ("feat",))
    both = dp + ("feat",)
    in_specs = (
        P(both, None),
        P(both, None),
        P(both, None),
        P(both, None),
        P(None, both),
        P(dp, "feat"),
        P(dp, "feat"),
        P("feat", dp),
        P(both),
        P(both),
        P(dp),
        P(both, None),
    )
    out_specs = (
        P(both, None),
        P(both, None),
        P(both, None),
        P(both, None),
        P(both, None),
        P(None, both),
        P(dp, "feat"),
        P(dp, "feat"),
        P("feat", dp),
        P(both),
        P(both),
    )
    return jax.shard_map(
        partial(on_device, dp), mesh=fine, in_specs=in_specs, out_specs=out_specs, check_vma=False
    )
```

```python
from functools import partial

import jax
import jax.numpy as jnp
from jax import lax
from jax.experimental import pallas as pl
from jax.experimental.pallas import tpu as pltpu
from jax.sharding import PartitionSpec as P

H = 16
HF = 16
DV = 64
SEQ_LEN = 1024
EPSILON = 1e-05

LANES = 128
TILE = 256
GROUPS = 4
F32 = jnp.float32
BF16 = jnp.bfloat16

SLOT_MASKS = (0, 2, 1, 3)
SPLIT_BITS = 2
SPLIT = 1 << SPLIT_BITS


def matmul(first_matrix, second_matrix):
    return jnp.dot(first_matrix, second_matrix, preferred_element_type=F32)


def dot_first(first_matrix, second_matrix):
    return lax.dot_general(
        first_matrix, second_matrix, (((0,), (0,)), ((), ())), preferred_element_type=F32
    )


def dot_last(first_matrix, second_matrix):
    return lax.dot_general(
        first_matrix, second_matrix, (((1,), (1,)), ((), ())), preferred_element_type=F32
    )


def hop(block, bit):
    return lax.ppermute(block, f"bit{bit}", [(0, 1), (1, 0)])


def cross(block, mask):
    return lax.ppermute(block, "feat", [(i, i ^ mask) for i in range(GROUPS)])


def home_pairs(mask):
    pairs = []
    for core in range(2):
        for z in range(GROUPS):
            group = 2 * (z & 1) + core
            pairs.append((core * GROUPS + z, (z >> 1) * GROUPS + (group ^ mask)))
    return pairs


def home(block, mask):
    return lax.ppermute(block, ("bit0", "feat"), home_pairs(mask))


def away(block, mask):
    return lax.ppermute(block, ("bit0", "feat"), [(b, a) for a, b in home_pairs(mask)])


def after(block, *earlier):
    return lax.optimization_barrier((block,) + earlier)[0]


def add_rounded(first, second):
    return (first.astype(F32) + second.astype(F32)).astype(BF16)


def pick(blocks, index, axis=0):
    return lax.dynamic_index_in_dim(blocks, index, axis, keepdims=False)


def place(blocks, sources):
    total = jnp.zeros((len(blocks),) + blocks[0].shape, blocks[0].dtype)
    for block, source in zip(blocks, sources):
        total = lax.dynamic_update_index_in_dim(total, block, source, 0)
    return total


def pair_up(bit, own, other, axis):
    return jnp.where(bit == 0, jnp.stack([own, other], axis), jnp.stack([other, own], axis))


def kernel_call(body, outs, operands, scalars=0, remote=0, scratch=(), flops=0, limit=56):
    smem = pl.BlockSpec(memory_space=pltpu.SMEM)
    vmem = pl.BlockSpec(memory_space=pltpu.VMEM)
    hbm = pl.BlockSpec(memory_space=pl.ANY)
    out_specs = [hbm if len(out) > 2 else vmem for out in outs]
    outs = [jax.ShapeDtypeStruct(out[0], out[1]) for out in outs]
    nbytes = sum(o.size * o.dtype.itemsize for o in list(operands) + outs)
    return pl.pallas_call(
        body,
        out_shape=outs,
        in_specs=[smem] * scalars + [vmem] * (len(operands) - scalars - remote) + [hbm] * remote,
        out_specs=out_specs,
        scratch_shapes=list(scratch),
        compiler_params=pltpu.CompilerParams(vmem_limit_bytes=limit * 1024 * 1024),
        cost_estimate=pl.CostEstimate(flops=flops, bytes_accessed=nbytes, transcendentals=0),
    )(*operands)


def lane_in(width, low, high):
    lane = lax.broadcasted_iota(jnp.int32, (1, width), 1)
    return (lane >= low) & (lane < high)


def block_at(index, size):
    return pl.ds(pl.multiple_of(index * size, size), size)


def masked(own, values):
    return jnp.where(own, values, jnp.zeros_like(values))


def front_body(
    first_ref, group_ref, h0_ref, h1_ref, pair_ref, w_ref,
    hr_ref, qkv_ref, kept_ref, sent_ref, attf_ref, rden_ref, att_ref,
):
    first, group = first_ref[0], group_ref[0]
    tokens = h0_ref.shape[0]
    length, width = att_ref.shape
    heads = width // DV
    qk = heads * HF
    for k, (h_ref, at) in enumerate(((h0_ref, 0), (h1_ref, 0), (pair_ref, 0), (pair_ref, tokens))):
        rows = h_ref[at : at + tokens, :].astype(F32)
        scale = lax.rsqrt(jnp.mean(rows * rows, axis=1, keepdims=True) + EPSILON)
        normed = (rows * scale).astype(BF16)
        hr_ref[k] = normed
        qkv_ref[block_at(group ^ SLOT_MASKS[k], tokens), :] = matmul(normed, w_ref[...]).astype(BF16)
    lower = lane_in(LANES, 0, DV)
    keys = qkv_ref[:, qk : 2 * qk]
    head_keys = [masked(lane_in(qk, h * HF, (h + 1) * HF), keys) for h in range(heads)]
    head_values = []
    for h in range(heads):
        low = 2 * qk + (h // 2) * LANES
        tile = qkv_ref[:, low : low + LANES]
        own = lower if h % 2 == 0 else jnp.logical_not(lower)
        head_values.append(jnp.where(own, tile, jnp.ones_like(tile)))
    for i in range(length // TILE):
        extent = (i + 1) * TILE
        rows = slice(i * TILE, extent)
        t_pos = i * TILE + lax.broadcasted_iota(jnp.int32, (TILE, 1), 0)
        s_pos = lax.broadcasted_iota(jnp.int32, (1, extent), 1)
        start = jnp.where(t_pos >= first, first, 0)
        allowed = (s_pos <= t_pos) & (s_pos >= start)
        queries = (qkv_ref[rows, :qk].astype(F32) * 0.25).astype(BF16)
        for pair in range(heads // 2):
            outs = []
            for h in (2 * pair, 2 * pair + 1):
                inner = dot_last(queries, head_keys[h][:extent])
                scores = jnp.where(allowed, 1.0 + inner * (1.0 + 0.5 * inner), 0.0)
                outs.append(matmul(scores.astype(BF16), head_values[h][:extent]))
            numer = jnp.where(lower, outs[0], outs[1])
            denom = pltpu.roll(jnp.where(lower, outs[1], outs[0]), DV, 1)
            recip = 1.0 / denom
            attended = numer * recip
            lanes = slice(pair * LANES, (pair + 1) * LANES)
            att_ref[rows, lanes] = attended.astype(BF16)
            attf_ref[rows, lanes] = attended
            rden_ref[rows, lanes] = recip
    for k, mask in enumerate(SLOT_MASKS):
        out_ref = (kept_ref, sent_ref)[k // 2]
        at = (k % 2) * width
        out_ref[:, at : at + width] = att_ref[block_at(group ^ mask, tokens), :]


def back_body(
    first_ref, group_ref, g0_ref, g1_ref, near_ref, qkv_ref, attf_ref, rden_ref, hr_in, w_in,
    kept_ref, sent_ref, term_ref, qt_ref, aug_ref, nb_ref, ag_ref, bars_ref, hr_ref, w_ref, sems,
):
    loads = start_copies([(hr_in, hr_ref), (w_in, w_ref)], sems, 0)
    first, group = first_ref[0], group_ref[0]
    tokens = g0_ref.shape[0]
    length, width = ag_ref.shape
    heads = width // DV
    qk = heads * HF
    for k, (g_ref, at) in enumerate(((g0_ref, 0), (g1_ref, 0), (near_ref, 0), (near_ref, width))):
        ag_ref[block_at(group ^ SLOT_MASKS[k], tokens), :] = g_ref[:, at : at + width]
    lower = lane_in(LANES, 0, DV)
    queries = (qkv_ref[:, :qk].astype(F32) * 0.25).astype(BF16)
    raw_keys = qkv_ref[:, qk : 2 * qk]
    keys = (raw_keys.astype(F32) * 0.25).astype(BF16)
    head_queries, head_keys, head_values = [], [], []
    for h in range(heads):
        own = lane_in(qk, h * HF, (h + 1) * HF)
        head_queries.append(masked(own, queries))
        head_keys.append(masked(own, keys))
    for h in range(heads):
        lanes = slice((h // 2) * LANES, (h // 2 + 1) * LANES)
        own = lower if h % 2 == 0 else jnp.logical_not(lower)
        numer_bar = ag_ref[:, lanes].astype(F32) * rden_ref[:, lanes]
        products = jnp.where(own, numer_bar * attf_ref[:, lanes], 0.0)
        denom_bar = -jnp.sum(products, axis=1, keepdims=True)
        column = DV if h % 2 == 0 else 0
        numer_bar = jnp.where(own, numer_bar, 0.0)
        nb_ref[h] = numer_bar.astype(BF16)
        aug_ref[h] = jnp.where(
            lane_in(LANES, column, column + 1), denom_bar, numer_bar
        ).astype(BF16)
        low = 2 * qk + (h // 2) * LANES
        tile = qkv_ref[:, low : low + LANES]
        head_values.append(jnp.where(own, tile, jnp.ones_like(tile)))
    qt_ref[...] = jnp.zeros_like(qt_ref)
    for i in range(length // TILE):
        low = i * TILE
        extent = length - low
        rows = slice(low, low + TILE)
        s_pos = low + lax.broadcasted_iota(jnp.int32, (TILE, 1), 0)
        t_pos = low + lax.broadcasted_iota(jnp.int32, (1, extent), 1)
        start = jnp.where(t_pos >= first, first, 0)
        allowed = (s_pos <= t_pos) & (s_pos >= start)
        key_total = jnp.zeros((TILE, qk), F32)
        query_total = jnp.zeros((qk, extent), F32)
        for pair in range(heads // 2):
            value_total = jnp.zeros((TILE, LANES), F32)
            for h in (2 * pair, 2 * pair + 1):
                inner = dot_last(raw_keys[rows], head_queries[h][low:])
                scores = jnp.where(allowed, 1.0 + inner * (1.0 + 0.5 * inner), 0.0)
                value_total += matmul(scores.astype(BF16), nb_ref[h, low:, :])
                bar = dot_last(head_values[h][rows], aug_ref[h, low:, :])
                slope = jnp.where(allowed, bar * (1.0 + inner), 0.0).astype(BF16)
                key_total += matmul(slope, head_queries[h][low:])
                query_total += dot_first(head_keys[h][rows], slope)
            lanes = slice(2 * qk + pair * LANES, 2 * qk + (pair + 1) * LANES)
            bars_ref[rows, lanes] = value_total.astype(BF16)
        bars_ref[rows, qk : 2 * qk] = key_total.astype(BF16)
        qt_ref[:, low:] += query_total
    bars_ref[:, :qk] = qt_ref[...].T.astype(BF16)
    for copy in loads:
        copy.wait()
    term = jnp.zeros((bars_ref.shape[1], hr_ref.shape[2]), F32)
    for k, mask in enumerate(SLOT_MASKS):
        bars = bars_ref[block_at(group ^ mask, tokens), :]
        (kept_ref, sent_ref)[k // 2][k % 2] = dot_last(bars, w_ref[...]).astype(BF16)
        term += dot_first(bars, hr_ref[k])
    term_ref[...] = term.T.astype(BF16)


def project(member_ref, a0_ref, a1_ref, hidden_ref, w_ref, att_ref):
    member = member_ref[0]
    part = a0_ref.shape[1] // 2
    for m, mask in enumerate((0, 1, 2, 3)):
        at = (m % 2) * part
        att_ref[:, block_at(member ^ mask, part)] = (a0_ref, a1_ref)[m // 2][:, at : at + part]
    width = att_ref.shape[1]
    pick_gain = jnp.where(lane_in(LANES, 0, 1), jnp.ones((8, LANES), BF16), 0)
    gain = dot_last(pick_gain, w_ref[:, width:])[:1]
    middle = hidden_ref[...].astype(F32) + dot_last(att_ref[...], w_ref[:, :width])
    scale = lax.rsqrt(jnp.mean(middle * middle, axis=1, keepdims=True) + EPSILON)
    return middle, scale, gain


def middle_body(member_ref, a0_ref, a1_ref, hidden_ref, w_ref, mlp_ref, att_ref):
    middle, scale, gain = project(member_ref, a0_ref, a1_ref, hidden_ref, w_ref, att_ref)
    mlp_ref[...] = (middle * scale * gain).astype(BF16)


def middle_back_body(
    blocks, member_ref, core_ref, own_ref, near_ref, far_ref, a0_ref, a1_ref, hidden_ref, cot_ref, w_ref,
    grad_ref, g0_ref, g1_ref, kept_ref, sent_ref, middle_ref, attended_ref, att_ref, out_ref,
):
    middle, scale, gain = project(member_ref, a0_ref, a1_ref, hidden_ref, w_ref, attended_ref)
    middle_ref[...] = middle
    member = member_ref[0]
    width = att_ref.shape[1]
    part = g0_ref.shape[1] // 2
    mlp_grad = own_ref[0].astype(F32) + near_ref[0].astype(F32) + far_ref[...].astype(F32)
    normed = middle * scale
    scaled = mlp_grad * gain
    inner = jnp.mean(normed * scaled, axis=1, keepdims=True)
    grad = cot_ref[...].astype(F32) + scale * (scaled - normed * inner)
    grad_ref[...] = grad
    bar = grad.astype(BF16)
    att_ref[...] = matmul(bar, w_ref[:, :width]).astype(BF16)
    for m, mask in enumerate((0, 1, 2, 3)):
        at = (m % 2) * part
        (g0_ref, g1_ref)[m // 2][:, at : at + part] = att_ref[:, block_at(member ^ mask, part)]
    out_ref[:, :width] = dot_first(bar, attended_ref[...]).astype(BF16)
    term = jnp.sum(mlp_grad * normed, axis=0, keepdims=True)
    out_ref[:, width:] = jnp.broadcast_to(term, (LANES, term.shape[1])).T.astype(BF16)
    block = out_ref.shape[0] // blocks
    for n in range(blocks // 2):
        low = out_ref[2 * n * block : (2 * n + 1) * block, :]
        high = out_ref[(2 * n + 1) * block : (2 * n + 2) * block, :]
        rows = slice(n * block, (n + 1) * block)
        kept_ref[rows, :] = jnp.where(core_ref[0] == 0, low, high)
        sent_ref[rows, :] = jnp.where(core_ref[0] == 0, high, low)


def start_copies(pairs, sems, first):
    copies = [
        pltpu.make_async_copy(source, target, sems.at[first + n])
        for n, (source, target) in enumerate(pairs)
    ]
    for copy in copies:
        copy.start()
    return copies


def forward_units(x_blocks, c_blocks, weights_ref, hidden_refs, put):
    wg_ref, wu_ref, wd_ref = (weights_ref.at[m] for m in range(3))
    total = weights_ref.shape[1]
    edges = list(range(0, total, TILE)) + [total]
    spans = list(zip(edges[:-1], edges[1:]))
    tokens = TILE

    for b, (x_ref, c_ref) in enumerate(zip(x_blocks, c_blocks)):
        rows = slice(b * tokens, (b + 1) * tokens)
        x_rows = x_ref[...]
        c_rows = c_ref[...]
        kept = []
        for low, high in spans:
            gate = dot_last(x_rows, wg_ref[low:high, :])
            up = dot_last(x_rows, wu_ref[low:high, :])
            back = dot_last(c_rows, wd_ref[low:high, :])
            sig = 1.0 / (1.0 + jnp.exp(-gate))
            silu = gate * sig
            act = (silu * up).astype(BF16)
            gate_bar = (back * up * (sig + silu * (1.0 - sig))).astype(BF16)
            up_bar = (back * silu).astype(BF16)
            for value, ref in zip((act, gate_bar, up_bar), hidden_refs):
                ref[low:high, rows] = value.T
            kept.append((act, gate_bar, up_bar))
        branch = sum(matmul(kept[n][0], wd_ref[low:high, :]) for n, (low, high) in enumerate(spans))
        grad = sum(matmul(kept[n][1], wg_ref[low:high, :]) for n, (low, high) in enumerate(spans))
        grad += sum(matmul(kept[n][2], wu_ref[low:high, :]) for n, (low, high) in enumerate(spans))
        put(b, branch, grad)


def weight_terms(units, index, m, left_ref, rows_ref, term_ref):
    slots, _, part = term_ref.shape
    step = min(part, 256)
    for at in range(0, part, step):
        lanes = pl.ds(pl.multiple_of(index * part + at, step), step)
        out = matmul(left_ref[...], rows_ref[:, lanes]).astype(BF16)
        for s in range(slots):
            term_ref[s, m * units : (m + 1) * units, at : at + step] = out[s * units : (s + 1) * units]


def weight_body(units, parts, sides, *refs):
    index_ref, lefts, refs = refs[0], refs[1 : 1 + len(sides)], refs[1 + len(sides) :]
    count = 3 * len(set(sides))
    sources, term_refs, refs = refs[:count], refs[count : count + parts], refs[count + parts :]
    rows_ref, left_refs, sems = refs[0], refs[1 : 1 + len(sides)], refs[1 + len(sides)]
    tokens = sources[0].shape[0]
    pairs = [
        (source, rows_ref.at[n // 3, pl.ds(tokens * (n % 3), source.shape[0]), :])
        for n, source in enumerate(sources)
    ]
    for copy in start_copies(pairs + list(zip(lefts, left_refs)), sems, 0):
        copy.wait()
    for n, term_ref in enumerate(term_refs):
        index = index_ref[0] if n == parts - 1 else 1 - index_ref[0]
        for m, side in enumerate(sides):
            weight_terms(units, index, m, left_refs[m], rows_ref.at[side], term_ref)


def feed_forward_body(units, parts, *refs):
    index_ref, sources, piece_ref, refs = refs[0], refs[1:7], refs[7], refs[8:]
    grad_refs, branch_refs, hidden_outs, refs = refs[:2], refs[2:4], refs[4:6], refs[6:]
    term_refs, refs = refs[:parts], refs[parts:]
    rows_ref, weights_ref, hidden_refs, branch_buf, grad_buf, term_buf, sems = *refs[:2], refs[2:5], *refs[5:]
    tokens = sources[0].shape[0]
    pairs = [
        (source, rows_ref.at[n // 3, pl.ds(tokens * (n % 3), source.shape[0]), :])
        for n, source in enumerate(sources)
    ]
    count, slots, _, part = piece_ref.shape
    pairs += [
        (
            piece_ref.at[y, s, pl.ds(m * units, units), :],
            weights_ref.at[m, pl.ds(s * units, units), pl.ds(y * part, part)],
        )
        for m in range(3)
        for y in range(count)
        for s in range(slots)
    ]
    for copy in start_copies(pairs, sems, 0):
        copy.wait()
    x_blocks, c_blocks = (
        [rows_ref.at[n, pl.ds(tokens * b, tokens), :] for b in range(SPLIT)] for n in range(2)
    )
    stores = []

    def put(b, branch, grad):
        branch_buf[b] = branch.astype(BF16)
        grad_buf[b] = grad.astype(BF16)
        done = [
            (grad_buf.at[b], grad_refs[b // 2].at[b % 2]),
            (branch_buf.at[b], branch_refs[b // 2].at[b % 2]),
        ]
        lanes = pl.ds(b * tokens, tokens)
        outs = zip((hidden_refs[0], hidden_refs[2]), hidden_outs)
        done += [(ref.at[:, lanes], out.at[:, lanes]) for ref, out in outs]
        stores.extend(start_copies(done, sems, len(pairs) + len(stores)))

    forward_units(x_blocks, c_blocks, weights_ref, hidden_refs, put)
    for n, term_ref in enumerate(term_refs):
        index = index_ref[0] if n == parts - 1 else 1 - index_ref[0]
        weight_terms(units, index, 0, hidden_refs[1], rows_ref.at[0], term_buf.at[n])
        stores.extend(start_copies([(term_buf.at[n], term_ref)], sems, len(pairs) + len(stores)))
    for copy in stores:
        copy.wait()


def on_device(
    dp,
    hidden_in,
    query_weight,
    key_weight,
    value_weight,
    output_weight,
    gate_weight,
    up_weight,
    down_weight,
    gain_attn,
    gain_mlp,
    first_length,
    cotangent,
):
    member = lax.axis_index("feat")
    me = lax.axis_index(dp)
    bits = len(dp)
    size = 1 << bits
    links = list(range(1, bits))
    core = me & 1
    group = 2 * (member & 1) + core
    tokens, width = hidden_in.shape
    length = GROUPS * tokens
    member_arr, group_arr = member.reshape(1), group.reshape(1)

    latest = {}

    def send(link, how, *blocks):
        blocks = [after(block, *latest.get(link, ())) for block in blocks]
        latest[link] = tuple(how(block) for block in blocks)
        return latest[link] if len(blocks) > 1 else latest[link][0]

    def link_of(bit):
        return ("core", "x", "y")[min(bit, 2)]

    def swap_bit(block, bit):
        return send(link_of(bit), partial(hop, bit=bit), block)

    def reduce_bits(term, order, left):
        left = sorted(left, reverse=True)
        for bit in order:
            axis = left.index(bit)
            mine = (me >> bit) & 1
            other = swap_bit(pick(term, 1 - mine, axis), bit)
            term = add_rounded(pick(term, mine, axis), other)
            left.remove(bit)
        return term

    side = (me >> 1) & 1

    def in_place(shares):
        shares = [jnp.where(core == 0, shares[k], shares[k ^ 1]) for k in range(SPLIT)]
        return [jnp.where(side == 0, shares[k], shares[k ^ 2]) for k in range(SPLIT)]

    rows = query_weight.shape[0]
    qk = H * HF // GROUPS
    vw = H * DV // GROUPS
    attn_pack = jnp.concatenate(
        [
            query_weight.reshape(rows, GROUPS, qk),
            key_weight.reshape(rows, GROUPS, qk),
            value_weight.reshape(rows, GROUPS, vw),
        ],
        axis=2,
    )
    attn_pack = (attn_pack.astype(F32) * gain_attn.astype(F32)[:, None, None]).astype(BF16)
    cols = attn_pack.shape[2]
    attn_pack = attn_pack.transpose(1, 0, 2).reshape(2, 2, rows, cols)
    sent = pick(attn_pack, 1 - core, 1).reshape(2 * rows, cols)
    lengths = jnp.broadcast_to(first_length.astype(BF16)[:, None], (16, cols))
    sent = swap_bit(jnp.concatenate([lengths, sent], axis=0), 0)
    first = jnp.where((member >> 1) == core, first_length, sent[0, :1].astype(jnp.int32))
    sent = sent[16:].reshape(2, rows, cols)
    attn_pack = pair_up(core, pick(attn_pack, core, 1), sent, 2)

    output_pack = jnp.concatenate(
        [output_weight.T, jnp.pad(gain_mlp[:, None], ((0, 0), (0, LANES - 1)))], axis=1
    )
    same = pick(attn_pack, member & 1).reshape(rows, 2 * cols)
    flip = pick(attn_pack, 1 - (member & 1)).reshape(rows, 2 * cols)
    far = cross(jnp.concatenate([same, flip, output_pack], axis=1), 2)
    flips = [
        jnp.concatenate([flip, output_pack], axis=1),
        far[:, 2 * cols :],
    ]
    hidden = [away(hidden_in, mask) for mask in (0, 2)]
    near = cross(after(jnp.concatenate(flips, axis=0), *hidden), 1)
    both = [
        jnp.concatenate([same, output_pack], axis=1),
        near[:rows],
        jnp.concatenate([far[:, : 2 * cols], far[:, 4 * cols :]], axis=1),
        near[rows:],
    ]
    both = after(place(both, [member ^ m for m in range(GROUPS)]), *hidden)
    hidden_units = down_weight.shape[0]
    units = -(-hidden_units // (16 * SPLIT)) * 16
    stacked = jnp.stack([gate_weight.T, up_weight.T, down_weight])
    stacked = jnp.pad(stacked, ((0, 0), (0, SPLIT * units - hidden_units), (0, 0)))
    block = stacked.shape[2]
    aligned = block % LANES == 0
    stacked = stacked.reshape(3, 2, 2, units, block)
    kept = [pick(stacked, side, 1), swap_bit(pick(stacked, 1 - side, 1), 1)]
    sent = swap_bit(jnp.concatenate([pick(part, 1 - core, 1) for part in kept], axis=2), 0)
    kept = [pick(part, core, 1) for part in kept]
    own = in_place([kept[0], sent[:, :, :block], kept[1], sent[:, :, block:]])
    own = jnp.concatenate(own, axis=2)
    output_mat = both[:, :, 2 * cols :].reshape(GROUPS * rows, -1)
    output_mat = pair_up((me >> links[-1]) & 1, output_mat, swap_bit(output_mat, links[-1]), 0)
    attn_mat = both[:, :, : 2 * cols].reshape(GROUPS, rows, 2, cols).transpose(2, 0, 1, 3)
    for bit in links:
        attn_mat = pair_up((me >> bit) & 1, attn_mat, swap_bit(attn_mat, bit), 0)
        attn_mat = attn_mat.reshape((-1,) + attn_mat.shape[2:])
    attn_mat = attn_mat.reshape(width, cols)
    hidden_pair = swap_bit(jnp.concatenate(hidden, axis=0), 0)

    far_axes = dp[: bits - SPLIT_BITS] + ("feat",)

    weights = lax.all_gather(after(own.reshape(3 * units, SPLIT * block), *hidden), far_axes)
    weights = weights.reshape(-1, GROUPS, 3 * units, SPLIT * block)
    if not aligned:
        weights = weights.transpose(1, 2, 0, 3).reshape(1, GROUPS, 3 * units, width)

    def pair_with(own, far):
        return [own, far, swap_bit(jnp.concatenate([own, far], axis=0), 0)]

    hr, qkv, out, sent, attf, rden = kernel_call(
        front_body,
        [((GROUPS, tokens, width), BF16), ((length, cols), BF16)]
        + [((tokens, 2 * vw), BF16)] * 2
        + [((length, vw), F32)] * 2,
        (first, group_arr, *hidden, hidden_pair, attn_mat),
        scalars=2,
        scratch=(pltpu.VMEM((length, vw), BF16),),
        flops=8 * 2**30,
        limit=24,
    )
    sent = swap_bit(sent, 0)
    for axis, bit in enumerate(links[-2::-1], 1):
        output_mat = pair_up((me >> bit) & 1, output_mat, swap_bit(output_mat, bit), axis)
    cot_far = swap_bit(cotangent, 1)
    for axis, bit in ((len(links), 0),):
        output_mat = pair_up((me >> bit) & 1, output_mat, swap_bit(output_mat, bit), axis)
    output_mat = output_mat.reshape(width, -1)
    cots = pair_with(cotangent, cot_far)
    out = [jnp.concatenate([part[:, at : at + vw] for part in (out, sent)], axis=1) for at in (0, vw)]
    out = [home(out[0], 0), home(out[1], 2)]
    (mlp_in,) = kernel_call(
        middle_body,
        [((tokens, width), BF16)],
        (member_arr, *out, hidden_in, output_mat),
        scalars=1,
        scratch=(pltpu.VMEM((tokens, H * DV), BF16),),
        flops=2**30,
        limit=12,
    )

    mlps = pair_with(mlp_in, swap_bit(mlp_in, 1))
    blocks = (SPLIT, tokens, width)
    parts = 2 if aligned and bits == SPLIT_BITS + 1 else 1
    part = me >> SPLIT_BITS if parts == 2 else jnp.zeros((), jnp.int32)
    hidden_shape = (GROUPS * units, SPLIT * tokens)
    outs = kernel_call(
        partial(feed_forward_body, units, parts),
        [((2, tokens, width), BF16, True)] * 4
        + [(hidden_shape, BF16, True)] * 2
        + [((GROUPS, units, width // parts), BF16, True)] * parts,
        (part.reshape(1), *mlps, *cots, weights),
        scalars=1,
        remote=7,
        scratch=(
            pltpu.VMEM((2, SPLIT * tokens, width), BF16),
            pltpu.VMEM((3, GROUPS * units, width), BF16),
            *[pltpu.VMEM(hidden_shape, BF16)] * 3,
            pltpu.VMEM(blocks, BF16),
            pltpu.VMEM(blocks, BF16),
            pltpu.VMEM((parts, GROUPS, units, width // parts), BF16),
            pltpu.SemaphoreType.DMA((6 + 3 * weights.shape[0] * GROUPS + 4 * SPLIT + parts,)),
        ),
        flops=14 * 2**30,
        limit=56,
    )
    grads, grads_sent, branch, branch_sent, act_t, up_t = outs[:6]

    late = kernel_call(
        partial(weight_body, units, parts, (0, 1)),
        [((GROUPS, 2 * units, width // parts), BF16)] * parts,
        (part.reshape(1), up_t, act_t, *mlps, *cots),
        scalars=1,
        remote=8,
        scratch=(
            pltpu.VMEM((2, SPLIT * tokens, width), BF16),
            *[pltpu.VMEM(hidden_shape, BF16)] * 2,
            pltpu.SemaphoreType.DMA((8,)),
        ),
        flops=4 * 2**30,
        limit=56,
    )
    terms = [pair[n] for n in range(parts) for pair in (outs[6:], late)]
    grads_sent = swap_bit(grads_sent, 0)
    grad_far = swap_bit(add_rounded(grads[1], grads_sent[1]), 1)
    branch_sent = swap_bit(branch_sent, 0)
    def reduce_terms(terms):
        if parts == 2:
            return add_rounded(terms[1], swap_bit(terms[0], SPLIT_BITS))
        far_bits = list(range(SPLIT_BITS, bits))[::-1]
        term = terms[0].reshape(GROUPS, terms[0].shape[1], -1, SPLIT * block).transpose(2, 0, 1, 3)
        return reduce_bits(term.reshape((2,) * len(far_bits) + term.shape[1:]), far_bits, far_bits)

    terms = [after(term, grad_far) if n >= 2 * (parts - 1) else term for n, term in enumerate(terms)]
    sums = [reduce_terms(terms[h::2]) for h in range(2)]
    totals = [lax.psum_scatter(term, "feat") for term in sums]

    middle_grad, *att_grad, output_kept, output_sent, middle = kernel_call(
        partial(middle_back_body, size),
        [((tokens, width), F32)]
        + [((tokens, 2 * vw), BF16)] * 2
        + [((width // 2, H * DV + LANES), BF16)] * 2
        + [((tokens, width), F32)],
        (member_arr, core.reshape(1), grads, grads_sent, after(grad_far, sums[0]), *out, hidden_in, cotangent, output_mat),
        scalars=2,
        scratch=(
            pltpu.VMEM((tokens, H * DV), BF16),
            pltpu.VMEM((tokens, H * DV), BF16),
            pltpu.VMEM((width, H * DV + LANES), BF16),
        ),
        flops=2**30,
        limit=56,
    )
    att_grad = [away(part, mask) for part, mask in zip(att_grad, (0, 2))]
    output_term = add_rounded(output_kept, swap_bit(after(output_sent, *att_grad), 0))
    output_term = output_term.reshape((2,) * len(links) + (GROUPS, rows, H * DV + LANES))
    att_sent = jnp.concatenate([part[:, vw:] for part in att_grad], axis=1)
    att_grad.append(swap_bit(after(att_sent, sums[0]), 0))
    output_term = reduce_bits(output_term, links[:1], links)
    branch_far = swap_bit(add_rounded(branch[1], branch_sent[1]), 1)
    att_grad = [after(part, sums[0]) for part in att_grad]
    input_parts, input_sent, attn_term = kernel_call(
        back_body,
        [((2, tokens, width), BF16)] * 2 + [((width, cols), BF16)],
        (first, group_arr, *att_grad, qkv, attf, rden, hr, attn_mat),
        scalars=2,
        scratch=(
            pltpu.VMEM((qk, length), F32),
            pltpu.VMEM((vw // DV, length, LANES), BF16),
            pltpu.VMEM((vw // DV, length, LANES), BF16),
            pltpu.VMEM((length, vw), BF16),
            pltpu.VMEM((length, cols), BF16),
            pltpu.VMEM(hr.shape, BF16),
            pltpu.VMEM(attn_mat.shape, BF16),
            pltpu.SemaphoreType.DMA((2,)),
        ),
        flops=12 * 2**30,
        remote=2,
        limit=56,
    )
    input_sent = swap_bit(input_sent, 0)
    input_parts = [after(add_rounded(input_parts[k], input_sent[k]), sums[1]) for k in range(2)]
    input_parts = [home(input_parts[0], 0), home(input_parts[1], 2)]
    total = jnp.concatenate(totals, axis=0).astype(F32)
    lanes = [total[:, j * block : (j + 1) * block] for j in range(SPLIT)]

    def share_total():
        own = [jnp.where(core == 0, lanes[x], lanes[x + 1]) for x in (0, 2)]
        sent = [jnp.where(core == 0, lanes[x + 1], lanes[x]) for x in (0, 2)]
        near = swap_bit(jnp.concatenate(sent, axis=1), 0)
        near = [near[:, :block], near[:, block:]]
        mine = [jnp.where(side == 0, both[0], both[1]) for both in (own, near)]
        sent = [jnp.where(side == 0, both[1], both[0]) for both in (own, near)]
        far = swap_bit(jnp.concatenate(sent, axis=0).astype(BF16), 1).astype(F32)
        return in_place([*mine, far[: 3 * units], far[3 * units :]]), far

    attn_term = after(attn_term, input_sent).reshape((2,) * len(links) + (2, GROUPS, rows, cols))
    attn_term = reduce_bits(attn_term, links[:0:-1], links)
    output_term = reduce_bits(output_term, links[1:], links[1:])
    attn_term = reduce_bits(attn_term, links[:1], links[:1])
    shares, shares_last = share_total()
    other = swap_bit(pick(attn_term, 1 - core), 0)
    attn_term = pair_up(core, pick(attn_term, core), other, 2).reshape(GROUPS, rows, 2 * cols)
    both = jnp.concatenate([attn_term, output_term], axis=2)
    kept, sent = ([pick(both, member ^ m) for m in pair] for pair in ((0, 2), (1, 3)))
    sent = after(jnp.stack(sent), *totals)
    input_parts = [after(part, sent) for part in input_parts]
    scaled_grad = input_parts[0].astype(F32) + input_parts[1].astype(F32)
    residual = hidden_in.astype(F32)
    scale = lax.rsqrt(jnp.mean(residual * residual, axis=1, keepdims=True) + EPSILON)
    normed = residual * scale
    inner = jnp.mean(normed * scaled_grad, axis=1, keepdims=True)
    input_grad = middle_grad + scale * (scaled_grad - normed * inner)

    sent = cross(sent, 1)
    out = [add_rounded(kept[k][:, 2 * cols :], sent[k][:, 2 * cols :]) for k in range(2)]
    same, flip = ([part[k][:, : 2 * cols] for k in range(2)] for part in (kept, sent))
    last = after(jnp.concatenate([same[1], flip[1], out[1]], axis=1), shares_last)
    last = cross(last, 2).astype(F32)
    output_sum = out[0].astype(F32) + last[:, 4 * cols :]
    output_grad = output_sum[:, : H * DV].T
    mlp_gain_grad = output_sum[:, H * DV]
    same = same[0].astype(F32) + last[:, : 2 * cols]
    flip = flip[0].astype(F32) + last[:, 2 * cols : 4 * cols]
    attn_grad = pair_up(member & 1, same, flip, 0).reshape(2, rows, 2, cols)
    attn_grad = attn_grad.transpose(1, 0, 2, 3).reshape(rows, GROUPS, cols)
    scale_rows = gain_attn.astype(F32)[:, None]
    query_raw = attn_grad[:, :, :qk].reshape(rows, H * HF)
    key_raw = attn_grad[:, :, qk : 2 * qk].reshape(rows, H * HF)
    value_raw = attn_grad[:, :, 2 * qk :].reshape(rows, H * DV)
    attn_gain_grad = (
        jnp.sum(query_raw * query_weight.astype(F32), axis=1)
        + jnp.sum(key_raw * key_weight.astype(F32), axis=1)
        + jnp.sum(value_raw * value_weight.astype(F32), axis=1)
    )

    block_out = (
        middle
        + branch[0].astype(F32)
        + branch_sent[0].astype(F32)
        + branch_far.astype(F32)
    ).astype(BF16)

    total = jnp.stack([share.reshape(3, units, block) for share in shares], axis=1)
    total = total.reshape(3, SPLIT * units, block)[:, :hidden_units]
    return (
        block_out,
        input_grad,
        query_raw * scale_rows,
        key_raw * scale_rows,
        value_raw * scale_rows,
        output_grad,
        total[0].T,
        total[1].T,
        total[2],
        attn_gain_grad,
        mlp_gain_grad,
    )


def solution(mesh):
    bits = mesh.shape["dp"].bit_length() - 1
    dp = tuple(f"bit{bit}" for bit in reversed(range(bits)))
    fine = jax.sharding.Mesh(mesh.devices.reshape((2,) * bits + (GROUPS,)), dp + ("feat",))
    both = dp + ("feat",)
    in_specs = (
        P(both, None),
        P(both, None),
        P(both, None),
        P(both, None),
        P(None, both),
        P(dp, "feat"),
        P(dp, "feat"),
        P("feat", dp),
        P(both),
        P(both),
        P(dp),
        P(both, None),
    )
    out_specs = (
        P(both, None),
        P(both, None),
        P(both, None),
        P(both, None),
        P(both, None),
        P(None, both),
        P(dp, "feat"),
        P(dp, "feat"),
        P("feat", dp),
        P(both),
        P(both),
    )
    return jax.shard_map(
        partial(on_device, dp), mesh=fine, in_specs=in_specs, out_specs=out_specs, check_vma=False
    )
```

```python
from functools import partial

import jax
import jax.numpy as jnp
from jax import lax
from jax.experimental import pallas as pl
from jax.experimental.pallas import tpu as pltpu
from jax.sharding import PartitionSpec as P

H = 16
HF = 16
DV = 64
SEQ_LEN = 1024
EPSILON = 1e-05

LANES = 128
TILE = 256
GROUPS = 4
F32 = jnp.float32
BF16 = jnp.bfloat16

SLOT_MASKS = (0, 2, 1, 3)
SPLIT_BITS = 2
SPLIT = 1 << SPLIT_BITS


def matmul(first_matrix, second_matrix):
    return jnp.dot(first_matrix, second_matrix, preferred_element_type=F32)


def dot_first(first_matrix, second_matrix):
    return lax.dot_general(
        first_matrix, second_matrix, (((0,), (0,)), ((), ())), preferred_element_type=F32
    )


def dot_last(first_matrix, second_matrix):
    return lax.dot_general(
        first_matrix, second_matrix, (((1,), (1,)), ((), ())), preferred_element_type=F32
    )


def hop(block, bit):
    return lax.ppermute(block, f"bit{bit}", [(0, 1), (1, 0)])


def cross(block, mask):
    return lax.ppermute(block, "feat", [(i, i ^ mask) for i in range(GROUPS)])


def home_pairs(mask):
    pairs = []
    for core in range(2):
        for z in range(GROUPS):
            group = 2 * (z & 1) + core
            pairs.append((core * GROUPS + z, (z >> 1) * GROUPS + (group ^ mask)))
    return pairs


def home(block, mask):
    return lax.ppermute(block, ("bit0", "feat"), home_pairs(mask))


def away(block, mask):
    return lax.ppermute(block, ("bit0", "feat"), [(b, a) for a, b in home_pairs(mask)])


def after(block, *earlier):
    return lax.optimization_barrier((block,) + earlier)[0]


def add_rounded(first, second):
    return (first.astype(F32) + second.astype(F32)).astype(BF16)


def pick(blocks, index, axis=0):
    return lax.dynamic_index_in_dim(blocks, index, axis, keepdims=False)


def place(blocks, sources):
    total = jnp.zeros((len(blocks),) + blocks[0].shape, blocks[0].dtype)
    for block, source in zip(blocks, sources):
        total = lax.dynamic_update_index_in_dim(total, block, source, 0)
    return total


def pair_up(bit, own, other, axis):
    return jnp.where(bit == 0, jnp.stack([own, other], axis), jnp.stack([other, own], axis))


def kernel_call(body, outs, operands, scalars=0, remote=0, scratch=(), flops=0, limit=56):
    smem = pl.BlockSpec(memory_space=pltpu.SMEM)
    vmem = pl.BlockSpec(memory_space=pltpu.VMEM)
    hbm = pl.BlockSpec(memory_space=pl.ANY)
    out_specs = [hbm if len(out) > 2 else vmem for out in outs]
    outs = [jax.ShapeDtypeStruct(out[0], out[1]) for out in outs]
    nbytes = sum(o.size * o.dtype.itemsize for o in list(operands) + outs)
    return pl.pallas_call(
        body,
        out_shape=outs,
        in_specs=[smem] * scalars + [vmem] * (len(operands) - scalars - remote) + [hbm] * remote,
        out_specs=out_specs,
        scratch_shapes=list(scratch),
        compiler_params=pltpu.CompilerParams(vmem_limit_bytes=limit * 1024 * 1024),
        cost_estimate=pl.CostEstimate(flops=flops, bytes_accessed=nbytes, transcendentals=0),
    )(*operands)


def lane_in(width, low, high):
    lane = lax.broadcasted_iota(jnp.int32, (1, width), 1)
    return (lane >= low) & (lane < high)


def block_at(index, size):
    return pl.ds(pl.multiple_of(index * size, size), size)


def masked(own, values):
    return jnp.where(own, values, jnp.zeros_like(values))


def front_body(
    first_ref, group_ref, h0_ref, h1_ref, pair_ref, w_ref,
    hr_ref, qkv_ref, kept_ref, sent_ref, attf_ref, rden_ref, att_ref,
):
    first, group = first_ref[0], group_ref[0]
    tokens = h0_ref.shape[0]
    length, width = att_ref.shape
    heads = width // DV
    qk = heads * HF
    for k, (h_ref, at) in enumerate(((h0_ref, 0), (h1_ref, 0), (pair_ref, 0), (pair_ref, tokens))):
        rows = h_ref[at : at + tokens, :].astype(F32)
        scale = lax.rsqrt(jnp.mean(rows * rows, axis=1, keepdims=True) + EPSILON)
        normed = (rows * scale).astype(BF16)
        hr_ref[k] = normed
        qkv_ref[block_at(group ^ SLOT_MASKS[k], tokens), :] = matmul(normed, w_ref[...]).astype(BF16)
    lower = lane_in(LANES, 0, DV)
    keys = qkv_ref[:, qk : 2 * qk]
    head_keys = [masked(lane_in(qk, h * HF, (h + 1) * HF), keys) for h in range(heads)]
    head_values = []
    for h in range(heads):
        low = 2 * qk + (h // 2) * LANES
        tile = qkv_ref[:, low : low + LANES]
        own = lower if h % 2 == 0 else jnp.logical_not(lower)
        head_values.append(jnp.where(own, tile, jnp.ones_like(tile)))
    for i in range(length // TILE):
        extent = (i + 1) * TILE
        rows = slice(i * TILE, extent)
        t_pos = i * TILE + lax.broadcasted_iota(jnp.int32, (TILE, 1), 0)
        s_pos = lax.broadcasted_iota(jnp.int32, (1, extent), 1)
        start = jnp.where(t_pos >= first, first, 0)
        allowed = (s_pos <= t_pos) & (s_pos >= start)
        queries = (qkv_ref[rows, :qk].astype(F32) * 0.25).astype(BF16)
        for pair in range(heads // 2):
            outs = []
            for h in (2 * pair, 2 * pair + 1):
                inner = dot_last(queries, head_keys[h][:extent])
                scores = jnp.where(allowed, 1.0 + inner * (1.0 + 0.5 * inner), 0.0)
                outs.append(matmul(scores.astype(BF16), head_values[h][:extent]))
            numer = jnp.where(lower, outs[0], outs[1])
            denom = pltpu.roll(jnp.where(lower, outs[1], outs[0]), DV, 1)
            recip = 1.0 / denom
            attended = numer * recip
            lanes = slice(pair * LANES, (pair + 1) * LANES)
            att_ref[rows, lanes] = attended.astype(BF16)
            attf_ref[rows, lanes] = attended
            rden_ref[rows, lanes] = recip
    for k, mask in enumerate(SLOT_MASKS):
        out_ref = (kept_ref, sent_ref)[k // 2]
        at = (k % 2) * width
        out_ref[:, at : at + width] = att_ref[block_at(group ^ mask, tokens), :]


def back_body(
    first_ref, group_ref, g0_ref, g1_ref, near_ref, qkv_ref, attf_ref, rden_ref, hr_in, w_in,
    kept_ref, sent_ref, term_ref, qt_ref, aug_ref, nb_ref, ag_ref, bars_ref, hr_ref, w_ref, sems,
):
    loads = start_copies([(hr_in, hr_ref), (w_in, w_ref)], sems, 0)
    first, group = first_ref[0], group_ref[0]
    tokens = g0_ref.shape[0]
    length, width = ag_ref.shape
    heads = width // DV
    qk = heads * HF
    for k, (g_ref, at) in enumerate(((g0_ref, 0), (g1_ref, 0), (near_ref, 0), (near_ref, width))):
        ag_ref[block_at(group ^ SLOT_MASKS[k], tokens), :] = g_ref[:, at : at + width]
    lower = lane_in(LANES, 0, DV)
    queries = (qkv_ref[:, :qk].astype(F32) * 0.25).astype(BF16)
    raw_keys = qkv_ref[:, qk : 2 * qk]
    keys = (raw_keys.astype(F32) * 0.25).astype(BF16)
    head_queries, head_keys, head_values = [], [], []
    for h in range(heads):
        own = lane_in(qk, h * HF, (h + 1) * HF)
        head_queries.append(masked(own, queries))
        head_keys.append(masked(own, keys))
    for h in range(heads):
        lanes = slice((h // 2) * LANES, (h // 2 + 1) * LANES)
        own = lower if h % 2 == 0 else jnp.logical_not(lower)
        numer_bar = ag_ref[:, lanes].astype(F32) * rden_ref[:, lanes]
        products = jnp.where(own, numer_bar * attf_ref[:, lanes], 0.0)
        denom_bar = -jnp.sum(products, axis=1, keepdims=True)
        column = DV if h % 2 == 0 else 0
        numer_bar = jnp.where(own, numer_bar, 0.0)
        nb_ref[h] = numer_bar.astype(BF16)
        aug_ref[h] = jnp.where(
            lane_in(LANES, column, column + 1), denom_bar, numer_bar
        ).astype(BF16)
        low = 2 * qk + (h // 2) * LANES
        tile = qkv_ref[:, low : low + LANES]
        head_values.append(jnp.where(own, tile, jnp.ones_like(tile)))
    qt_ref[...] = jnp.zeros_like(qt_ref)
    for i in range(length // TILE):
        low = i * TILE
        extent = length - low
        rows = slice(low, low + TILE)
        s_pos = low + lax.broadcasted_iota(jnp.int32, (TILE, 1), 0)
        t_pos = low + lax.broadcasted_iota(jnp.int32, (1, extent), 1)
        start = jnp.where(t_pos >= first, first, 0)
        allowed = (s_pos <= t_pos) & (s_pos >= start)
        key_total = jnp.zeros((TILE, qk), F32)
        query_total = jnp.zeros((qk, extent), F32)
        for pair in range(heads // 2):
            value_total = jnp.zeros((TILE, LANES), F32)
            for h in (2 * pair, 2 * pair + 1):
                inner = dot_last(raw_keys[rows], head_queries[h][low:])
                scores = jnp.where(allowed, 1.0 + inner * (1.0 + 0.5 * inner), 0.0)
                value_total += matmul(scores.astype(BF16), nb_ref[h, low:, :])
                bar = dot_last(head_values[h][rows], aug_ref[h, low:, :])
                slope = jnp.where(allowed, bar * (1.0 + inner), 0.0).astype(BF16)
                key_total += matmul(slope, head_queries[h][low:])
                query_total += dot_first(head_keys[h][rows], slope)
            lanes = slice(2 * qk + pair * LANES, 2 * qk + (pair + 1) * LANES)
            bars_ref[rows, lanes] = value_total.astype(BF16)
        bars_ref[rows, qk : 2 * qk] = key_total.astype(BF16)
        qt_ref[:, low:] += query_total
    bars_ref[:, :qk] = qt_ref[...].T.astype(BF16)
    for copy in loads:
        copy.wait()
    term = jnp.zeros((bars_ref.shape[1], hr_ref.shape[2]), F32)
    for k, mask in enumerate(SLOT_MASKS):
        bars = bars_ref[block_at(group ^ mask, tokens), :]
        (kept_ref, sent_ref)[k // 2][k % 2] = dot_last(bars, w_ref[...]).astype(BF16)
        term += dot_first(bars, hr_ref[k])
    term_ref[...] = term.T.astype(BF16)


def project(member_ref, a0_ref, a1_ref, hidden_ref, w_ref, att_ref):
    member = member_ref[0]
    part = a0_ref.shape[1] // 2
    for m, mask in enumerate((0, 1, 2, 3)):
        at = (m % 2) * part
        att_ref[:, block_at(member ^ mask, part)] = (a0_ref, a1_ref)[m // 2][:, at : at + part]
    width = att_ref.shape[1]
    pick_gain = jnp.where(lane_in(LANES, 0, 1), jnp.ones((8, LANES), BF16), 0)
    gain = dot_last(pick_gain, w_ref[:, width:])[:1]
    middle = hidden_ref[...].astype(F32) + dot_last(att_ref[...], w_ref[:, :width])
    scale = lax.rsqrt(jnp.mean(middle * middle, axis=1, keepdims=True) + EPSILON)
    return middle, scale, gain


def middle_body(member_ref, a0_ref, a1_ref, hidden_ref, w_ref, mlp_ref, att_ref):
    middle, scale, gain = project(member_ref, a0_ref, a1_ref, hidden_ref, w_ref, att_ref)
    mlp_ref[...] = (middle * scale * gain).astype(BF16)


def middle_back_body(
    blocks, member_ref, core_ref, own_ref, near_ref, far_ref, a0_ref, a1_ref, hidden_ref, cot_ref, w_ref,
    grad_ref, g0_ref, g1_ref, kept_ref, sent_ref, middle_ref, attended_ref, att_ref, out_ref,
):
    middle, scale, gain = project(member_ref, a0_ref, a1_ref, hidden_ref, w_ref, attended_ref)
    middle_ref[...] = middle
    member = member_ref[0]
    width = att_ref.shape[1]
    part = g0_ref.shape[1] // 2
    mlp_grad = own_ref[0].astype(F32) + near_ref[0].astype(F32) + far_ref[...].astype(F32)
    normed = middle * scale
    scaled = mlp_grad * gain
    inner = jnp.mean(normed * scaled, axis=1, keepdims=True)
    grad = cot_ref[...].astype(F32) + scale * (scaled - normed * inner)
    grad_ref[...] = grad
    bar = grad.astype(BF16)
    att_ref[...] = matmul(bar, w_ref[:, :width]).astype(BF16)
    for m, mask in enumerate((0, 1, 2, 3)):
        at = (m % 2) * part
        (g0_ref, g1_ref)[m // 2][:, at : at + part] = att_ref[:, block_at(member ^ mask, part)]
    out_ref[:, :width] = dot_first(bar, attended_ref[...]).astype(BF16)
    term = jnp.sum(mlp_grad * normed, axis=0, keepdims=True)
    out_ref[:, width:] = jnp.broadcast_to(term, (LANES, term.shape[1])).T.astype(BF16)
    block = out_ref.shape[0] // blocks
    for n in range(blocks // 2):
        low = out_ref[2 * n * block : (2 * n + 1) * block, :]
        high = out_ref[(2 * n + 1) * block : (2 * n + 2) * block, :]
        rows = slice(n * block, (n + 1) * block)
        kept_ref[rows, :] = jnp.where(core_ref[0] == 0, low, high)
        sent_ref[rows, :] = jnp.where(core_ref[0] == 0, high, low)


def start_copies(pairs, sems, first):
    copies = [
        pltpu.make_async_copy(source, target, sems.at[first + n])
        for n, (source, target) in enumerate(pairs)
    ]
    for copy in copies:
        copy.start()
    return copies


def forward_units(x_blocks, c_blocks, weights_ref, hidden_refs, ready, put):
    wg_ref, wu_ref, wd_ref = (weights_ref.at[m] for m in range(3))
    total = weights_ref.shape[1]
    edges = list(range(0, total, TILE)) + [total]
    spans = list(zip(edges[:-1], edges[1:]))
    tokens = TILE

    for b, (x_ref, c_ref) in enumerate(zip(x_blocks, c_blocks)):
        rows = slice(b * tokens, (b + 1) * tokens)
        x_rows = x_ref[...]
        kept = []
        for low, high in spans:
            gate = dot_last(x_rows, wg_ref[low:high, :])
            up = dot_last(x_rows, wu_ref[low:high, :])
            if b == 0 and low == 0:
                ready()
            back = dot_last(c_ref[...], wd_ref[low:high, :])
            sig = 1.0 / (1.0 + jnp.exp(-gate))
            silu = gate * sig
            act = (silu * up).astype(BF16)
            gate_bar = (back * up * (sig + silu * (1.0 - sig))).astype(BF16)
            up_bar = (back * silu).astype(BF16)
            for value, ref in zip((act, gate_bar, up_bar), hidden_refs):
                ref[low:high, rows] = value.T
            kept.append((act, gate_bar, up_bar))
        branch = sum(matmul(kept[n][0], wd_ref[low:high, :]) for n, (low, high) in enumerate(spans))
        grad = sum(matmul(kept[n][1], wg_ref[low:high, :]) for n, (low, high) in enumerate(spans))
        grad += sum(matmul(kept[n][2], wu_ref[low:high, :]) for n, (low, high) in enumerate(spans))
        put(b, branch, grad)


def weight_terms(units, index, m, left_ref, rows_ref, term_ref):
    slots, _, part = term_ref.shape
    step = min(part, 256)
    for at in range(0, part, step):
        lanes = pl.ds(pl.multiple_of(index * part + at, step), step)
        out = matmul(left_ref[...], rows_ref[:, lanes]).astype(BF16)
        for s in range(slots):
            term_ref[s, m * units : (m + 1) * units, at : at + step] = out[s * units : (s + 1) * units]


def weight_body(units, parts, sides, *refs):
    index_ref, lefts, refs = refs[0], refs[1 : 1 + len(sides)], refs[1 + len(sides) :]
    count = 3 * len(set(sides))
    sources, term_refs, refs = refs[:count], refs[count : count + parts], refs[count + parts :]
    rows_ref, left_refs, sems = refs[0], refs[1 : 1 + len(sides)], refs[1 + len(sides)]
    tokens = sources[0].shape[0]
    pairs = [
        (source, rows_ref.at[n // 3, pl.ds(tokens * (n % 3), source.shape[0]), :])
        for n, source in enumerate(sources)
    ]
    for copy in start_copies(pairs + list(zip(lefts, left_refs)), sems, 0):
        copy.wait()
    for n, term_ref in enumerate(term_refs):
        index = index_ref[0] if n == parts - 1 else 1 - index_ref[0]
        for m, side in enumerate(sides):
            weight_terms(units, index, m, left_refs[m], rows_ref.at[side], term_ref)


def feed_forward_body(units, parts, *refs):
    index_ref, sources, piece_ref, refs = refs[0], refs[1:7], refs[7], refs[8:]
    grad_refs, branch_refs, hidden_outs, refs = refs[:2], refs[2:4], refs[4:6], refs[6:]
    term_refs, refs = refs[:parts], refs[parts:]
    rows_ref, weights_ref, hidden_refs, branch_buf, grad_buf, term_buf, sems = *refs[:2], refs[2:5], *refs[5:]
    tokens = sources[0].shape[0]
    rows = [
        (source, rows_ref.at[n // 3, pl.ds(tokens * (n % 3), source.shape[0]), :])
        for n, source in enumerate(sources)
    ]
    count, slots, _, part = piece_ref.shape
    mats = [
        [
            (
                piece_ref.at[y, s, pl.ds(m * units, units), :],
                weights_ref.at[m, pl.ds(s * units, units), pl.ds(y * part, part)],
            )
            for y in range(count)
            for s in range(slots)
        ]
        for m in range(3)
    ]
    early = rows[:3] + mats[0] + mats[1]
    pairs = early + rows[3:] + mats[2]
    loads = start_copies(pairs, sems, 0)
    for copy in loads[: len(early)]:
        copy.wait()

    def ready():
        for copy in loads[len(early) :]:
            copy.wait()

    x_blocks, c_blocks = (
        [rows_ref.at[n, pl.ds(tokens * b, tokens), :] for b in range(SPLIT)] for n in range(2)
    )
    stores = []

    def put(b, branch, grad):
        branch_buf[b] = branch.astype(BF16)
        grad_buf[b] = grad.astype(BF16)
        done = [
            (grad_buf.at[b], grad_refs[b // 2].at[b % 2]),
            (branch_buf.at[b], branch_refs[b // 2].at[b % 2]),
        ]
        lanes = pl.ds(b * tokens, tokens)
        outs = zip((hidden_refs[0], hidden_refs[2]), hidden_outs)
        done += [(ref.at[:, lanes], out.at[:, lanes]) for ref, out in outs]
        stores.extend(start_copies(done, sems, len(pairs) + len(stores)))

    forward_units(x_blocks, c_blocks, weights_ref, hidden_refs, ready, put)
    for n, term_ref in enumerate(term_refs):
        index = index_ref[0] if n == parts - 1 else 1 - index_ref[0]
        weight_terms(units, index, 0, hidden_refs[1], rows_ref.at[0], term_buf.at[n])
        stores.extend(start_copies([(term_buf.at[n], term_ref)], sems, len(pairs) + len(stores)))
    for copy in stores:
        copy.wait()


def on_device(
    dp,
    hidden_in,
    query_weight,
    key_weight,
    value_weight,
    output_weight,
    gate_weight,
    up_weight,
    down_weight,
    gain_attn,
    gain_mlp,
    first_length,
    cotangent,
):
    member = lax.axis_index("feat")
    me = lax.axis_index(dp)
    bits = len(dp)
    size = 1 << bits
    links = list(range(1, bits))
    core = me & 1
    group = 2 * (member & 1) + core
    tokens, width = hidden_in.shape
    length = GROUPS * tokens
    member_arr, group_arr = member.reshape(1), group.reshape(1)

    latest = {}

    def send(link, how, *blocks):
        blocks = [after(block, *latest.get(link, ())) for block in blocks]
        latest[link] = tuple(how(block) for block in blocks)
        return latest[link] if len(blocks) > 1 else latest[link][0]

    def link_of(bit):
        return ("core", "x", "y")[min(bit, 2)]

    def swap_bit(block, bit):
        return send(link_of(bit), partial(hop, bit=bit), block)

    def reduce_bits(term, order, left):
        left = sorted(left, reverse=True)
        for bit in order:
            axis = left.index(bit)
            mine = (me >> bit) & 1
            other = swap_bit(pick(term, 1 - mine, axis), bit)
            term = add_rounded(pick(term, mine, axis), other)
            left.remove(bit)
        return term

    side = (me >> 1) & 1

    def in_place(shares):
        shares = [jnp.where(core == 0, shares[k], shares[k ^ 1]) for k in range(SPLIT)]
        return [jnp.where(side == 0, shares[k], shares[k ^ 2]) for k in range(SPLIT)]

    rows = query_weight.shape[0]
    qk = H * HF // GROUPS
    vw = H * DV // GROUPS
    attn_pack = jnp.concatenate(
        [
            query_weight.reshape(rows, GROUPS, qk),
            key_weight.reshape(rows, GROUPS, qk),
            value_weight.reshape(rows, GROUPS, vw),
        ],
        axis=2,
    )
    attn_pack = (attn_pack.astype(F32) * gain_attn.astype(F32)[:, None, None]).astype(BF16)
    cols = attn_pack.shape[2]
    attn_pack = attn_pack.transpose(1, 0, 2).reshape(2, 2, rows, cols)
    sent = pick(attn_pack, 1 - core, 1).reshape(2 * rows, cols)
    lengths = jnp.broadcast_to(first_length.astype(BF16)[:, None], (16, cols))
    sent = swap_bit(jnp.concatenate([lengths, sent], axis=0), 0)
    first = jnp.where((member >> 1) == core, first_length, sent[0, :1].astype(jnp.int32))
    sent = sent[16:].reshape(2, rows, cols)
    attn_pack = pair_up(core, pick(attn_pack, core, 1), sent, 2)

    output_pack = jnp.concatenate(
        [output_weight.T, jnp.pad(gain_mlp[:, None], ((0, 0), (0, LANES - 1)))], axis=1
    )
    same = pick(attn_pack, member & 1).reshape(rows, 2 * cols)
    flip = pick(attn_pack, 1 - (member & 1)).reshape(rows, 2 * cols)
    far = cross(jnp.concatenate([same, flip, output_pack], axis=1), 2)
    flips = [
        jnp.concatenate([flip, output_pack], axis=1),
        far[:, 2 * cols :],
    ]
    hidden = [away(hidden_in, mask) for mask in (0, 2)]
    near = cross(after(jnp.concatenate(flips, axis=0), *hidden), 1)
    both = [
        jnp.concatenate([same, output_pack], axis=1),
        near[:rows],
        jnp.concatenate([far[:, : 2 * cols], far[:, 4 * cols :]], axis=1),
        near[rows:],
    ]
    both = after(place(both, [member ^ m for m in range(GROUPS)]), *hidden)
    hidden_units = down_weight.shape[0]
    units = -(-hidden_units // (16 * SPLIT)) * 16
    stacked = jnp.stack([gate_weight.T, up_weight.T, down_weight])
    stacked = jnp.pad(stacked, ((0, 0), (0, SPLIT * units - hidden_units), (0, 0)))
    block = stacked.shape[2]
    aligned = block % LANES == 0
    stacked = stacked.reshape(3, 2, 2, units, block)
    kept = [pick(stacked, side, 1), swap_bit(pick(stacked, 1 - side, 1), 1)]
    sent = swap_bit(jnp.concatenate([pick(part, 1 - core, 1) for part in kept], axis=2), 0)
    kept = [pick(part, core, 1) for part in kept]
    own = in_place([kept[0], sent[:, :, :block], kept[1], sent[:, :, block:]])
    own = jnp.concatenate(own, axis=2)
    output_mat = both[:, :, 2 * cols :].reshape(GROUPS * rows, -1)
    output_mat = pair_up((me >> links[-1]) & 1, output_mat, swap_bit(output_mat, links[-1]), 0)
    attn_mat = both[:, :, : 2 * cols].reshape(GROUPS, rows, 2, cols).transpose(2, 0, 1, 3)
    for bit in links:
        attn_mat = pair_up((me >> bit) & 1, attn_mat, swap_bit(attn_mat, bit), 0)
        attn_mat = attn_mat.reshape((-1,) + attn_mat.shape[2:])
    attn_mat = attn_mat.reshape(width, cols)
    hidden_pair = swap_bit(jnp.concatenate(hidden, axis=0), 0)

    far_axes = dp[: bits - SPLIT_BITS] + ("feat",)

    weights = lax.all_gather(after(own.reshape(3 * units, SPLIT * block), *hidden), far_axes)
    weights = weights.reshape(-1, GROUPS, 3 * units, SPLIT * block)
    if not aligned:
        weights = weights.transpose(1, 2, 0, 3).reshape(1, GROUPS, 3 * units, width)

    def pair_with(own, far):
        return [own, far, swap_bit(jnp.concatenate([own, far], axis=0), 0)]

    hr, qkv, out, sent, attf, rden = kernel_call(
        front_body,
        [((GROUPS, tokens, width), BF16), ((length, cols), BF16)]
        + [((tokens, 2 * vw), BF16)] * 2
        + [((length, vw), F32)] * 2,
        (first, group_arr, *hidden, hidden_pair, attn_mat),
        scalars=2,
        scratch=(pltpu.VMEM((length, vw), BF16),),
        flops=8 * 2**30,
        limit=24,
    )
    sent = swap_bit(sent, 0)
    for axis, bit in enumerate(links[-2::-1], 1):
        output_mat = pair_up((me >> bit) & 1, output_mat, swap_bit(output_mat, bit), axis)
    cot_far = swap_bit(cotangent, 1)
    for axis, bit in ((len(links), 0),):
        output_mat = pair_up((me >> bit) & 1, output_mat, swap_bit(output_mat, bit), axis)
    output_mat = output_mat.reshape(width, -1)
    cots = pair_with(cotangent, cot_far)
    out = [jnp.concatenate([part[:, at : at + vw] for part in (out, sent)], axis=1) for at in (0, vw)]
    out = [home(out[0], 0), home(out[1], 2)]
    (mlp_in,) = kernel_call(
        middle_body,
        [((tokens, width), BF16)],
        (member_arr, *out, hidden_in, output_mat),
        scalars=1,
        scratch=(pltpu.VMEM((tokens, H * DV), BF16),),
        flops=2**30,
        limit=12,
    )

    mlps = pair_with(mlp_in, swap_bit(mlp_in, 1))
    blocks = (SPLIT, tokens, width)
    parts = 2 if aligned and bits == SPLIT_BITS + 1 else 1
    part = me >> SPLIT_BITS if parts == 2 else jnp.zeros((), jnp.int32)
    hidden_shape = (GROUPS * units, SPLIT * tokens)
    outs = kernel_call(
        partial(feed_forward_body, units, parts),
        [((2, tokens, width), BF16, True)] * 4
        + [(hidden_shape, BF16, True)] * 2
        + [((GROUPS, units, width // parts), BF16, True)] * parts,
        (part.reshape(1), *mlps, *cots, weights),
        scalars=1,
        remote=7,
        scratch=(
            pltpu.VMEM((2, SPLIT * tokens, width), BF16),
            pltpu.VMEM((3, GROUPS * units, width), BF16),
            *[pltpu.VMEM(hidden_shape, BF16)] * 3,
            pltpu.VMEM(blocks, BF16),
            pltpu.VMEM(blocks, BF16),
            pltpu.VMEM((parts, GROUPS, units, width // parts), BF16),
            pltpu.SemaphoreType.DMA((6 + 3 * weights.shape[0] * GROUPS + 4 * SPLIT + parts,)),
        ),
        flops=14 * 2**30,
        limit=56,
    )
    grads, grads_sent, branch, branch_sent, act_t, up_t = outs[:6]

    late = kernel_call(
        partial(weight_body, units, parts, (0, 1)),
        [((GROUPS, 2 * units, width // parts), BF16)] * parts,
        (part.reshape(1), up_t, act_t, *mlps, *cots),
        scalars=1,
        remote=8,
        scratch=(
            pltpu.VMEM((2, SPLIT * tokens, width), BF16),
            *[pltpu.VMEM(hidden_shape, BF16)] * 2,
            pltpu.SemaphoreType.DMA((8,)),
        ),
        flops=4 * 2**30,
        limit=56,
    )
    terms = [pair[n] for n in range(parts) for pair in (outs[6:], late)]
    grads_sent = swap_bit(grads_sent, 0)
    grad_far = swap_bit(add_rounded(grads[1], grads_sent[1]), 1)
    branch_sent = swap_bit(branch_sent, 0)
    def reduce_terms(terms):
        if parts == 2:
            return add_rounded(terms[1], swap_bit(terms[0], SPLIT_BITS))
        far_bits = list(range(SPLIT_BITS, bits))[::-1]
        term = terms[0].reshape(GROUPS, terms[0].shape[1], -1, SPLIT * block).transpose(2, 0, 1, 3)
        return reduce_bits(term.reshape((2,) * len(far_bits) + term.shape[1:]), far_bits, far_bits)

    terms = [after(term, grad_far) if n >= 2 * (parts - 1) else term for n, term in enumerate(terms)]
    sums = [reduce_terms(terms[h::2]) for h in range(2)]
    totals = [lax.psum_scatter(term, "feat") for term in sums]

    middle_grad, *att_grad, output_kept, output_sent, middle = kernel_call(
        partial(middle_back_body, size),
        [((tokens, width), F32)]
        + [((tokens, 2 * vw), BF16)] * 2
        + [((width // 2, H * DV + LANES), BF16)] * 2
        + [((tokens, width), F32)],
        (member_arr, core.reshape(1), grads, grads_sent, after(grad_far, sums[0]), *out, hidden_in, cotangent, output_mat),
        scalars=2,
        scratch=(
            pltpu.VMEM((tokens, H * DV), BF16),
            pltpu.VMEM((tokens, H * DV), BF16),
            pltpu.VMEM((width, H * DV + LANES), BF16),
        ),
        flops=2**30,
        limit=56,
    )
    att_grad = [away(part, mask) for part, mask in zip(att_grad, (0, 2))]
    output_term = add_rounded(output_kept, swap_bit(after(output_sent, *att_grad), 0))
    output_term = output_term.reshape((2,) * len(links) + (GROUPS, rows, H * DV + LANES))
    att_sent = jnp.concatenate([part[:, vw:] for part in att_grad], axis=1)
    att_grad.append(swap_bit(after(att_sent, sums[0]), 0))
    output_term = reduce_bits(output_term, links[:1], links)
    branch_far = swap_bit(add_rounded(branch[1], branch_sent[1]), 1)
    att_grad = [after(part, sums[0]) for part in att_grad]
    input_parts, input_sent, attn_term = kernel_call(
        back_body,
        [((2, tokens, width), BF16)] * 2 + [((width, cols), BF16)],
        (first, group_arr, *att_grad, qkv, attf, rden, hr, attn_mat),
        scalars=2,
        scratch=(
            pltpu.VMEM((qk, length), F32),
            pltpu.VMEM((vw // DV, length, LANES), BF16),
            pltpu.VMEM((vw // DV, length, LANES), BF16),
            pltpu.VMEM((length, vw), BF16),
            pltpu.VMEM((length, cols), BF16),
            pltpu.VMEM(hr.shape, BF16),
            pltpu.VMEM(attn_mat.shape, BF16),
            pltpu.SemaphoreType.DMA((2,)),
        ),
        flops=12 * 2**30,
        remote=2,
        limit=56,
    )
    input_sent = swap_bit(input_sent, 0)
    input_parts = [after(add_rounded(input_parts[k], input_sent[k]), sums[1]) for k in range(2)]
    input_parts = [home(input_parts[0], 0), home(input_parts[1], 2)]
    total = jnp.concatenate(totals, axis=0).astype(F32)
    lanes = [total[:, j * block : (j + 1) * block] for j in range(SPLIT)]

    def share_total():
        own = [jnp.where(core == 0, lanes[x], lanes[x + 1]) for x in (0, 2)]
        sent = [jnp.where(core == 0, lanes[x + 1], lanes[x]) for x in (0, 2)]
        near = swap_bit(jnp.concatenate(sent, axis=1), 0)
        near = [near[:, :block], near[:, block:]]
        mine = [jnp.where(side == 0, both[0], both[1]) for both in (own, near)]
        sent = [jnp.where(side == 0, both[1], both[0]) for both in (own, near)]
        far = swap_bit(jnp.concatenate(sent, axis=0).astype(BF16), 1).astype(F32)
        return in_place([*mine, far[: 3 * units], far[3 * units :]]), far

    attn_term = after(attn_term, input_sent).reshape((2,) * len(links) + (2, GROUPS, rows, cols))
    attn_term = reduce_bits(attn_term, links[:0:-1], links)
    output_term = reduce_bits(output_term, links[1:], links[1:])
    attn_term = reduce_bits(attn_term, links[:1], links[:1])
    shares, shares_last = share_total()
    other = swap_bit(pick(attn_term, 1 - core), 0)
    attn_term = pair_up(core, pick(attn_term, core), other, 2).reshape(GROUPS, rows, 2 * cols)
    both = jnp.concatenate([attn_term, output_term], axis=2)
    kept, sent = ([pick(both, member ^ m) for m in pair] for pair in ((0, 2), (1, 3)))
    sent = after(jnp.stack(sent), *totals)
    input_parts = [after(part, sent) for part in input_parts]
    scaled_grad = input_parts[0].astype(F32) + input_parts[1].astype(F32)
    residual = hidden_in.astype(F32)
    scale = lax.rsqrt(jnp.mean(residual * residual, axis=1, keepdims=True) + EPSILON)
    normed = residual * scale
    inner = jnp.mean(normed * scaled_grad, axis=1, keepdims=True)
    input_grad = middle_grad + scale * (scaled_grad - normed * inner)

    sent = cross(sent, 1)
    out = [add_rounded(kept[k][:, 2 * cols :], sent[k][:, 2 * cols :]) for k in range(2)]
    same, flip = ([part[k][:, : 2 * cols] for k in range(2)] for part in (kept, sent))
    last = after(jnp.concatenate([same[1], flip[1], out[1]], axis=1), shares_last)
    last = cross(last, 2).astype(F32)
    output_sum = out[0].astype(F32) + last[:, 4 * cols :]
    output_grad = output_sum[:, : H * DV].T
    mlp_gain_grad = output_sum[:, H * DV]
    same = same[0].astype(F32) + last[:, : 2 * cols]
    flip = flip[0].astype(F32) + last[:, 2 * cols : 4 * cols]
    attn_grad = pair_up(member & 1, same, flip, 0).reshape(2, rows, 2, cols)
    attn_grad = attn_grad.transpose(1, 0, 2, 3).reshape(rows, GROUPS, cols)
    scale_rows = gain_attn.astype(F32)[:, None]
    query_raw = attn_grad[:, :, :qk].reshape(rows, H * HF)
    key_raw = attn_grad[:, :, qk : 2 * qk].reshape(rows, H * HF)
    value_raw = attn_grad[:, :, 2 * qk :].reshape(rows, H * DV)
    attn_gain_grad = (
        jnp.sum(query_raw * query_weight.astype(F32), axis=1)
        + jnp.sum(key_raw * key_weight.astype(F32), axis=1)
        + jnp.sum(value_raw * value_weight.astype(F32), axis=1)
    )

    block_out = (
        middle
        + branch[0].astype(F32)
        + branch_sent[0].astype(F32)
        + branch_far.astype(F32)
    ).astype(BF16)

    total = jnp.stack([share.reshape(3, units, block) for share in shares], axis=1)
    total = total.reshape(3, SPLIT * units, block)[:, :hidden_units]
    return (
        block_out,
        input_grad,
        query_raw * scale_rows,
        key_raw * scale_rows,
        value_raw * scale_rows,
        output_grad,
        total[0].T,
        total[1].T,
        total[2],
        attn_gain_grad,
        mlp_gain_grad,
    )


def solution(mesh):
    bits = mesh.shape["dp"].bit_length() - 1
    dp = tuple(f"bit{bit}" for bit in reversed(range(bits)))
    fine = jax.sharding.Mesh(mesh.devices.reshape((2,) * bits + (GROUPS,)), dp + ("feat",))
    both = dp + ("feat",)
    in_specs = (
        P(both, None),
        P(both, None),
        P(both, None),
        P(both, None),
        P(None, both),
        P(dp, "feat"),
        P(dp, "feat"),
        P("feat", dp),
        P(both),
        P(both),
        P(dp),
        P(both, None),
    )
    out_specs = (
        P(both, None),
        P(both, None),
        P(both, None),
        P(both, None),
        P(both, None),
        P(None, both),
        P(dp, "feat"),
        P(dp, "feat"),
        P("feat", dp),
        P(both),
        P(both),
    )
    return jax.shard_map(
        partial(on_device, dp), mesh=fine, in_specs=in_specs, out_specs=out_specs, check_vma=False
    )
```
